32 devices in a mesh: dp: 8 (over y, x, core), seq: 4 (over z).
Axes of the slice: x: 2, y: 2, z: 4, core: 2. Of those that a mesh axis runs over, the one named last changes fastest.
Arguments:
- tokens: bfloat16 [32, 512, 768], P('dp', 'seq'), may hold values from -6 to 6
- segments: int32 [32, 512], P('dp', 'seq'), may hold values from 0 to 2, as said below
- offset_buckets: int32 [1023], replicated, may hold values from 0 to 31
- norm_attn: float32 [768], replicated, may hold values from 0.5 to 1.5
- w_query: bfloat16 [768, 768], replicated, may hold values from -0.109375 to 0.109375
- w_key: bfloat16 [768, 768], replicated, may hold values from -0.078125 to 0.078125
- w_value: bfloat16 [768, 768], replicated, may hold values from -0.21875 to 0.21875
- w_output: bfloat16 [768, 768], replicated, may hold values from -1.75 to 1.75
- bias_table: float32 [32, 12], replicated, may hold values from -4 to 4
- norm_ff: float32 [768], replicated, may hold values from 0.5 to 1.5
- w_gate: bfloat16 [768, 2048], replicated, may hold values from -0.21875 to 0.21875
- w_up: bfloat16 [768, 2048], replicated, may hold values from -0.21875 to 0.21875
- w_down: bfloat16 [2048, 768], replicated, may hold values from -0.125 to 0.125
- cotangent: bfloat16 [32, 512, 768], P('dp', 'seq'), may hold values from -6 to 6
Outputs:
- mixed: bfloat16 [32, 512, 768], P('dp', 'seq')
- grad_tokens: float32 [32, 512, 768], P('dp', 'seq')
- grad_norm_attn: float32 [768], P('dp')
- grad_query: float32 [768, 768], P('dp')
- grad_key: float32 [768, 768], P('dp')
- grad_value: float32 [768, 768], P('dp')
- grad_output: float32 [768, 768], P('dp')
- grad_table: float32 [32, 12], replicated
- grad_norm_ff: float32 [768], P('dp')
- grad_gate: float32 [768, 2048], P('dp')
- grad_up: float32 [768, 2048], P('dp')
- grad_down: float32 [2048, 768], P('dp')
The draws below stay inside these ranges and needn't reach their ends.
Inputs may be any that keep to these rules, and one draw needn't show every extreme that they name: `segments`: within each row the ids never fall, the first position has id 0 and the last id 2; each id is one document.
All inputs are finite; a program needn't handle non-finite values.
Results may differ from the reference program's by a relative error of at most 0.017.
Values may be sent and summed in bfloat16 or wider, within the bound.
A program may use at most 192 MiB of HBM per device.

```python
import jax
import jax.numpy as jnp
from jax import lax

D = 768
H = 12
DH = 64
FF = 2048
BUCKETS = 32
SPAN = 128
ROWS_DEV = 4
LEN = 512
ROWS = 32
OFFSETS = 1023


def draw_segments(key, part):
    key = jax.random.fold_in(key, 11)
    first_key, second_key = jax.random.split(key)
    first = jax.random.randint(first_key, (ROWS, 1), 1, SPAN // 2)
    second = jax.random.randint(second_key, (ROWS, 1), LEN - SPAN // 2, LEN)
    places = jnp.arange(LEN)[None, :]
    return (places >= first).astype(jnp.int32) + (places >= second).astype(jnp.int32)


def touch_ends(result, stream_key, least, high):
    index_at = [jax.random.randint(jax.random.fold_in(stream_key, axis), (), 0, length) for axis, length in enumerate(result.shape)]
    main_axis = result.shape.index(max(result.shape))
    next_to = index_at[:main_axis] + [(index_at[main_axis] + 1) % result.shape[main_axis]] + index_at[main_axis + 1:]
    return result.at[tuple(index_at)].set(least).at[tuple(next_to)].set(high)


def shard_levels(stream_key, dims, cuts, least, high):
    level = 1.0
    for position, shards_of in cuts:
        steps = jax.random.uniform(jax.random.fold_in(jax.random.fold_in(stream_key, 6), position), (shards_of,), jnp.float32, least / len(cuts), high / len(cuts))
        level = level * jnp.repeat(jnp.exp(steps), dims[position] // shards_of).reshape((-1,) + (1,) * (len(dims) - 1 - position))
    return level


def noise(rng, dims, spread, bound, cuts=(), dtype=jnp.bfloat16):
    result = jax.random.normal(rng, dims, jnp.float32) * spread
    if len(cuts) > 0:
        result = shard_levels(rng, dims, cuts, -0.22, 0.18) * result
    return jnp.clip(result, min=-bound, max=bound).astype(dtype)


def setup_inputs(seed: int = 0) -> dict:
    key_list = jax.random.split(jax.random.key(seed), 15)
    return {
        "tokens": noise(key_list[0], (ROWS, LEN, D), 1.0, 6.0, ((0, 8), (1, 4))),
        "segments": draw_segments(jax.random.fold_in(key_list[14], 71), 0),
        "offset_buckets": touch_ends(jax.random.randint(key_list[2], (OFFSETS,), 0, BUCKETS), jax.random.fold_in(key_list[2], 1), 0, BUCKETS - 1).astype(jnp.int32),
        "norm_attn": jnp.clip(1.0 + 0.1 * jax.random.normal(key_list[3], (D,), jnp.float32), 0.5, 1.5),
        "w_query": noise(key_list[4], (D, D), (D * 4) ** -0.5, 0.109375),
        "w_key": noise(key_list[5], (D, D), (D * 8) ** -0.5, 0.078125),
        "w_value": noise(key_list[6], (D, D), D ** -0.5, 0.21875),
        "w_output": noise(key_list[7], (D, D), (D // 64) ** -0.5, 1.75),
        "bias_table": noise(key_list[8], (BUCKETS, H), 1.0, 4.0, (), jnp.float32),
        "norm_ff": jnp.clip(1.0 + 0.1 * jax.random.normal(key_list[9], (D,), jnp.float32), 0.5, 1.5),
        "w_gate": noise(key_list[10], (D, FF), D ** -0.5, 0.21875),
        "w_up": noise(key_list[11], (D, FF), D ** -0.5, 0.21875),
        "w_down": noise(key_list[12], (FF, D), FF ** -0.5, 0.125),
        "cotangent": noise(key_list[13], (ROWS, LEN, D), 1.0, 6.0, ((0, 8), (1, 4))),
    }


@jax.custom_vjp
def low(v):
    return lax.optimization_barrier(v.astype(jnp.bfloat16)).astype(jnp.float32)

@jax.custom_vjp
def low_back(v):
    return v

def low_keep(v):
    return (low(v), None)

def low_pass(kept, grad):
    return (grad,)

def back_keep(v):
    return (v, None)

def back_low(kept, grad):
    return (low(grad),)
low.defvjp(low_keep, low_pass)
low_back.defvjp(back_keep, back_low)
EPSILON = 1e-06

def normalize(values, gain):
    scale = lax.rsqrt(lax.optimization_barrier(jnp.mean(values * values, -1, keepdims=True)) + EPSILON)
    return values * scale * gain

def matmul(left, right):
    return jnp.matmul(left, right, precision=lax.Precision.HIGHEST)

def layer(params, inputs, seg_rows, offset_buckets):
    gain_one, w_query, w_key, w_value, w_output, table, gain_two, w_gate, w_up, w_down = params
    groups = inputs.shape[0]
    hidden_one = low(normalize(inputs, gain_one))
    queries = low_back(low(matmul(hidden_one, w_query))).reshape(groups, LEN, H, DH)
    keys = low_back(low(matmul(hidden_one, w_key))).reshape(groups, LEN, H, DH)
    values = low_back(low(matmul(hidden_one, w_value))).reshape(groups, LEN, H, DH)
    offsets = (jnp.arange(LEN)[None, :] - jnp.arange(LEN)[:, None] + LEN - 1).astype(jnp.int32)
    pair_bucket = offset_buckets[offsets]
    bias = jnp.transpose(table[pair_bucket], (2, 0, 1))
    raw = jnp.einsum('gqhd,gkhd->ghqk', queries, keys, precision=lax.Precision.HIGHEST) + bias[None]
    raw = low_back(raw)
    allowed = seg_rows[:, None, :, None] == seg_rows[:, None, None, :]
    scores = jnp.where(allowed, raw, -1e+30)
    probs = low(jax.nn.softmax(scores, axis=-1))
    attended = jnp.einsum('ghqk,gkhd->gqhd', probs, values, precision=lax.Precision.HIGHEST)
    attended = low_back(low(attended)).reshape(groups, LEN, D)
    resid = inputs + low_back(matmul(attended, w_output))
    hidden_two = low(normalize(resid, gain_two))
    gate = low_back(matmul(hidden_two, w_gate))
    upper = low_back(matmul(hidden_two, w_up))
    activ = low(jax.nn.gelu(gate, approximate=True) * upper)
    return resid + low_back(matmul(activ, w_down))

def reference(tokens, segments, offset_buckets, norm_attn, w_query, w_key, w_value, w_output, bias_table, norm_ff, w_gate, w_up, w_down, cotangent):
    params = (norm_attn.astype(jnp.float32), w_query.astype(jnp.float32), w_key.astype(jnp.float32), w_value.astype(jnp.float32), w_output.astype(jnp.float32), bias_table.astype(jnp.float32), norm_ff.astype(jnp.float32), w_gate.astype(jnp.float32), w_up.astype(jnp.float32), w_down.astype(jnp.float32))
    groups = ROWS // ROWS_DEV
    inputs = tokens.astype(jnp.float32).reshape(groups, ROWS_DEV, LEN, D)
    seg_groups = segments.reshape(groups, ROWS_DEV, LEN)
    grads_in = cotangent.astype(jnp.float32).reshape(groups, ROWS_DEV, LEN, D)

    def step(totals, item):
        block, seg_rows, grad_block = item
        output, pull = jax.vjp(lambda weights, values: layer(weights, values, seg_rows, offset_buckets), params, block)
        grad_params, grad_input = pull(grad_block)
        totals = jax.tree.map(lambda first, second: first + second, totals, grad_params)
        return (totals, (output.astype(jnp.bfloat16), grad_input))
    zeros = jax.tree.map(jnp.zeros_like, params)
    totals, (outputs, grad_inputs) = lax.scan(step, zeros, (inputs, seg_groups, grads_in))
    return (outputs.reshape(ROWS, LEN, D), grad_inputs.reshape(ROWS, LEN, D), totals[0], totals[1], totals[2], totals[3], totals[4], totals[5], totals[6], totals[7], totals[8], totals[9])
```

```python
import functools

import jax
import jax.numpy as jnp
from jax import lax
from jax.experimental import pallas as pl
from jax.experimental.pallas import tpu as pltpu
from jax.sharding import PartitionSpec as P

MESH = pl.DeviceIdType.MESH
VMEM = pltpu.VMEM
LOW = jnp.bfloat16
F32 = jnp.float32
EPSILON = 1e-06
MASKED = -1e30
GROUP = 8
VMEM_BYTES = 63 * 2**20


def dot(left, right):
    return jnp.dot(left, right, preferred_element_type=F32)


def dot_back(left, right):
    return lax.dot_general(left, right, (((1,), (1,)), ((), ())), preferred_element_type=F32)


def inverse_rms(values):
    return lax.rsqrt(jnp.mean(values * values, -1, keepdims=True) + EPSILON)


def zero_padded(block, half):
    blank = jnp.zeros_like(block)
    return jnp.concatenate([blank, block] if half else [block, blank], axis=0)


def forward_kernel(
    x_ref, seg_ref, bucket_ref, gain_one_ref, wq_ref, wk_ref, wv_ref, wo_ref, table_ref, gain_two_ref,
    wg_ref, wu_ref, wd_ref,
    probs_ref, slope_up_ref, slope_gate_ref, activ_t_ref, attended_t_ref, q_ref, k_ref, v_ref, k_t_ref,
    resid_ref, mixed_ref,
    bias_ref, mask_ref, offset_ref, hidden_ref, q_t_ref, v_t_ref, activ_ref,
):
    span, width = x_ref.shape
    buckets, heads = table_ref.shape
    head_dim = width // heads
    blocks = span // 128
    pairs = heads // 2

    one_hot = (
        lax.broadcasted_iota(jnp.int32, (buckets, bucket_ref.shape[1]), 0) == bucket_ref[...]
    ).astype(F32)
    offset_ref[:heads, :] = lax.dot_general(
        table_ref[...], one_hot, (((0,), (0,)), ((), ())),
        precision=lax.Precision.HIGHEST, preferred_element_type=F32,
    )

    @pl.loop(0, heads)
    def _(h):
        row = offset_ref[pl.ds(h, 1), :]
        for d in range(2 * blocks - 1):
            window = jnp.broadcast_to(row[:, 128 * d : 128 * d + 256], (128, 256))
            bias_ref[h, d] = pltpu.roll(window, 129, 1, stride=1, stride_axis=0)[:, :128].T

    seg_row = seg_ref[...].astype(F32)
    for kb in range(blocks):
        column = jnp.broadcast_to(seg_row[:, 128 * kb : 128 * kb + 128], (128, 128)).T
        for qb in range(blocks):
            same = column == seg_row[:, 128 * qb : 128 * qb + 128]
            mask_ref[128 * kb : 128 * kb + 128, 128 * qb : 128 * qb + 128] = jnp.where(same, 0.0, MASKED)

    @pl.loop(0, blocks)
    def _(i):
        rows = pl.ds(pl.multiple_of(i * 128, 128), 128)
        inputs = x_ref[rows, :].astype(F32)
        hidden_ref[rows, :] = (inputs * inverse_rms(inputs) * gain_one_ref[...]).astype(LOW)

    for tile in range(width // 256):
        cols = slice(256 * tile, 256 * tile + 256)
        q = dot(hidden_ref[...], wq_ref[:, cols])
        q_t_ref[cols, :] = q.T.astype(LOW)
        k = dot(hidden_ref[...], wk_ref[:, cols])
        k_t_ref[cols, :] = k.T.astype(LOW)
        v = dot(hidden_ref[...], wv_ref[:, cols])
        v_t_ref[cols, :] = v.T.astype(LOW)
        for i in range(2):
            lanes = slice(128 * i, 128 * i + 128)
            q_ref[2 * tile + i] = q[:, lanes].astype(LOW)
            k_ref[2 * tile + i] = k[:, lanes].astype(LOW)
            v_ref[2 * tile + i] = v[:, lanes].astype(LOW)

    @pl.loop(0, pairs)
    def _(pair):
        keys = k_ref[pair]
        for b in range(2):
            h = 2 * pair + b
            rows = pl.ds(pl.multiple_of(h * head_dim, head_dim), head_dim)
            q_t = zero_padded(q_t_ref[rows, :], b)
            v_t = v_t_ref[rows, :]
            for half in range(span // 256):
                cols = slice(256 * half, 256 * half + 256)
                bias = jnp.concatenate(
                    [
                        jnp.concatenate(
                            [bias_ref[h, kb - qb + blocks - 1] for qb in (2 * half, 2 * half + 1)], axis=1
                        )
                        for kb in range(blocks)
                    ],
                    axis=0,
                )
                scores = dot(keys, q_t[:, cols]) + bias + mask_ref[:, cols]
                powers = jnp.exp(scores - jnp.max(scores, axis=0, keepdims=True))
                probs = (powers * (1.0 / jnp.sum(powers, axis=0, keepdims=True))).astype(LOW)
                probs_ref[h, :, cols] = probs
                attended_t_ref[rows, cols] = dot(v_t, probs).astype(LOW)

    attended = attended_t_ref[...].T
    for tile in range(width // 256):
        cols = slice(256 * tile, 256 * tile + 256)
        resid_ref[:, cols] = x_ref[:, cols].astype(F32) + dot(attended, wo_ref[:, cols])

    @pl.loop(0, blocks)
    def _(i):
        rows = pl.ds(pl.multiple_of(i * 128, 128), 128)
        resid = resid_ref[rows, :]
        hidden_ref[rows, :] = (resid * inverse_rms(resid) * gain_two_ref[...]).astype(LOW)

    @pl.loop(0, wg_ref.shape[1] // 512)
    def _(g):
        for sub in range(2):
            cols = pl.ds(pl.multiple_of(512 * g + 256 * sub, 256), 256)
            gate = dot(hidden_ref[...], wg_ref[:, cols])
            upper = dot(hidden_ref[...], wu_ref[:, cols])
            square = gate * gate
            curve = jnp.tanh(0.7978845608028654 * gate * (1.0 + 0.044715 * square))
            gelu = 0.5 * gate * (1.0 + curve)
            slope = 0.5 * (1.0 + curve) + 0.5 * gate * (1.0 - curve * curve) * (
                0.7978845608028654 * (1.0 + 3 * 0.044715 * square)
            )
            activ = gelu * upper
            lanes = slice(256 * sub, 256 * sub + 256)
            slope_up_ref[g, :, lanes] = gelu.astype(LOW)
            slope_gate_ref[g, :, lanes] = (upper * slope).astype(LOW)
            activ_ref[:, cols] = activ.astype(LOW)
            activ_t_ref[2 * g + sub] = activ.T.astype(LOW)

    for tile in range(width // 256):
        cols = slice(256 * tile, 256 * tile + 256)
        mixed_ref[:, cols] = (resid_ref[:, cols] + dot(activ_ref[...], wd_ref[:, cols])).astype(LOW)


def forward(x, seg, buckets, gain_one, wq, wk, wv, wo, table, gain_two, wg, wu, wd):
    span, width = x.shape
    ff = wg.shape[1]
    heads = table.shape[1]
    low = lambda *shape: jax.ShapeDtypeStruct(shape, LOW)
    pairs = low(heads // 2, span, 128)
    return pl.pallas_call(
        forward_kernel,
        out_shape=[
            low(heads, span, span), low(ff // 512, span, 512), low(ff // 512, span, 512),
            low(ff // 256, 256, span), low(width, span), pairs, pairs, pairs, low(width, span),
            jax.ShapeDtypeStruct((span, width), F32), low(span, width),
        ],
        scratch_shapes=[
            VMEM((heads, 2 * (span // 128) - 1, 128, 128), F32), VMEM((span, span), F32), VMEM((16, 1024), F32),
            VMEM((span, width), LOW), VMEM((width, span), LOW), VMEM((width, span), LOW), VMEM((span, ff), LOW),
        ],
        compiler_params=pltpu.CompilerParams(vmem_limit_bytes=VMEM_BYTES),
        name="forward",
    )(x, seg, buckets, gain_one, wq, wk, wv, wo, table, gain_two, wg, wu, wd)


class Place:
    def __init__(self, n_dp, n_seq):
        stride = n_dp // GROUP
        dp = lax.axis_index("dp")
        z = lax.axis_index("seq")
        index = dp // stride
        self.n_seq = n_seq
        self.core, self.x, self.y, self.z = index % 2, (index // 2) % 2, index // 4, z
        self.dp = dp
        self.core_peer = (dp + stride * (1 - 2 * self.core), z)
        self.x_peer = (dp + 2 * stride * (1 - 2 * self.x), z)
        self.y_peer = (dp + 4 * stride * (1 - 2 * self.y), z)

    def z_peer(self, z):
        return (self.dp, z)

    def z_pair(self, bit):
        return (self.dp, self.z + bit * (1 - 2 * ((self.z // bit) % 2)))


def remote(src, dst, sems, index, peer):
    return pltpu.make_async_remote_copy(
        src_ref=src, dst_ref=dst, send_sem=sems.at[0, index], recv_sem=sems.at[1, index],
        device_id=peer, device_id_type=MESH,
    )


class Sums:
    def __init__(self, place, own, sems, got0, got1, got2, low_z, high_z):
        self.place, self.own, self.sems = place, own, sems
        self.got0, self.got1, self.got2, self.low_z, self.high_z = got0, got1, got2, low_z, high_z

    def copy0(self, p):
        at = self.place
        return remote(self.own.at[p, 1 - at.core], self.got0.at[p], self.sems.at[0], p, at.core_peer)

    def copy1(self, p, k):
        at = self.place
        mine = self.own.at[p, at.core]
        src = mine.at[1 - at.y] if k else mine.at[:, 1 - at.x]
        return remote(src, self.got1.at[p], self.sems.at[1], p, at.y_peer if k else at.x_peer)

    def copy2(self, p, k):
        at = self.place
        mine = self.own.at[p, at.core]
        src = mine.at[at.y, 1 - at.x] if k else mine.at[1 - at.y, at.x]
        return remote(src, self.got2.at[p], self.sems.at[2], p, at.x_peer if k else at.y_peer)

    def kept(self, p):
        at = self.place
        return self.own.at[p, at.core, at.y, at.x]

    def up(self, p, first):
        src = self.kept(p) if first else self.got2.at[p]
        return remote(src, self.low_z.at[p], self.sems.at[3], p, self.place.z_peer(self.place.z + 1))

    def down(self, p, first):
        src = self.kept(p) if first else self.got1.at[p, 0]
        return remote(src, self.high_z.at[p], self.sems.at[4], p, self.place.z_peer(self.place.z - 1))

    def stage0(self, j):
        for k in range(2):
            self.copy0(2 * j + k).start()

    def stage1(self, j):
        at = self.place
        for k in range(2):
            p = 2 * j + k
            self.copy0(p).wait_recv()
            for a in range(2):
                for b in range(2):
                    self.own[p, at.core, a, b] = self.own[p, at.core, a, b] + self.got0[p, a, b]
            self.copy1(p, k).start()

    def stage2(self, j):
        at = self.place
        for k in range(2):
            p = 2 * j + k
            self.copy1(p, k).wait_recv()
            for a in range(2):
                if k:
                    self.own[p, at.core, at.y, a] = self.own[p, at.core, at.y, a] + self.got1[p, a]
                else:
                    self.own[p, at.core, a, at.x] = self.own[p, at.core, a, at.x] + self.got1[p, a]
            self.copy2(p, k).start()

    def stage3(self, j):
        at = self.place
        for k in range(2):
            p = 2 * j + k
            self.copy2(p, k).wait_recv()
            self.own[p, at.core, at.y, at.x] = self.own[p, at.core, at.y, at.x] + self.got2[p]
        self.hop(j, 0)

    def hop(self, j, step):
        at = self.place
        last = at.n_seq - 1

        @pl.when(at.z == step)
        def _():
            for k in range(2):
                p = 2 * j + k
                if step:
                    self.up(p, False).wait_recv()
                    self.got2[p] = self.low_z[p] + self.own[p, at.core, at.y, at.x]
                self.up(p, step == 0).start()

        @pl.when(at.z == last - step)
        def _():
            for k in range(2):
                p = 2 * j + k
                if step:
                    self.down(p, False).wait_recv()
                    self.got1[p, 0] = self.high_z[p] + self.own[p, at.core, at.y, at.x]
                self.down(p, step == 0).start()

    def finish(self, j, out, out_sems):
        at = self.place
        last = at.n_seq - 1
        for k in range(2):
            p = 2 * j + k

            @pl.when(at.z == last)
            def _():
                self.up(p, False).wait_recv()
                self.low_z[p] = self.low_z[p] + self.own[p, at.core, at.y, at.x]

            @pl.when(at.z == 0)
            def _():
                self.down(p, False).wait_recv()
                self.low_z[p] = self.high_z[p] + self.own[p, at.core, at.y, at.x]

            @pl.when((at.z > 0) & (at.z < last))
            def _():
                total = self.low_z[p].astype(F32) + self.high_z[p].astype(F32)
                self.low_z[p] = (total + self.own[p, at.core, at.y, at.x].astype(F32)).astype(LOW)

            pltpu.make_async_copy(self.low_z.at[p], out.at[p], out_sems.at[p]).start()

    def drain(self, j, out, out_sems):
        at = self.place
        last = at.n_seq - 1
        for k in range(2):
            p = 2 * j + k
            self.copy0(p).wait_send()
            self.copy1(p, k).wait_send()
            self.copy2(p, k).wait_send()

            @pl.when(at.z == 0)
            def _():
                self.up(p, True).wait_send()

            @pl.when((at.z > 0) & (at.z < last))
            def _():
                self.up(p, False).wait_send()
                self.down(p, False).wait_send()

            @pl.when(at.z == last)
            def _():
                self.down(p, True).wait_send()

            pltpu.make_async_copy(self.low_z.at[p], out.at[p], out_sems.at[p]).wait()


FF_JOBS, ATT_JOBS = 6, 4
FF_ROWS, ATT_ROWS = 384, 288


def backward_kernel(
    n_dp, n_seq,
    x_hbm, cot_hbm, mixed_ref, bucket_ref, gain_one_ref, gain_two_ref,
    wq_hbm, wk_hbm, wv_hbm, wo_hbm, wg_hbm, wu_hbm, wd_hbm,
    probs_hbm, slope_up_hbm, slope_gate_hbm, activ_t_hbm, attended_t_hbm, q_hbm, k_hbm, v_hbm, k_t_hbm, resid_hbm,
    mixed_out, tokens_out, ff_out, att_out, small_out,
    ff_own, ff_got0, ff_got1, ff_got2, ff_low, ff_high, ff_sems, ff_out_sems,
    att_own, att_got0, att_got1, att_got2, att_low, att_high, att_sems, att_out_sems,
    small_own, small_got, small_sems,
    wq_ref, wk_ref, wv_ref, wo_ref, wgu_ref, wd_ref, probs_ref, slope_up_ref, slope_gate_ref,
    activ_t_ref, attended_t_ref, q_ref, k_ref, v_ref, k_t_ref, resid_ref,
    hidden_t_ref, acc_ref, branch_ref, d_att_ref, d_att_t_ref, d_q_t_ref, d_k_ref, d_v_ref, offset_ref,
    x_ref, load_sems, ff_load_sems, probs_sems, row_sems, own_sems,
):
    span, width = x_hbm.shape
    cot_ref = x_ref
    buckets_wide = bucket_ref.shape[1]
    heads = probs_hbm.shape[0]
    head_dim = width // heads
    blocks = span // 128
    pairs = heads // 2
    at = Place(n_dp, n_seq)

    loads = [
        pltpu.make_async_copy(src, dst, load_sems.at[i])
        for i, (src, dst) in enumerate(
            [
                (activ_t_hbm, activ_t_ref), (resid_hbm, resid_ref), (attended_t_hbm, attended_t_ref), (wo_hbm, wo_ref),
                (q_hbm, q_ref), (k_hbm, k_ref), (v_hbm, v_ref), (k_t_hbm, k_t_ref),
                (wq_hbm, wq_ref), (wk_hbm, wk_ref), (wv_hbm, wv_ref), (cot_hbm, x_ref),
            ]
        )
    ]
    for load in loads:
        load.start()

    def ff_loads(g, sub):
        cols = pl.ds(pl.multiple_of(g * 512 + sub * 256, 256), 256)
        lanes = pl.ds(sub * 256, 256)
        pairs_ = [
            (wd_hbm.at[cols, :], wd_ref.at[sub]),
            (wg_hbm.at[:, cols], wgu_ref.at[sub, :, pl.ds(0, 256)]),
            (wu_hbm.at[:, cols], wgu_ref.at[sub, :, pl.ds(256, 256)]),
            (slope_up_hbm.at[g, :, lanes], slope_up_ref.at[sub]),
            (slope_gate_hbm.at[g, :, lanes], slope_gate_ref.at[sub]),
        ]
        return [
            pltpu.make_async_copy(src, dst, ff_load_sems.at[i, sub]) for i, (src, dst) in enumerate(pairs_)
        ]

    def probs_load(pair, slot):
        return pltpu.make_async_copy(probs_hbm.at[pl.ds(2 * pair, 2)], probs_ref.at[slot], probs_sems.at[slot])

    for sub in range(2):
        for load in ff_loads(0, sub):
            load.start()
    probs_load(0, 0).start()

    barrier = pltpu.get_barrier_semaphore()
    peers = [at.core_peer, at.x_peer, at.y_peer] + [
        at.z_peer(lax.rem(at.z + i, n_seq)) for i in range(1, n_seq)
    ]
    for peer in peers:
        pl.semaphore_signal(barrier, inc=1, device_id=peer, device_id_type=MESH)
    pl.semaphore_wait(barrier, len(peers))

    ff = Sums(at, ff_own, ff_sems, ff_got0, ff_got1, ff_got2, ff_low, ff_high)
    att = Sums(at, att_own, att_sems, att_got0, att_got1, att_got2, att_low, att_high)

    def rows_back(src, out, kind):
        copies = []
        for i in range(1, n_seq):
            to = lax.rem(at.z + i, n_seq)
            copies.append(
                pltpu.make_async_remote_copy(
                    src_ref=src.at[pl.ds(pl.multiple_of(to * 128, 128), 128), :], dst_ref=out.at[at.z],
                    send_sem=row_sems.at[kind, 0, i], recv_sem=row_sems.at[kind, 1, i],
                    device_id=at.z_peer(to), device_id_type=MESH,
                )
            )
        copies.append(
            pltpu.make_async_copy(
                src.at[pl.ds(pl.multiple_of(at.z * 128, 128), 128), :], out.at[at.z], own_sems.at[kind]
            )
        )
        return copies

    for copy in rows_back(mixed_ref, mixed_out, 0):
        copy.start()

    loads[0].wait()
    loads[11].wait()
    for j in range(2):

        @pl.loop(0, GROUP)
        def _(s):
            product = dot(activ_t_ref[s, 128 * j : 128 * j + 128, :], cot_ref[...]).astype(LOW)
            for k in range(2):
                for i in range(width // 128):
                    ff_own[2 * j + k, s % 2, s // 4, (s // 2) % 2, 64 * i : 64 * i + 64, :] = product[
                        64 * k : 64 * k + 64, 128 * i : 128 * i + 128
                    ]

        ff.stage0(j)
    loads[1].wait()

    @pl.loop(0, blocks)
    def _(i):
        rows = pl.ds(pl.multiple_of(i * 128, 128), 128)
        resid = resid_ref[rows, :]
        hidden_t_ref[:, rows] = (resid * inverse_rms(resid) * gain_two_ref[...]).T.astype(LOW)

    ff.stage1(0)
    shard = width // GROUP
    tiles = wg_hbm.shape[1] // 512
    acc_ref[...] = jnp.zeros_like(acc_ref)

    @pl.loop(0, tiles)
    def _(g):
        job = 2 + g
        for sub in range(2):
            for load in ff_loads(g, sub):
                load.wait()
            d_act = dot_back(cot_ref[...], wd_ref[sub])
            d_gate = (d_act * slope_gate_ref[sub].astype(F32)).astype(LOW)
            d_upper = (d_act * slope_up_ref[sub].astype(F32)).astype(LOW)
            for k, d_half in enumerate((d_gate, d_upper)):
                product = dot(hidden_t_ref[...], d_half).astype(LOW)
                for s in range(GROUP):
                    for i in range(2):
                        place = shard * (2 * sub + i)
                        ff_own[2 * job + k, s % 2, s // 4, (s // 2) % 2, place : place + shard, :] = product[
                            shard * s : shard * s + shard, 128 * i : 128 * i + 128
                        ]
            if sub:
                ff.stage0(job)
            d_both = jnp.concatenate([d_gate, d_upper], axis=1)
            for tile in range(width // 256):
                cols = slice(256 * tile, 256 * tile + 256)
                acc_ref[:, cols] += dot_back(d_both, wgu_ref[sub, cols, :])

            @pl.when(g < tiles - 1)
            def _():
                for load in ff_loads(g + 1, sub):
                    load.start()

        ff.stage1(job - 1)

    def norm_back(vector_ref, gain_ref, extra_ref, low_ref, row):
        total = jnp.zeros((1, width), F32)
        for i in range(blocks):
            rows = slice(128 * i, 128 * i + 128)
            vector = vector_ref[rows, :].astype(F32)
            scale = inverse_rms(vector)
            normed = vector * scale
            grad = acc_ref[rows, :]
            total = total + jnp.sum(grad * normed, axis=0, keepdims=True)
            inner = grad * gain_ref[...]
            result = extra_ref[rows, :].astype(F32) + scale * (
                inner - normed * jnp.mean(inner * normed, -1, keepdims=True)
            )
            acc_ref[rows, :] = result
            low_ref[rows, :] = result.astype(LOW)
        small_own[0, row : row + 1, :] = total

    norm_back(resid_ref, gain_two_ref, cot_ref, branch_ref, 12)
    x_load = pltpu.make_async_copy(x_hbm, x_ref, load_sems.at[12])
    x_load.start()
    ff.stage1(FF_JOBS - 1)

    def share(sums, j, left_t, right):
        for k in range(2):
            half = slice(width // 2 * k, width // 2 * k + width // 2)
            product = dot(left_t, right[:, half]).astype(LOW)
            for s in range(GROUP):
                for i in range(width // 256):
                    sums.own[2 * j + k, s % 2, s // 4, (s // 2) % 2, shard * i : shard * i + shard, :] = product[
                        shard * s : shard * s + shard, 128 * i : 128 * i + 128
                    ]
        sums.stage0(j)

    loads[2].wait()
    share(att, 0, attended_t_ref[...], branch_ref[...])
    loads[3].wait()
    for tile in range(width // 256):
        rows = slice(256 * tile, 256 * tile + 256)
        d_att = dot_back(branch_ref[...], wo_ref[rows, :])
        d_att_t_ref[rows, :] = d_att.T.astype(LOW)
        for i in range(2):
            d_att_ref[2 * tile + i] = d_att[:, 128 * i : 128 * i + 128].astype(LOW)
    att.stage1(0)
    for i in range(4, 8):
        loads[i].wait()
    left_half = lax.broadcasted_iota(jnp.int32, (span, 128), 1) < head_dim
    flip = (
        lax.broadcasted_iota(jnp.int32, (128, 128), 0) + lax.broadcasted_iota(jnp.int32, (128, 128), 1) == 127
    ).astype(F32)

    @pl.loop(0, pairs)
    def _(pair):
        slot = lax.rem(pair, 2)
        probs_load(pair, slot).wait()

        @pl.when(pair < pairs - 1)
        def _():
            probs_load(pair + 1, 1 - slot).start()

        values = v_ref[pair]
        d_att = d_att_ref[pair]
        queries = q_ref[pair]
        lanes = pl.ds(pl.multiple_of(pair * 128, 128), 128)
        d_values = jnp.zeros((span, 128), F32)
        d_keys = jnp.zeros((span, 128), F32)
        for b in range(2):
            h = 2 * pair + b
            rows = pl.ds(pl.multiple_of(h * head_dim, head_dim), head_dim)
            d_att_t = zero_padded(d_att_t_ref[rows, :], b)
            k_t = k_t_ref[rows, :]
            sides = []
            sums = [None] * (2 * blocks - 1)
            for half in range(span // 256):
                cols = slice(256 * half, 256 * half + 256)
                d_probs = dot(values, d_att_t[:, cols])
                probs = probs_ref[slot, b, :, cols].astype(F32)
                inner = jnp.sum(probs * d_probs, axis=0, keepdims=True)
                d_scores = probs * (d_probs - inner)
                for kb in range(blocks):
                    for i in range(2):
                        d = kb - (2 * half + i) + blocks - 1
                        block = d_scores[128 * kb : 128 * kb + 128, 128 * i : 128 * i + 128]
                        sums[d] = block if sums[d] is None else sums[d] + block
                d_scores = d_scores.astype(LOW)
                d_q_t_ref[rows, cols] = dot(k_t, d_scores).astype(LOW)
                sides.append(d_scores)
            mine = left_half if b == 0 else jnp.logical_not(left_half)
            d_values = d_values + dot(probs_ref[slot, b], jnp.where(mine, d_att, jnp.zeros_like(d_att)))
            d_keys = d_keys + dot(
                jnp.concatenate(sides, axis=1), jnp.where(mine, queries, jnp.zeros_like(queries))
            )
            totals = []
            for d in range(2 * blocks - 1):
                flipped = jnp.dot(sums[d], flip, precision=lax.Precision.HIGHEST, preferred_element_type=F32)
                wide = jnp.concatenate([flipped, jnp.zeros((128, 128), F32)], axis=1)
                totals.append(jnp.sum(pltpu.roll(wide, 0, 1, stride=1, stride_axis=0), axis=0, keepdims=True))
            pieces = [totals[0][:, :128]]
            for d in range(1, 2 * blocks - 1):
                pieces.append(totals[d - 1][:, 128:] + totals[d][:, :128])
            pieces.append(totals[-1][:, 128:])
            offset_ref[pl.ds(h, 1), :] = jnp.concatenate(pieces, axis=1)
        d_v_ref[:, lanes] = d_values.astype(LOW)
        d_k_ref[:, lanes] = d_keys.astype(LOW)

    x_load.wait()

    @pl.loop(0, blocks)
    def _(i):
        rows = pl.ds(pl.multiple_of(i * 128, 128), 128)
        inputs = x_ref[rows, :].astype(F32)
        hidden_t_ref[:, rows] = (inputs * inverse_rms(inputs) * gain_one_ref[...]).T.astype(LOW)

    share(att, 1, hidden_t_ref[...], d_v_ref[...])
    share(att, 2, hidden_t_ref[...], d_k_ref[...])
    att.stage1(1)
    branch_ref[...] = d_q_t_ref[...].T
    share(att, 3, hidden_t_ref[...], branch_ref[...])
    att.stage1(2)
    for i in range(8, 11):
        loads[i].wait()
    for tile in range(width // 256):
        rows = slice(256 * tile, 256 * tile + 256)
        resid_ref[:, rows] = acc_ref[:, rows]
        acc_ref[:, rows] = (
            dot_back(branch_ref[...], wq_ref[rows, :])
            + dot_back(d_k_ref[...], wk_ref[rows, :])
            + dot_back(d_v_ref[...], wv_ref[rows, :])
        )
    att.stage1(3)
    norm_back(x_ref, gain_one_ref, resid_ref, branch_ref, 13)
    for copy in rows_back(branch_ref, tokens_out, 1):
        copy.start()

    one_hot = (
        lax.broadcasted_iota(jnp.int32, (128, buckets_wide), 0) == bucket_ref[...]
    ).astype(F32)
    small_own[0, :12, :128] = lax.dot_general(
        offset_ref[:12, :], one_hot, (((1,), (1,)), ((), ())),
        precision=lax.Precision.HIGHEST, preferred_element_type=F32,
    )
    small_peers = [at.core_peer, at.x_peer, at.y_peer]
    bit = 1
    while bit < n_seq:
        small_peers.append(at.z_pair(bit))
        bit *= 2

    def small_copy(i):
        return remote(small_own.at[i], small_got.at[i], small_sems, i, small_peers[i])

    small_copy(0).start()

    def small_step(i):
        small_copy(i).wait_recv()
        small_own[i + 1] = small_own[i] + small_got[i]
        if i + 1 < len(small_peers):
            small_copy(i + 1).start()

    for sums, jobs in ((ff, FF_JOBS), (att, ATT_JOBS)):

        @pl.loop(0, jobs)
        def _(j):
            sums.stage2(j)

    for sums, jobs in ((ff, FF_JOBS), (att, ATT_JOBS)):

        @pl.loop(0, jobs)
        def _(j):
            sums.stage3(j)

    for step in range(1, n_seq - 1):
        for sums, jobs in ((ff, FF_JOBS), (att, ATT_JOBS)):

            @pl.loop(0, jobs)
            def _(j):
                sums.hop(j, step)

    for i in range(len(small_peers)):
        small_step(i)
    for sums, jobs, out, sems in ((ff, FF_JOBS, ff_out, ff_out_sems), (att, ATT_JOBS, att_out, att_out_sems)):

        @pl.loop(0, jobs)
        def _(j):
            sums.finish(j, out, sems)

    small_out[...] = small_own[len(small_peers)]
    for sums, jobs, out, sems in ((ff, FF_JOBS, ff_out, ff_out_sems), (att, ATT_JOBS, att_out, att_out_sems)):

        @pl.loop(0, jobs)
        def _(j):
            sums.drain(j, out, sems)

    for i in range(len(small_peers)):
        small_copy(i).wait_send()
    for copy in rows_back(mixed_ref, mixed_out, 0) + rows_back(branch_ref, tokens_out, 1):
        copy.wait()


def backward(n_dp, n_seq, x, cot, mixed, buckets, gain_one, gain_two, weights, saved):
    span, width = x.shape
    wq, wk, wv, wo, wg, wu, wd = weights
    probs = saved[0]
    heads = probs.shape[0]
    ff_pieces, att_pieces = 2 * FF_JOBS, 2 * ATT_JOBS
    low = lambda *shape: VMEM(shape, LOW)
    dma = pltpu.SemaphoreType.DMA
    steps = 3 + (n_seq - 1).bit_length()

    def sums(pieces, rows):
        return [
            low(pieces, 2, 2, 2, rows, 128), low(pieces, 2, 2, rows, 128), low(pieces, 2, rows, 128),
            low(pieces, rows, 128), low(pieces, rows, 128), low(pieces, rows, 128),
            dma((5, 2, pieces)), dma((pieces,)),
        ]

    pairs = low(heads // 2, span, 128)
    whole = low(width, width)
    any_, vmem = pl.BlockSpec(memory_space=pl.ANY), pl.BlockSpec(memory_space=VMEM)
    return pl.pallas_call(
        functools.partial(backward_kernel, n_dp, n_seq),
        out_shape=[
            jax.ShapeDtypeStruct((n_seq, span // n_seq, width), LOW),
            jax.ShapeDtypeStruct((n_seq, span // n_seq, width), LOW),
            jax.ShapeDtypeStruct((ff_pieces, FF_ROWS, 128), LOW),
            jax.ShapeDtypeStruct((att_pieces, ATT_ROWS, 128), LOW),
            jax.ShapeDtypeStruct((16, width), F32),
        ],
        in_specs=[any_] * 3 + [vmem] * 3 + [any_] * (7 + len(saved)),
        out_specs=[any_] * 4 + [vmem],
        scratch_shapes=sums(ff_pieces, FF_ROWS)
        + sums(att_pieces, ATT_ROWS)
        + [VMEM((steps + 1, 16, width), F32), VMEM((steps, 16, width), F32), dma((2, steps))]
        + [
            whole, whole, whole, whole, low(2, width, 512), low(2, 256, width),
            low(2, 2, span, span), low(2, span, 256), low(2, span, 256),
            low(*saved[3].shape), low(width, span), pairs, pairs, pairs, low(width, span), VMEM((span, width), F32),
            low(width, span), VMEM((span, width), F32), low(span, width), pairs, low(width, span),
            low(width, span), low(span, width), low(span, width), VMEM((16, 1024), F32),
            low(span, width), dma((13,)), dma((5, 2)), dma((2,)), dma((2, 2, n_seq)), dma((2,)),
        ],
        compiler_params=pltpu.CompilerParams(
            collective_id=0, has_side_effects=True, vmem_limit_bytes=VMEM_BYTES
        ),
        name="backward",
    )(x, cot, mixed, buckets, gain_one, gain_two, wq, wk, wv, wo, wg, wu, wd, *saved)


def outputs_kernel(
    n_dp, mixed_ref, tokens_ref, ff_ref, att_ref, small_ref,
    mixed_out, tokens_out, gn_one_out, gq_out, gk_out, gv_out, go_out, table_out, gn_two_out, gg_out, gu_out, gd_out,
):
    mixed_out[...] = mixed_ref[...]
    tokens_out[...] = tokens_ref[...].astype(F32)
    width = mixed_ref.shape[-1]
    shard = width // GROUP
    for j, out in enumerate((go_out, gv_out, gk_out, gq_out)):
        for k in range(2):
            for i in range(width // 256):
                col = width // 2 * k + 128 * i
                out[:, col : col + 128] = att_ref[2 * j + k, shard * i : shard * i + shard, :].astype(F32)
    for p in range(4):
        for i in range(width // 128):
            gd_out[64 * p : 64 * p + 64, 128 * i : 128 * i + 128] = ff_ref[p, 64 * i : 64 * i + 64, :].astype(F32)
    for g in range(4):
        for k, out in enumerate((gg_out, gu_out)):
            for i in range(4):
                col = 512 * g + 128 * i
                out[:, col : col + 128] = ff_ref[4 + 2 * g + k, shard * i : shard * i + shard, :].astype(F32)
    table_out[...] = small_ref[: table_out.shape[1], :128].T[: table_out.shape[0], :]
    mine = lax.axis_index("dp") // (n_dp // GROUP)
    for row, out in ((12, gn_two_out), (13, gn_one_out)):
        total = jnp.zeros((1, shard), F32)
        for s in range(GROUP):
            total = total + jnp.where(mine == s, small_ref[row : row + 1, shard * s : shard * s + shard], 0.0)
        out[...] = total


def outputs(n_dp, buckets, heads, mixed, tokens, ff, att, small):
    width = mixed.shape[-1]
    shard = width // GROUP
    full = lambda *shape: jax.ShapeDtypeStruct(shape, F32)
    return pl.pallas_call(
        functools.partial(outputs_kernel, n_dp),
        out_shape=[
            jax.ShapeDtypeStruct(mixed.shape, LOW), full(*tokens.shape), full(1, shard),
            full(shard, width), full(shard, width), full(shard, width), full(shard, width), full(buckets, heads),
            full(1, shard), full(shard, 2048), full(shard, 2048), full(256, width),
        ],
        compiler_params=pltpu.CompilerParams(vmem_limit_bytes=VMEM_BYTES),
        name="outputs",
    )(mixed, tokens, ff, att, small)


def solution(mesh):
    n_dp, n_seq = mesh.shape["dp"], mesh.shape["seq"]

    def on_device(
        tokens, segments, offset_buckets, norm_attn, w_query, w_key, w_value, w_output, bias_table,
        norm_ff, w_gate, w_up, w_down, cotangent,
    ):
        width = tokens.shape[-1]
        x, seg, cot = [
            lax.all_to_all(v, "seq", split_axis=0, concat_axis=1, tiled=True) for v in (tokens, segments, cotangent)
        ]
        x, cot = x.reshape(-1, width), cot.reshape(-1, width)
        buckets = jnp.pad(offset_buckets, (0, 1)).reshape(1, -1)
        gain_one, gain_two = norm_attn.reshape(1, -1), norm_ff.reshape(1, -1)
        *saved, mixed = forward(
            x, seg, buckets, gain_one, w_query, w_key, w_value, w_output, bias_table, gain_two, w_gate, w_up, w_down
        )
        weights = (w_query, w_key, w_value, w_output, w_gate, w_up, w_down)
        sums = backward(n_dp, n_seq, x, cot, mixed, buckets, gain_one, gain_two, weights, saved)
        results = list(outputs(n_dp, bias_table.shape[0], bias_table.shape[1], *sums))
        results[2], results[8] = results[2].reshape(-1), results[8].reshape(-1)
        rest = n_dp // GROUP
        if rest > 1:
            groups = [[i * rest + j for j in range(rest)] for i in range(GROUP)]
            for i in (2, 3, 4, 5, 6, 8, 9, 10, 11):
                results[i] = lax.psum_scatter(
                    results[i], "dp", scatter_dimension=0, axis_index_groups=groups, tiled=True
                )
            results[7] = lax.psum(results[7], "dp", axis_index_groups=groups)
        return tuple(results)

    rows, shares = P("dp", "seq", None), P("dp", None)
    return jax.shard_map(
        on_device,
        mesh=mesh,
        in_specs=(rows, P("dp", "seq")) + (P(),) * 11 + (rows,),
        out_specs=(rows, rows, P("dp"), shares, shares, shares, shares, P(), P("dp"), shares, shares, shares),
        check_vma=False,
    )
```

```python
import functools

import jax
import jax.numpy as jnp
from jax import lax
from jax.experimental import pallas as pl
from jax.experimental.pallas import tpu as pltpu
from jax.sharding import PartitionSpec as P

MESH = pl.DeviceIdType.MESH
VMEM = pltpu.VMEM
LOW = jnp.bfloat16
F32 = jnp.float32
EPSILON = 1e-06
MASKED = -1e30
GROUP = 8
VMEM_BYTES = 63 * 2**20


def dot(left, right):
    return jnp.dot(left, right, preferred_element_type=F32)


def dot_back(left, right):
    return lax.dot_general(left, right, (((1,), (1,)), ((), ())), preferred_element_type=F32)


def inverse_rms(values):
    return lax.rsqrt(jnp.mean(values * values, -1, keepdims=True) + EPSILON)


def zero_padded(block, half):
    blank = jnp.zeros_like(block)
    return jnp.concatenate([blank, block] if half else [block, blank], axis=0)


class Place:
    def __init__(self, n_dp, n_seq):
        stride = n_dp // GROUP
        dp = lax.axis_index("dp")
        z = lax.axis_index("seq")
        index = dp // stride
        self.n_seq = n_seq
        self.core, self.x, self.y, self.z = index % 2, (index // 2) % 2, index // 4, z
        self.dp = dp
        self.core_peer = (dp + stride * (1 - 2 * self.core), z)
        self.x_peer = (dp + 2 * stride * (1 - 2 * self.x), z)
        self.y_peer = (dp + 4 * stride * (1 - 2 * self.y), z)

    def z_peer(self, z):
        return (self.dp, z)

    def z_pair(self, bit):
        return (self.dp, self.z + bit * (1 - 2 * ((self.z // bit) % 2)))


def remote(src, dst, sems, index, peer):
    return pltpu.make_async_remote_copy(
        src_ref=src, dst_ref=dst, send_sem=sems.at[0, index], recv_sem=sems.at[1, index],
        device_id=peer, device_id_type=MESH,
    )


class Sums:
    def __init__(self, place, own, sems, got0, got1, got2, low_z, high_z):
        self.place, self.own, self.sems = place, own, sems
        self.got0, self.got1, self.got2, self.low_z, self.high_z = got0, got1, got2, low_z, high_z

    def copy0(self, p):
        at = self.place
        return remote(self.own.at[p, 1 - at.core], self.got0.at[p], self.sems.at[0], p, at.core_peer)

    def copy1(self, p, k):
        at = self.place
        mine = self.own.at[p, at.core]
        src = mine.at[1 - at.y] if k else mine.at[:, 1 - at.x]
        return remote(src, self.got1.at[p], self.sems.at[1], p, at.y_peer if k else at.x_peer)

    def copy2(self, p, k):
        at = self.place
        mine = self.own.at[p, at.core]
        src = mine.at[at.y, 1 - at.x] if k else mine.at[1 - at.y, at.x]
        return remote(src, self.got2.at[p], self.sems.at[2], p, at.x_peer if k else at.y_peer)

    def kept(self, p):
        at = self.place
        return self.own.at[p, at.core, at.y, at.x]

    def up(self, p, first):
        src = self.kept(p) if first else self.got2.at[p]
        return remote(src, self.low_z.at[p], self.sems.at[3], p, self.place.z_peer(self.place.z + 1))

    def down(self, p, first):
        src = self.kept(p) if first else self.got1.at[p, 0]
        return remote(src, self.high_z.at[p], self.sems.at[4], p, self.place.z_peer(self.place.z - 1))

    def stage0(self, j):
        for k in range(2):
            self.copy0(2 * j + k).start()

    def stage1(self, j):
        at = self.place
        for k in range(2):
            p = 2 * j + k
            self.copy0(p).wait_recv()
            for a in range(2):
                for b in range(2):
                    self.own[p, at.core, a, b] = self.own[p, at.core, a, b] + self.got0[p, a, b]
            self.copy1(p, k).start()

    def stage2(self, j):
        at = self.place
        for k in range(2):
            p = 2 * j + k
            self.copy1(p, k).wait_recv()
            for a in range(2):
                if k:
                    self.own[p, at.core, at.y, a] = self.own[p, at.core, at.y, a] + self.got1[p, a]
                else:
                    self.own[p, at.core, a, at.x] = self.own[p, at.core, a, at.x] + self.got1[p, a]
            self.copy2(p, k).start()

    def stage3(self, j):
        at = self.place
        for k in range(2):
            p = 2 * j + k
            self.copy2(p, k).wait_recv()
            self.own[p, at.core, at.y, at.x] = self.own[p, at.core, at.y, at.x] + self.got2[p]
        self.hop(j, 0)

    def hop(self, j, step):
        at = self.place
        last = at.n_seq - 1

        @pl.when(at.z == step)
        def _():
            for k in range(2):
                p = 2 * j + k
                if step:
                    self.up(p, False).wait_recv()
                    self.got2[p] = self.low_z[p] + self.own[p, at.core, at.y, at.x]
                self.up(p, step == 0).start()

        @pl.when(at.z == last - step)
        def _():
            for k in range(2):
                p = 2 * j + k
                if step:
                    self.down(p, False).wait_recv()
                    self.got1[p, 0] = self.high_z[p] + self.own[p, at.core, at.y, at.x]
                self.down(p, step == 0).start()

    def finish(self, j, out, out_sems):
        at = self.place
        last = at.n_seq - 1
        for k in range(2):
            p = 2 * j + k

            @pl.when(at.z == last)
            def _():
                self.up(p, False).wait_recv()
                self.low_z[p] = self.low_z[p] + self.own[p, at.core, at.y, at.x]

            @pl.when(at.z == 0)
            def _():
                self.down(p, False).wait_recv()
                self.low_z[p] = self.high_z[p] + self.own[p, at.core, at.y, at.x]

            @pl.when((at.z > 0) & (at.z < last))
            def _():
                total = self.low_z[p].astype(F32) + self.high_z[p].astype(F32)
                self.low_z[p] = (total + self.own[p, at.core, at.y, at.x].astype(F32)).astype(LOW)

            pltpu.make_async_copy(self.low_z.at[p], out.at[p], out_sems.at[p]).start()

    def drain(self, j, out, out_sems):
        at = self.place
        last = at.n_seq - 1
        for k in range(2):
            p = 2 * j + k
            self.copy0(p).wait_send()
            self.copy1(p, k).wait_send()
            self.copy2(p, k).wait_send()

            @pl.when(at.z == 0)
            def _():
                self.up(p, True).wait_send()

            @pl.when((at.z > 0) & (at.z < last))
            def _():
                self.up(p, False).wait_send()
                self.down(p, False).wait_send()

            @pl.when(at.z == last)
            def _():
                self.down(p, True).wait_send()

            pltpu.make_async_copy(self.low_z.at[p], out.at[p], out_sems.at[p]).wait()


FF_JOBS, ATT_JOBS = 6, 4
FF_ROWS, ATT_ROWS = 384, 288


def layer_kernel(
    n_dp, n_seq,
    tokens_hbm, cot_hbm, seg_ref, bucket_ref, gain_one_ref, gain_two_ref, table_ref,
    wq_hbm, wk_hbm, wv_hbm, wo_hbm, wg_hbm, wu_hbm, wd_hbm,
    mixed_out, tokens_out, ff_out, att_out, small_out, probs_hbm, slope_up_hbm, slope_gate_hbm,
    ff_own, ff_got0, ff_got1, ff_got2, ff_low, ff_high, ff_sems, ff_out_sems,
    att_own, att_got0, att_got1, att_got2, att_low, att_high, att_sems, att_out_sems,
    small_own, small_got, small_sems,
    x_ref, cot_ref, seg_send_ref, seg_rows_ref, mixed_ref,
    wq_ref, wk_ref, wv_ref, wo_ref, wgu_ref, wd_ref, probs_ref, slope_up_ref, slope_gate_ref,
    activ_t_ref, attended_t_ref, q_ref, k_ref, v_ref, k_t_ref, resid_ref, acc_ref, branch_ref,
    d_att_t_ref, d_q_t_ref, offset_ref,
    load_sems, ff_load_sems, slope_sems, probs_sems, row_sems, own_sems,
):
    span, width = x_ref.shape
    buckets, heads = table_ref.shape
    buckets_wide = bucket_ref.shape[1]
    head_dim = width // heads
    blocks = span // 128
    pairs = heads // 2
    tiles = wg_hbm.shape[1] // 512
    shard = width // GROUP
    at = Place(n_dp, n_seq)

    loads = [
        pltpu.make_async_copy(src, dst, load_sems.at[i])
        for i, (src, dst) in enumerate([(wq_hbm, wq_ref), (wk_hbm, wk_ref), (wv_hbm, wv_ref), (wo_hbm, wo_ref)])
    ]

    def weight_loads(g, sub):
        cols = pl.ds(pl.multiple_of(g * 512 + sub * 256, 256), 256)
        sides = [
            (wd_hbm.at[cols, :], wd_ref.at[sub]),
            (wg_hbm.at[:, cols], wgu_ref.at[sub, :, pl.ds(0, 256)]),
            (wu_hbm.at[:, cols], wgu_ref.at[sub, :, pl.ds(256, 256)]),
        ]
        return [pltpu.make_async_copy(src, dst, ff_load_sems.at[i, sub]) for i, (src, dst) in enumerate(sides)]

    def slope_copies(g, sub, store):
        sides = [
            (slope_up_hbm.at[2 * g + sub], slope_up_ref.at[sub]),
            (slope_gate_hbm.at[2 * g + sub], slope_gate_ref.at[sub]),
        ]
        return [
            pltpu.make_async_copy(*((dst, src) if store else (src, dst)), slope_sems.at[i, sub])
            for i, (src, dst) in enumerate(sides)
        ]

    def probs_copy(pair, slot, store):
        sides = (probs_hbm.at[pl.ds(2 * pair, 2)], probs_ref.at[slot])
        return pltpu.make_async_copy(*(sides[::-1] if store else sides), probs_sems.at[slot])

    def start(copies):
        for copy in copies:
            copy.start()

    def wait(copies):
        for copy in copies:
            copy.wait()

    start(loads)
    for i in range(n_seq):
        seg_send_ref[i] = jnp.broadcast_to(seg_ref[i : i + 1, :], (8, 128))

    barrier = pltpu.get_barrier_semaphore()
    peers = [at.core_peer, at.x_peer, at.y_peer] + [
        at.z_peer(lax.rem(at.z + i, n_seq)) for i in range(1, n_seq)
    ]
    for peer in peers:
        pl.semaphore_signal(barrier, inc=1, device_id=peer, device_id_type=MESH)
    pl.semaphore_wait(barrier, len(peers))

    ff = Sums(at, ff_own, ff_sems, ff_got0, ff_got1, ff_got2, ff_low, ff_high)
    att = Sums(at, att_own, att_sems, att_got0, att_got1, att_got2, att_low, att_high)

    def block(z):
        return pl.ds(pl.multiple_of(z * 128, 128), 128)

    def exchange(kind, src, dst):
        copies = []
        for i in range(1, n_seq):
            to = lax.rem(at.z + i, n_seq)
            copies.append(
                pltpu.make_async_remote_copy(
                    src_ref=src(to), dst_ref=dst(at.z),
                    send_sem=row_sems.at[kind, 0, i], recv_sem=row_sems.at[kind, 1, i],
                    device_id=at.z_peer(to), device_id_type=MESH,
                )
            )
        copies.append(pltpu.make_async_copy(src(at.z), dst(at.z), own_sems.at[kind]))
        return copies

    segs = exchange(0, lambda z: seg_send_ref.at[z], lambda z: seg_rows_ref.at[z])
    tokens_in = exchange(1, lambda z: tokens_hbm.at[z], lambda z: x_ref.at[block(z), :])
    cot_in = exchange(2, lambda z: cot_hbm.at[z], lambda z: cot_ref.at[block(z), :])
    mixed_back = exchange(3, lambda z: mixed_ref.at[block(z), :], lambda z: mixed_out.at[z])
    tokens_back = exchange(4, lambda z: branch_ref.at[block(z), :], lambda z: tokens_out.at[z])
    start(segs)
    start(tokens_in)
    for sub in range(2):
        start(weight_loads(0, sub))

    def forward(bias_ref, mask_ref):
        one_hot = (lax.broadcasted_iota(jnp.int32, (buckets, buckets_wide), 0) == bucket_ref[...]).astype(F32)
        offset_ref[:heads, :] = lax.dot_general(
            table_ref[...], one_hot, (((0,), (0,)), ((), ())),
            precision=lax.Precision.HIGHEST, preferred_element_type=F32,
        )

        @pl.loop(0, heads)
        def _(h):
            row = offset_ref[pl.ds(h, 1), :]
            for d in range(2 * blocks - 1):
                window = jnp.broadcast_to(row[:, 128 * d : 128 * d + 256], (128, 256))
                bias_ref[h, d] = pltpu.roll(window, 129, 1, stride=1, stride_axis=0)[:, :128].T

        wait(segs)
        seg_rows = [seg_rows_ref[i, 0:1, :].astype(F32) for i in range(blocks)]
        for kb in range(blocks):
            column = jnp.broadcast_to(seg_rows[kb], (128, 128)).T
            for qb in range(blocks):
                mask_ref[128 * kb : 128 * kb + 128, 128 * qb : 128 * qb + 128] = jnp.where(
                    column == seg_rows[qb], 0.0, MASKED
                )
        wait(loads)
        wait(tokens_in)
        start(cot_in)

        @pl.loop(0, blocks)
        def _(i):
            inputs = x_ref[block(i), :].astype(F32)
            branch_ref[block(i), :] = (inputs * inverse_rms(inputs) * gain_one_ref[...]).astype(LOW)

        q_t_ref, v_t_ref = d_att_t_ref, d_q_t_ref
        for tile in range(width // 256):
            cols = slice(256 * tile, 256 * tile + 256)
            q = dot(branch_ref[...], wq_ref[:, cols])
            q_t_ref[cols, :] = q.T.astype(LOW)
            k = dot(branch_ref[...], wk_ref[:, cols])
            k_t_ref[cols, :] = k.T.astype(LOW)
            v = dot(branch_ref[...], wv_ref[:, cols])
            v_t_ref[cols, :] = v.T.astype(LOW)
            for i in range(2):
                lanes = slice(128 * i, 128 * i + 128)
                q_ref[2 * tile + i] = q[:, lanes].astype(LOW)
                k_ref[2 * tile + i] = k[:, lanes].astype(LOW)
                v_ref[2 * tile + i] = v[:, lanes].astype(LOW)

        @pl.loop(0, pairs)
        def _(pair):
            slot = lax.rem(pair, 2)

            @pl.when(pair >= 2)
            def _():
                probs_copy(pair - 2, slot, True).wait()

            keys = k_ref[pair]
            for b in range(2):
                h = 2 * pair + b
                rows = pl.ds(pl.multiple_of(h * head_dim, head_dim), head_dim)
                q_t = zero_padded(q_t_ref[rows, :], b)
                v_t = v_t_ref[rows, :]
                for half in range(span // 256):
                    cols = slice(256 * half, 256 * half + 256)
                    bias = jnp.concatenate(
                        [
                            jnp.concatenate(
                                [bias_ref[h, kb - qb + blocks - 1] for qb in (2 * half, 2 * half + 1)], axis=1
                            )
                            for kb in range(blocks)
                        ],
                        axis=0,
                    )
                    scores = dot(keys, q_t[:, cols]) + bias + mask_ref[:, cols]
                    powers = jnp.exp(scores - jnp.max(scores, axis=0, keepdims=True))
                    probs = (powers * (1.0 / jnp.sum(powers, axis=0, keepdims=True))).astype(LOW)
                    probs_ref[slot, b, :, cols] = probs
                    attended_t_ref[rows, cols] = dot(v_t, probs).astype(LOW)
            probs_copy(pair, slot, True).start()

        attended = attended_t_ref[...].T
        for tile in range(width // 256):
            cols = slice(256 * tile, 256 * tile + 256)
            resid_ref[:, cols] = x_ref[:, cols].astype(F32) + dot(attended, wo_ref[:, cols])

        @pl.loop(0, blocks)
        def _(i):
            resid = resid_ref[block(i), :]
            branch_ref[block(i), :] = (resid * inverse_rms(resid) * gain_two_ref[...]).astype(LOW)
            acc_ref[block(i), :] = resid

        for pair in (pairs - 2, pairs - 1):
            probs_copy(pair, pair % 2, True).wait()

        @pl.loop(0, tiles)
        def _(g):
            for sub in range(2):
                wait(weight_loads(g, sub))
                gate = dot(branch_ref[...], wgu_ref[sub, :, :256])
                upper = dot(branch_ref[...], wgu_ref[sub, :, 256:])
                square = gate * gate
                curve = jnp.tanh(0.7978845608028654 * gate * (1.0 + 0.044715 * square))
                gelu = 0.5 * gate * (1.0 + curve)
                slope = 0.5 * (1.0 + curve) + 0.5 * gate * (1.0 - curve * curve) * (
                    0.7978845608028654 * (1.0 + 3 * 0.044715 * square)
                )
                activ = gelu * upper

                @pl.when(g > 0)
                def _():
                    wait(slope_copies(g - 1, sub, True))

                slope_up_ref[sub] = gelu.astype(LOW)
                slope_gate_ref[sub] = (upper * slope).astype(LOW)
                start(slope_copies(g, sub, True))
                activ_t_ref[2 * g + sub] = activ.T.astype(LOW)
                acc_ref[...] += dot(activ.astype(LOW), wd_ref[sub])
                start(weight_loads(lax.rem(g + 1, tiles), sub))

        mixed_ref[...] = acc_ref[...].astype(LOW)

    pl.run_scoped(
        forward,
        bias_ref=VMEM((heads, 2 * blocks - 1, 128, 128), F32),
        mask_ref=VMEM((span, span), F32),
    )
    start(mixed_back)
    for sub in range(2):
        wait(slope_copies(tiles - 1, sub, True))
        start(slope_copies(0, sub, False))
    wait(cot_in)
    probs_copy(0, 0, False).start()

    def backward(hidden_t_ref, d_att_ref, d_k_ref, d_v_ref):
        for s in range(GROUP):
            product = dot(activ_t_ref[s], cot_ref[...]).astype(LOW)
            for p in range(4):
                for i in range(width // 128):
                    ff_own[p, s % 2, s // 4, (s // 2) % 2, 64 * i : 64 * i + 64, :] = product[
                        64 * p : 64 * p + 64, 128 * i : 128 * i + 128
                    ]
        ff.stage0(0)
        ff.stage0(1)

        @pl.loop(0, blocks)
        def _(i):
            resid = resid_ref[block(i), :]
            hidden_t_ref[:, block(i)] = (resid * inverse_rms(resid) * gain_two_ref[...]).T.astype(LOW)

        ff.stage1(0)
        acc_ref[...] = jnp.zeros_like(acc_ref)

        @pl.loop(0, tiles)
        def _(g):
            job = 2 + g
            for sub in range(2):
                wait(weight_loads(g, sub))
                wait(slope_copies(g, sub, False))
                d_act = dot_back(cot_ref[...], wd_ref[sub])
                d_gate = (d_act * slope_gate_ref[sub].astype(F32)).astype(LOW)
                d_upper = (d_act * slope_up_ref[sub].astype(F32)).astype(LOW)
                for k, d_half in enumerate((d_gate, d_upper)):
                    product = dot(hidden_t_ref[...], d_half).astype(LOW)
                    for s in range(GROUP):
                        for i in range(2):
                            place = shard * (2 * sub + i)
                            ff_own[2 * job + k, s % 2, s // 4, (s // 2) % 2, place : place + shard, :] = product[
                                shard * s : shard * s + shard, 128 * i : 128 * i + 128
                            ]
                if sub:
                    ff.stage0(job)
                d_both = jnp.concatenate([d_gate, d_upper], axis=1)
                for tile in range(width // 256):
                    cols = slice(256 * tile, 256 * tile + 256)
                    acc_ref[:, cols] += dot_back(d_both, wgu_ref[sub, cols, :])

                @pl.when(g < tiles - 1)
                def _():
                    start(weight_loads(g + 1, sub))
                    start(slope_copies(g + 1, sub, False))

            ff.stage1(job - 1)

            @pl.when(g >= 1)
            def _():
                ff.stage2(g - 1)

        def norm_back(vector_ref, gain_ref, extra_ref, low_ref, row):
            total = jnp.zeros((1, width), F32)
            for i in range(blocks):
                rows = slice(128 * i, 128 * i + 128)
                vector = vector_ref[rows, :].astype(F32)
                scale = inverse_rms(vector)
                normed = vector * scale
                grad = acc_ref[rows, :]
                total = total + jnp.sum(grad * normed, axis=0, keepdims=True)
                inner = grad * gain_ref[...]
                result = extra_ref[rows, :].astype(F32) + scale * (
                    inner - normed * jnp.mean(inner * normed, -1, keepdims=True)
                )
                acc_ref[rows, :] = result
                low_ref[rows, :] = result.astype(LOW)
            small_own[0, row : row + 1, :] = total

        norm_back(resid_ref, gain_two_ref, cot_ref, branch_ref, 12)
        ff.stage1(FF_JOBS - 1)

        def share(sums, j, left_t, right):
            for k in range(2):
                half = slice(width // 2 * k, width // 2 * k + width // 2)
                product = dot(left_t, right[:, half]).astype(LOW)
                for s in range(GROUP):
                    for i in range(width // 256):
                        sums.own[2 * j + k, s % 2, s // 4, (s // 2) % 2, shard * i : shard * i + shard, :] = product[
                            shard * s : shard * s + shard, 128 * i : 128 * i + 128
                        ]
            sums.stage0(j)

        share(att, 0, attended_t_ref[...], branch_ref[...])
        for tile in range(width // 256):
            rows = slice(256 * tile, 256 * tile + 256)
            d_att = dot_back(branch_ref[...], wo_ref[rows, :])
            d_att_t_ref[rows, :] = d_att.T.astype(LOW)
            for i in range(2):
                d_att_ref[2 * tile + i] = d_att[:, 128 * i : 128 * i + 128].astype(LOW)
        att.stage1(0)
        left_half = lax.broadcasted_iota(jnp.int32, (span, 128), 1) < head_dim
        flip = (
            lax.broadcasted_iota(jnp.int32, (128, 128), 0) + lax.broadcasted_iota(jnp.int32, (128, 128), 1) == 127
        ).astype(F32)

        @pl.loop(0, pairs)
        def _(pair):
            slot = lax.rem(pair, 2)
            probs_copy(pair, slot, False).wait()

            @pl.when(pair < pairs - 1)
            def _():
                probs_copy(pair + 1, 1 - slot, False).start()

            values = v_ref[pair]
            d_att = d_att_ref[pair]
            queries = q_ref[pair]
            lanes = pl.ds(pl.multiple_of(pair * 128, 128), 128)
            d_values = jnp.zeros((span, 128), F32)
            d_keys = jnp.zeros((span, 128), F32)
            for b in range(2):
                h = 2 * pair + b
                rows = pl.ds(pl.multiple_of(h * head_dim, head_dim), head_dim)
                d_att_t = zero_padded(d_att_t_ref[rows, :], b)
                k_t = k_t_ref[rows, :]
                sides = []
                sums = [None] * (2 * blocks - 1)
                for half in range(span // 256):
                    cols = slice(256 * half, 256 * half + 256)
                    d_probs = dot(values, d_att_t[:, cols])
                    probs = probs_ref[slot, b, :, cols].astype(F32)
                    inner = jnp.sum(probs * d_probs, axis=0, keepdims=True)
                    d_scores = probs * (d_probs - inner)
                    for kb in range(blocks):
                        for i in range(2):
                            d = kb - (2 * half + i) + blocks - 1
                            part = d_scores[128 * kb : 128 * kb + 128, 128 * i : 128 * i + 128]
                            sums[d] = part if sums[d] is None else sums[d] + part
                    d_scores = d_scores.astype(LOW)
                    d_q_t_ref[rows, cols] = dot(k_t, d_scores).astype(LOW)
                    sides.append(d_scores)
                mine = left_half if b == 0 else jnp.logical_not(left_half)
                d_values = d_values + dot(probs_ref[slot, b], jnp.where(mine, d_att, jnp.zeros_like(d_att)))
                d_keys = d_keys + dot(
                    jnp.concatenate(sides, axis=1), jnp.where(mine, queries, jnp.zeros_like(queries))
                )
                totals = []
                for d in range(2 * blocks - 1):
                    flipped = jnp.dot(sums[d], flip, precision=lax.Precision.HIGHEST, preferred_element_type=F32)
                    wide = jnp.concatenate([flipped, jnp.zeros((128, 128), F32)], axis=1)
                    totals.append(jnp.sum(pltpu.roll(wide, 0, 1, stride=1, stride_axis=0), axis=0, keepdims=True))
                pieces = [totals[0][:, :128]]
                for d in range(1, 2 * blocks - 1):
                    pieces.append(totals[d - 1][:, 128:] + totals[d][:, :128])
                pieces.append(totals[-1][:, 128:])
                offset_ref[pl.ds(h, 1), :] = jnp.concatenate(pieces, axis=1)
            d_v_ref[:, lanes] = d_values.astype(LOW)
            d_k_ref[:, lanes] = d_keys.astype(LOW)

            @pl.when(pair < FF_JOBS - 3)
            def _():
                ff.stage2(pair + 3)

            ff.stage3(pair)

            @pl.when(pair >= 1)
            def _():
                ff.hop(pair - 1, 1)

            @pl.when(pair >= 2)
            def _():
                ff.hop(pair - 2, 2)

        @pl.loop(0, blocks)
        def _(i):
            inputs = x_ref[block(i), :].astype(F32)
            hidden_t_ref[:, block(i)] = (inputs * inverse_rms(inputs) * gain_one_ref[...]).T.astype(LOW)

        share(att, 1, hidden_t_ref[...], d_v_ref[...])
        share(att, 2, hidden_t_ref[...], d_k_ref[...])
        att.stage1(1)
        branch_ref[...] = d_q_t_ref[...].T
        share(att, 3, hidden_t_ref[...], branch_ref[...])
        att.stage1(2)
        att.stage2(0)
        for tile in range(width // 256):
            rows = slice(256 * tile, 256 * tile + 256)
            resid_ref[:, rows] = acc_ref[:, rows]
            acc_ref[:, rows] = (
                dot_back(branch_ref[...], wq_ref[rows, :])
                + dot_back(d_k_ref[...], wk_ref[rows, :])
                + dot_back(d_v_ref[...], wv_ref[rows, :])
            )
        att.stage1(3)
        norm_back(x_ref, gain_one_ref, resid_ref, branch_ref, 13)
        start(tokens_back)

    pl.run_scoped(
        backward,
        hidden_t_ref=VMEM((width, span), LOW),
        d_att_ref=VMEM((pairs, span, 128), LOW),
        d_k_ref=VMEM((span, width), LOW),
        d_v_ref=VMEM((span, width), LOW),
    )

    one_hot = (lax.broadcasted_iota(jnp.int32, (128, buckets_wide), 0) == bucket_ref[...]).astype(F32)
    small_own[0, :12, :128] = lax.dot_general(
        offset_ref[:12, :], one_hot, (((1,), (1,)), ((), ())),
        precision=lax.Precision.HIGHEST, preferred_element_type=F32,
    )
    small_peers = [at.core_peer, at.x_peer, at.y_peer]
    bit = 1
    while bit < n_seq:
        small_peers.append(at.z_pair(bit))
        bit *= 2

    def small_copy(i):
        return remote(small_own.at[i], small_got.at[i], small_sems, i, small_peers[i])

    small_copy(0).start()

    def small_step(i):
        small_copy(i).wait_recv()
        small_own[i + 1] = small_own[i] + small_got[i]
        if i + 1 < len(small_peers):
            small_copy(i + 1).start()

    att.stage3(0)
    att.stage2(1)
    ff.hop(FF_JOBS - 1, 1)
    ff.hop(FF_JOBS - 2, 2)
    small_step(0)
    att.stage2(2)
    att.stage3(1)
    att.hop(0, 1)
    ff.hop(FF_JOBS - 1, 2)
    small_step(1)
    att.stage2(3)
    att.stage3(2)
    att.hop(1, 1)
    att.hop(0, 2)
    small_step(2)
    att.stage3(3)
    att.hop(2, 1)
    att.hop(1, 2)
    small_step(3)

    @pl.loop(0, FF_JOBS)
    def _(j):
        ff.finish(j, ff_out, ff_out_sems)

    att.hop(3, 1)
    att.hop(2, 2)
    small_step(4)
    att.hop(3, 2)

    @pl.loop(0, ATT_JOBS)
    def _(j):
        att.finish(j, att_out, att_out_sems)

    small_out[...] = small_own[len(small_peers)]
    for sums, jobs, out, sems in ((ff, FF_JOBS, ff_out, ff_out_sems), (att, ATT_JOBS, att_out, att_out_sems)):

        @pl.loop(0, jobs)
        def _(j):
            sums.drain(j, out, sems)

    for i in range(len(small_peers)):
        small_copy(i).wait_send()
    wait(mixed_back)
    wait(tokens_back)


def layer(n_dp, n_seq, tokens, cot, seg, buckets, gain_one, gain_two, table, weights):
    width = tokens.shape[-1]
    span = tokens.shape[0] * tokens.shape[1]
    heads = table.shape[1]
    ff_width = weights[4].shape[1]
    ff_pieces, att_pieces = 2 * FF_JOBS, 2 * ATT_JOBS
    low = lambda *shape: VMEM(shape, LOW)
    dma = pltpu.SemaphoreType.DMA
    steps = 3 + (n_seq - 1).bit_length()

    def sums(pieces, rows):
        return [
            low(pieces, 2, 2, 2, rows, 128), low(pieces, 2, 2, rows, 128), low(pieces, 2, rows, 128),
            low(pieces, rows, 128), low(pieces, rows, 128), low(pieces, rows, 128),
            dma((5, 2, pieces)), dma((pieces,)),
        ]

    pairs = low(heads // 2, span, 128)
    whole = low(width, width)
    rows, turned = low(span, width), low(width, span)
    any_, vmem = pl.BlockSpec(memory_space=pl.ANY), pl.BlockSpec(memory_space=VMEM)
    result = lambda *shape: jax.ShapeDtypeStruct(shape, LOW)
    return pl.pallas_call(
        functools.partial(layer_kernel, n_dp, n_seq),
        out_shape=[
            result(n_seq, span // n_seq, width), result(n_seq, span // n_seq, width),
            result(ff_pieces, FF_ROWS, 128), result(att_pieces, ATT_ROWS, 128),
            jax.ShapeDtypeStruct((16, width), F32),
            result(heads, span, span), result(ff_width // 256, span, 256), result(ff_width // 256, span, 256),
        ],
        in_specs=[any_] * 2 + [vmem] * 5 + [any_] * 7,
        out_specs=[any_] * 4 + [vmem] + [any_] * 3,
        scratch_shapes=sums(ff_pieces, FF_ROWS)
        + sums(att_pieces, ATT_ROWS)
        + [VMEM((steps + 1, 16, width), F32), VMEM((steps, 16, width), F32), dma((2, steps))]
        + [
            rows, rows, VMEM((n_seq, 8, 128), jnp.int32), VMEM((n_seq, 8, 128), jnp.int32), rows,
            whole, whole, whole, whole, low(2, width, 512), low(2, 256, width),
            low(2, 2, span, span), low(2, span, 256), low(2, span, 256),
            low(ff_width // 256, 256, span), turned, pairs, pairs, pairs, turned, VMEM((span, width), F32),
            VMEM((span, width), F32), rows, turned, turned, VMEM((16, 1024), F32),
            dma((4,)), dma((3, 2)), dma((2, 2)), dma((2,)), dma((5, 2, n_seq)), dma((5,)),
        ],
        compiler_params=pltpu.CompilerParams(
            collective_id=0, has_side_effects=True, vmem_limit_bytes=VMEM_BYTES
        ),
        name="layer",
    )(tokens, cot, seg, buckets, gain_one, gain_two, table, *weights)


def outputs_kernel(
    n_dp, mixed_ref, tokens_ref, ff_ref, att_ref, small_ref,
    mixed_out, tokens_out, gn_one_out, gq_out, gk_out, gv_out, go_out, table_out, gn_two_out, gg_out, gu_out, gd_out,
):
    mixed_out[...] = mixed_ref[...]
    tokens_out[...] = tokens_ref[...].astype(F32)
    width = mixed_ref.shape[-1]
    shard = width // GROUP
    for j, out in enumerate((go_out, gv_out, gk_out, gq_out)):
        for k in range(2):
            for i in range(width // 256):
                col = width // 2 * k + 128 * i
                out[:, col : col + 128] = att_ref[2 * j + k, shard * i : shard * i + shard, :].astype(F32)
    for p in range(4):
        for i in range(width // 128):
            gd_out[64 * p : 64 * p + 64, 128 * i : 128 * i + 128] = ff_ref[p, 64 * i : 64 * i + 64, :].astype(F32)
    for g in range(4):
        for k, out in enumerate((gg_out, gu_out)):
            for i in range(4):
                col = 512 * g + 128 * i
                out[:, col : col + 128] = ff_ref[4 + 2 * g + k, shard * i : shard * i + shard, :].astype(F32)
    table_out[...] = small_ref[: table_out.shape[1], :128].T[: table_out.shape[0], :]
    mine = lax.axis_index("dp") // (n_dp // GROUP)
    for row, out in ((12, gn_two_out), (13, gn_one_out)):
        total = jnp.zeros((1, shard), F32)
        for s in range(GROUP):
            total = total + jnp.where(mine == s, small_ref[row : row + 1, shard * s : shard * s + shard], 0.0)
        out[...] = total


def outputs(n_dp, buckets, heads, mixed, tokens, ff, att, small):
    width = mixed.shape[-1]
    shard = width // GROUP
    full = lambda *shape: jax.ShapeDtypeStruct(shape, F32)
    return pl.pallas_call(
        functools.partial(outputs_kernel, n_dp),
        out_shape=[
            jax.ShapeDtypeStruct(mixed.shape, LOW), full(*tokens.shape), full(1, shard),
            full(shard, width), full(shard, width), full(shard, width), full(shard, width), full(buckets, heads),
            full(1, shard), full(shard, 2048), full(shard, 2048), full(256, width),
        ],
        compiler_params=pltpu.CompilerParams(vmem_limit_bytes=VMEM_BYTES),
        name="outputs",
    )(mixed, tokens, ff, att, small)


def solution(mesh):
    n_dp, n_seq = mesh.shape["dp"], mesh.shape["seq"]

    def on_device(
        tokens, segments, offset_buckets, norm_attn, w_query, w_key, w_value, w_output, bias_table,
        norm_ff, w_gate, w_up, w_down, cotangent,
    ):
        buckets = jnp.pad(offset_buckets, (0, 1)).reshape(1, -1)
        gain_one, gain_two = norm_attn.reshape(1, -1), norm_ff.reshape(1, -1)
        weights = (w_query, w_key, w_value, w_output, w_gate, w_up, w_down)
        sums = layer(
            n_dp, n_seq, tokens, cotangent, segments, buckets, gain_one, gain_two, bias_table, weights
        )[:5]
        results = list(outputs(n_dp, bias_table.shape[0], bias_table.shape[1], *sums))
        results[2], results[8] = results[2].reshape(-1), results[8].reshape(-1)
        rest = n_dp // GROUP
        if rest > 1:
            groups = [[i * rest + j for j in range(rest)] for i in range(GROUP)]
            for i in (2, 3, 4, 5, 6, 8, 9, 10, 11):
                results[i] = lax.psum_scatter(
                    results[i], "dp", scatter_dimension=0, axis_index_groups=groups, tiled=True
                )
            results[7] = lax.psum(results[7], "dp", axis_index_groups=groups)
        return tuple(results)

    rows, shares = P("dp", "seq", None), P("dp", None)
    return jax.shard_map(
        on_device,
        mesh=mesh,
        in_specs=(rows, P("dp", "seq")) + (P(),) * 11 + (rows,),
        out_specs=(rows, rows, P("dp"), shares, shares, shares, shares, P(), P("dp"), shares, shares, shares),
        check_vma=False,
    )
```

```python
import functools

import jax
import jax.numpy as jnp
from jax import lax
from jax.experimental import pallas as pl
from jax.experimental.pallas import tpu as pltpu
from jax.sharding import PartitionSpec as P

MESH = pl.DeviceIdType.MESH
VMEM = pltpu.VMEM
LOW = jnp.bfloat16
F32 = jnp.float32
EPSILON = 1e-06
MASKED = -1e30
GROUP = 8
VMEM_BYTES = 63 * 2**20


def dot(left, right):
    return jnp.dot(left, right, preferred_element_type=F32)


def dot_back(left, right):
    return lax.dot_general(left, right, (((1,), (1,)), ((), ())), preferred_element_type=F32)


def inverse_rms(values):
    return lax.rsqrt(jnp.mean(values * values, -1, keepdims=True) + EPSILON)


def zero_padded(block, half):
    blank = jnp.zeros_like(block)
    return jnp.concatenate([blank, block] if half else [block, blank], axis=0)


class Place:
    def __init__(self, n_dp, n_seq):
        stride = n_dp // GROUP
        dp = lax.axis_index("dp")
        z = lax.axis_index("seq")
        index = dp // stride
        self.n_seq = n_seq
        self.core, self.x, self.y, self.z = index % 2, (index // 2) % 2, index // 4, z
        self.dp = dp
        self.core_peer = (dp + stride * (1 - 2 * self.core), z)
        self.x_peer = (dp + 2 * stride * (1 - 2 * self.x), z)
        self.y_peer = (dp + 4 * stride * (1 - 2 * self.y), z)

    def z_peer(self, z):
        return (self.dp, z)

    def z_pair(self, bit):
        return (self.dp, self.z + bit * (1 - 2 * ((self.z // bit) % 2)))


def remote(src, dst, sems, index, peer):
    return pltpu.make_async_remote_copy(
        src_ref=src, dst_ref=dst, send_sem=sems.at[0, index], recv_sem=sems.at[1, index],
        device_id=peer, device_id_type=MESH,
    )


class Sums:
    def __init__(self, place, own, sems, got0, got1, got2, low_z, high_z):
        self.place, self.own, self.sems = place, own, sems
        self.got0, self.got1, self.got2, self.low_z, self.high_z = got0, got1, got2, low_z, high_z

    def copy0(self, p):
        at = self.place
        return remote(self.own.at[p, 1 - at.core], self.got0.at[p], self.sems.at[0], p, at.core_peer)

    def copy1(self, p, k):
        at = self.place
        mine = self.own.at[p, at.core]
        src = mine.at[1 - at.y] if k else mine.at[:, 1 - at.x]
        return remote(src, self.got1.at[p], self.sems.at[1], p, at.y_peer if k else at.x_peer)

    def copy2(self, p, k):
        at = self.place
        mine = self.own.at[p, at.core]
        src = mine.at[at.y, 1 - at.x] if k else mine.at[1 - at.y, at.x]
        return remote(src, self.got2.at[p], self.sems.at[2], p, at.x_peer if k else at.y_peer)

    def kept(self, p):
        at = self.place
        return self.own.at[p, at.core, at.y, at.x]

    def up(self, p, first):
        src = self.kept(p) if first else self.got2.at[p]
        return remote(src, self.low_z.at[p], self.sems.at[3], p, self.place.z_peer(self.place.z + 1))

    def down(self, p, first):
        src = self.kept(p) if first else self.got1.at[p, 0]
        return remote(src, self.high_z.at[p], self.sems.at[4], p, self.place.z_peer(self.place.z - 1))

    def stage0(self, j):
        for k in range(2):
            self.copy0(2 * j + k).start()

    def stage1(self, j):
        at = self.place
        for k in range(2):
            p = 2 * j + k
            self.copy0(p).wait_recv()
            for a in range(2):
                for b in range(2):
                    self.own[p, at.core, a, b] = self.own[p, at.core, a, b] + self.got0[p, a, b]
            self.copy1(p, k).start()

    def stage2(self, j):
        at = self.place
        for k in range(2):
            p = 2 * j + k
            self.copy1(p, k).wait_recv()
            for a in range(2):
                if k:
                    self.own[p, at.core, at.y, a] = self.own[p, at.core, at.y, a] + self.got1[p, a]
                else:
                    self.own[p, at.core, a, at.x] = self.own[p, at.core, a, at.x] + self.got1[p, a]
            self.copy2(p, k).start()

    def stage3(self, j):
        at = self.place
        for k in range(2):
            p = 2 * j + k
            self.copy2(p, k).wait_recv()
            self.own[p, at.core, at.y, at.x] = self.own[p, at.core, at.y, at.x] + self.got2[p]
        self.hop(j, 0)

    def hop(self, j, step):
        at = self.place
        last = at.n_seq - 1

        @pl.when(at.z == step)
        def _():
            for k in range(2):
                p = 2 * j + k
                if step:
                    self.up(p, False).wait_recv()
                    self.got2[p] = self.low_z[p] + self.own[p, at.core, at.y, at.x]
                self.up(p, step == 0).start()

        @pl.when(at.z == last - step)
        def _():
            for k in range(2):
                p = 2 * j + k
                if step:
                    self.down(p, False).wait_recv()
                    self.got1[p, 0] = self.high_z[p] + self.own[p, at.core, at.y, at.x]
                self.down(p, step == 0).start()

    def finish(self, j, out, out_sems):
        at = self.place
        last = at.n_seq - 1
        for k in range(2):
            p = 2 * j + k

            @pl.when(at.z == last)
            def _():
                self.up(p, False).wait_recv()
                self.low_z[p] = self.low_z[p] + self.own[p, at.core, at.y, at.x]

            @pl.when(at.z == 0)
            def _():
                self.down(p, False).wait_recv()
                self.low_z[p] = self.high_z[p] + self.own[p, at.core, at.y, at.x]

            @pl.when((at.z > 0) & (at.z < last))
            def _():
                total = self.low_z[p].astype(F32) + self.high_z[p].astype(F32)
                self.low_z[p] = (total + self.own[p, at.core, at.y, at.x].astype(F32)).astype(LOW)

            pltpu.make_async_copy(self.low_z.at[p], out.at[p], out_sems.at[p]).start()

    def drain(self, j, out, out_sems):
        at = self.place
        last = at.n_seq - 1
        for k in range(2):
            p = 2 * j + k
            self.copy0(p).wait_send()
            self.copy1(p, k).wait_send()
            self.copy2(p, k).wait_send()

            @pl.when(at.z == 0)
            def _():
                self.up(p, True).wait_send()

            @pl.when((at.z > 0) & (at.z < last))
            def _():
                self.up(p, False).wait_send()
                self.down(p, False).wait_send()

            @pl.when(at.z == last)
            def _():
                self.down(p, True).wait_send()

            pltpu.make_async_copy(self.low_z.at[p], out.at[p], out_sems.at[p]).wait()


FF_JOBS, ATT_JOBS = 6, 4
FF_ROWS, ATT_ROWS = 384, 288


def layer_kernel(
    n_dp, n_seq,
    tokens_hbm, cot_hbm, seg_ref, bucket_ref, gain_one_ref, gain_two_ref, table_ref,
    wq_hbm, wk_hbm, wv_hbm, wo_hbm, wg_hbm, wu_hbm, wd_hbm,
    mixed_out, tokens_out, ff_out, att_out, small_out, probs_hbm, slope_hbm,
    ff_own, ff_got0, ff_got1, ff_got2, ff_low, ff_high, ff_sems, ff_out_sems,
    att_own, att_got0, att_got1, att_got2, att_low, att_high, att_sems, att_out_sems,
    small_own, small_got, small_rows, small_sems, small_row_sems,
    x_ref, cot_ref, seg_send_ref, seg_rows_ref, mixed_ref,
    wo_ref, wgu_ref, wd_ref, probs_ref, inverse_ref,
    activ_t_ref, attended_t_ref, q_ref, k_ref, v_ref, k_t_ref, resid_ref, acc_ref, branch_ref, d_branch_ref,
    d_att_t_ref, d_q_t_ref, offset_ref, diag_ref,
    load_sems, ff_load_sems, probs_sems, row_sems, own_sems,
):
    span, width = x_ref.shape
    heads, buckets = table_ref.shape
    buckets_wide = bucket_ref.shape[1]
    head_dim = width // heads
    blocks = span // 128
    pairs = heads // 2
    tiles = wg_hbm.shape[1] // 512
    shard = width // GROUP
    at = Place(n_dp, n_seq)
    d_back_ref = cot_ref

    wq_ref, wk_ref, wv_ref = wgu_ref.at[0, :, pl.ds(0, width)], wgu_ref.at[1, :, pl.ds(0, width)], wd_ref.at[pl.ds(0, width)]
    loads = [
        pltpu.make_async_copy(src, dst, load_sems.at[i])
        for i, (src, dst) in enumerate([(wq_hbm, wq_ref), (wk_hbm, wk_ref), (wv_hbm, wv_ref)])
    ]
    output_load = pltpu.make_async_copy(wo_hbm, wo_ref, load_sems.at[3])

    def weight_loads(g, slot):
        cols = pl.ds(pl.multiple_of(g * 512, 512), 512)
        sides = [
            (wd_hbm.at[cols, :], wd_ref.at[pl.ds(pl.multiple_of(slot * 512, 512), 512)]),
            (wg_hbm.at[:, cols], wgu_ref.at[slot, :, pl.ds(0, 512)]),
            (wu_hbm.at[:, cols], wgu_ref.at[slot, :, pl.ds(512, 512)]),
        ]
        return [pltpu.make_async_copy(src, dst, ff_load_sems.at[i, slot]) for i, (src, dst) in enumerate(sides)]

    def slope_copy(g, slot, store):
        sides = (slope_hbm.at[g], probs_ref.at[slot])
        return pltpu.make_async_copy(*(sides[::-1] if store else sides), probs_sems.at[slot])

    def probs_copy(pair, slot, store):
        sides = (probs_hbm.at[pl.ds(2 * pair, 2)], probs_ref.at[slot])
        return pltpu.make_async_copy(*(sides[::-1] if store else sides), probs_sems.at[slot])

    def start(copies):
        for copy in copies:
            copy.start()

    def wait(copies):
        for copy in copies:
            copy.wait()

    start(loads)
    output_load.start()
    for i in range(n_seq):
        seg_send_ref[i] = jnp.broadcast_to(seg_ref[i : i + 1, :], (8, 128))

    barrier = pltpu.get_barrier_semaphore()
    peers = [at.core_peer, at.x_peer, at.y_peer] + [
        at.z_peer(lax.rem(at.z + i, n_seq)) for i in range(1, n_seq)
    ]
    for peer in peers:
        pl.semaphore_signal(barrier, inc=1, device_id=peer, device_id_type=MESH)
    pl.semaphore_wait(barrier, len(peers))

    ff = Sums(at, ff_own, ff_sems, ff_got0, ff_got1, ff_got2, ff_low, ff_high)
    att = Sums(at, att_own, att_sems, att_got0, att_got1, att_got2, att_low, att_high)

    def block(z):
        return pl.ds(pl.multiple_of(z * 128, 128), 128)

    def exchange(kind, src, dst):
        copies = []
        for i in range(1, n_seq):
            to = lax.rem(at.z + i, n_seq)
            copies.append(
                pltpu.make_async_remote_copy(
                    src_ref=src(to), dst_ref=dst(at.z),
                    send_sem=row_sems.at[kind, 0, i], recv_sem=row_sems.at[kind, 1, i],
                    device_id=at.z_peer(to), device_id_type=MESH,
                )
            )
        copies.append(pltpu.make_async_copy(src(at.z), dst(at.z), own_sems.at[kind]))
        return copies

    segs = exchange(0, lambda z: seg_send_ref.at[z], lambda z: seg_rows_ref.at[z])
    tokens_in = exchange(1, lambda z: tokens_hbm.at[z], lambda z: x_ref.at[block(z), :])
    cot_in = exchange(2, lambda z: cot_hbm.at[z], lambda z: cot_ref.at[block(z), :])
    mixed_back = exchange(3, lambda z: mixed_ref.at[block(z), :], lambda z: mixed_out.at[z])
    tokens_back = exchange(4, lambda z: d_back_ref.at[block(z), :], lambda z: tokens_out.at[z])
    start(segs)
    start(tokens_in)
    def forward(bias_ref, key_seg_ref, query_seg_ref):
        one_hot = (lax.broadcasted_iota(jnp.int32, (buckets, buckets_wide), 0) == bucket_ref[...]).astype(F32)
        offset_ref[:heads, :] = lax.dot_general(
            table_ref[...], one_hot, (((1,), (0,)), ((), ())),
            precision=lax.Precision.HIGHEST, preferred_element_type=F32,
        )

        @pl.loop(0, heads)
        def _(h):
            row = offset_ref[pl.ds(h, 1), :]
            for d in range(2 * blocks - 1):
                window = jnp.broadcast_to(row[:, 128 * d : 128 * d + 256], (128, 256))
                bias_ref[h, d] = pltpu.roll(window, 129, 1, stride=1, stride_axis=0)[:, :128].T

        wait(segs)
        seg_rows = [seg_rows_ref[i, 0:1, :].astype(F32) for i in range(blocks)]
        for i in range(blocks):
            column = jnp.broadcast_to(seg_rows[i], (128, 128)).T
            across = lax.broadcasted_iota(jnp.int32, (128, 128), 1).astype(F32)
            along = lax.broadcasted_iota(jnp.int32, (128, 128), 0).astype(F32)
            key_seg_ref[128 * i : 128 * i + 128, :] = jnp.where(column == across, 1.0, 0.0).astype(LOW)
            query_seg_ref[:, 128 * i : 128 * i + 128] = jnp.where(seg_rows[i] == along, 0.0, MASKED).astype(LOW)
        wait(loads)
        wait(tokens_in)
        start(cot_in)

        @pl.loop(0, blocks)
        def _(i):
            inputs = x_ref[block(i), :].astype(F32)
            branch_ref[block(i), :] = (inputs * inverse_rms(inputs) * gain_one_ref[...]).astype(LOW)

        q_t_ref, v_t_ref = d_att_t_ref, d_q_t_ref
        for tile in range(width // 256):
            cols = slice(256 * tile, 256 * tile + 256)
            q = dot(branch_ref[...], wq_ref[:, cols])
            q_t_ref[cols, :] = q.T.astype(LOW)
            k = dot(branch_ref[...], wk_ref[:, cols])
            k_t_ref[cols, :] = k.T.astype(LOW)
            v = dot(branch_ref[...], wv_ref[:, cols])
            v_t_ref[cols, :] = v.T.astype(LOW)
            for i in range(2):
                lanes = slice(128 * i, 128 * i + 128)
                q_ref[2 * tile + i] = q[:, lanes].astype(LOW)
                k_ref[2 * tile + i] = k[:, lanes].astype(LOW)
                v_ref[2 * tile + i] = v[:, lanes].astype(LOW)

        start(weight_loads(0, 0))
        score_refs = (acc_ref, resid_ref)

        def put_scores(pair, b):
            rows = pl.ds(pl.multiple_of((2 * pair + b) * head_dim, head_dim), head_dim)
            keys = jnp.concatenate([k_ref[pair], key_seg_ref[...]], axis=1)
            q_t = jnp.concatenate([zero_padded(q_t_ref[rows, :], b), query_seg_ref[...]], axis=0)

            def half_of(half):
                cols = slice(256 * half, 256 * half + 256)
                score_refs[b][:, cols] = dot(keys, q_t[:, cols])

            return half_of

        def put_attended(pair, b, slot):
            h = 2 * pair + b
            rows = pl.ds(pl.multiple_of(h * head_dim, head_dim), head_dim)
            v_t = v_t_ref[rows, :]

            def half_of(half):
                cols = slice(256 * half, 256 * half + 256)
                bias = jnp.concatenate(
                    [
                        jnp.concatenate(
                            [bias_ref[h, kb - qb + blocks - 1] for qb in (2 * half, 2 * half + 1)], axis=1
                        )
                        for kb in range(blocks)
                    ],
                    axis=0,
                )
                scores = score_refs[b][:, cols] + bias
                powers = jnp.exp(scores - jnp.max(scores, axis=0, keepdims=True))
                inverse = 1.0 / jnp.sum(powers, axis=0, keepdims=True)
                probs = powers.astype(LOW)
                probs_ref[slot, b, :, cols] = probs
                attended_t_ref[rows, cols] = (dot(v_t, probs) * inverse).astype(LOW)
                inverse_ref[pl.ds(h, 1), cols] = inverse

            return half_of

        first = put_scores(0, 0)
        for half in range(2):
            first(half)

        @pl.loop(0, pairs)
        def _(pair):
            slot = lax.rem(pair, 2)

            @pl.when(pair >= 2)
            def _():
                probs_copy(pair - 2, slot, True).wait()

            for b in range(2):
                ahead = put_scores(pair, 1) if b == 0 else put_scores(jnp.minimum(pair + 1, pairs - 1), 0)
                now = put_attended(pair, b, slot)
                for half in range(2):
                    ahead(half)
                    now(half)
            probs_copy(pair, slot, True).start()

        output_load.wait()
        attended = attended_t_ref[...].T
        for tile in range(width // 256):
            cols = slice(256 * tile, 256 * tile + 256)
            resid_ref[:, cols] = x_ref[:, cols].astype(F32) + dot(attended, wo_ref[:, cols])

        @pl.loop(0, blocks)
        def _(i):
            resid = resid_ref[block(i), :]
            branch_ref[block(i), :] = (resid * inverse_rms(resid) * gain_two_ref[...]).astype(LOW)
            acc_ref[block(i), :] = resid

        for pair in (pairs - 2, pairs - 1):
            probs_copy(pair, pair % 2, True).wait()

        @pl.loop(0, tiles)
        def _(g):
            slot = lax.rem(g, 2)

            @pl.when(g >= 2)
            def _():
                slope_copy(g - 2, slot, True).wait()

            wait(weight_loads(g, slot))
            start(weight_loads(lax.rem(g + 1, tiles), 1 - slot))
            gates = [dot(branch_ref[...], wgu_ref[slot, :, 256 * i : 256 * i + 256]) for i in range(4)]
            activs = []
            for sub in range(2):
                gate, upper = gates[sub], gates[2 + sub]
                lanes = slice(256 * sub, 256 * sub + 256)
                square = gate * gate
                curve = jnp.tanh(0.7978845608028654 * gate * (1.0 + 0.044715 * square))
                gelu = 0.5 * gate * (1.0 + curve)
                slope = 0.5 * (1.0 + curve) + 0.5 * gate * (1.0 - curve * curve) * (
                    0.7978845608028654 * (1.0 + 3 * 0.044715 * square)
                )
                activ = gelu * upper
                probs_ref[slot, 0, :, lanes] = gelu.astype(LOW)
                probs_ref[slot, 1, :, lanes] = (upper * slope).astype(LOW)
                activ_t_ref[2 * g + sub] = activ.T.astype(LOW)
                activs.append(activ.astype(LOW))
            down = wd_ref[pl.ds(pl.multiple_of(slot * 512, 512), 512)]
            acc_ref[...] += dot(jnp.concatenate(activs, axis=1), down)
            slope_copy(g, slot, True).start()

        mixed_ref[...] = acc_ref[...].astype(LOW)

    pl.run_scoped(
        forward,
        bias_ref=VMEM((heads, 2 * blocks - 1, 128, 128), F32),
        key_seg_ref=VMEM((span, 128), LOW),
        query_seg_ref=VMEM((128, span), LOW),
    )
    start(mixed_back)
    for g in (tiles - 2, tiles - 1):
        slope_copy(g, g % 2, True).wait()
    slope_copy(0, 0, False).start()
    wait(cot_in)

    def backward(hidden_t_ref, d_att_ref, d_k_ref, d_v_ref, d_probs_ref):
        for s in range(GROUP):
            product = dot(activ_t_ref[s], cot_ref[...]).astype(LOW)
            for p in range(4):
                for i in range(width // 128):
                    ff_own[p, s % 2, s // 4, (s // 2) % 2, 64 * i : 64 * i + 64, :] = product[
                        64 * p : 64 * p + 64, 128 * i : 128 * i + 128
                    ]
        ff.stage0(0)
        ff.stage0(1)

        acc_ref[...] = jnp.zeros_like(acc_ref)

        def d_slot(g, k, lanes, half):
            n = 2 * lanes + half
            return att_own.at[2 * g + k, n // 4, (n // 2) % 2, n % 2, pl.ds(0, 256), :]

        @pl.loop(0, tiles)
        def _(g):
            slot = lax.rem(g, 2)
            wait(weight_loads(g, slot))
            slope_copy(g, slot, False).wait()

            @pl.when(g < tiles - 1)
            def _():
                start(weight_loads(g + 1, 1 - slot))
                slope_copy(g + 1, 1 - slot, False).start()

            d_sides = [[], []]
            for sub in range(2):
                lanes = slice(256 * sub, 256 * sub + 256)
                down = wd_ref[pl.ds(pl.multiple_of(slot * 512 + 256 * sub, 256), 256)]
                d_act = dot_back(cot_ref[...], down)
                for k in range(2):
                    d_side = (d_act * probs_ref[slot, 1 - k, :, lanes].astype(F32)).astype(LOW)
                    d_sides[k].append(d_side)
                    for i in range(2):
                        for half in range(2):
                            d_slot(g, k, 2 * sub + i, half)[...] = d_side[
                                256 * half : 256 * half + 256, 128 * i : 128 * i + 128
                            ]
            d_both = jnp.concatenate(d_sides[0] + d_sides[1], axis=1)
            for tile in range(width // 256):
                cols = slice(256 * tile, 256 * tile + 256)
                acc_ref[:, cols] += dot_back(d_both, wgu_ref[slot, cols, :])

            @pl.when(g <= 1)
            def _():
                ff.stage1(g)

        start(loads)
        probs_copy(0, 0, False).start()

        @pl.loop(0, blocks)
        def _(i):
            resid = resid_ref[block(i), :]
            hidden_t_ref[:, block(i)] = (resid * inverse_rms(resid) * gain_two_ref[...]).T.astype(LOW)

        ff.stage2(0)

        def products(g):
            for k in range(2):
                for sub in range(2):
                    right = jnp.concatenate(
                        [
                            jnp.concatenate([d_slot(g, k, 2 * sub + i, half)[...] for half in range(2)], axis=0)
                            for i in range(2)
                        ],
                        axis=1,
                    )
                    product = dot(hidden_t_ref[...], right).astype(LOW)
                    for s in range(GROUP):
                        for i in range(2):
                            place = shard * (2 * sub + i)
                            ff_own[4 + 2 * g + k, s % 2, s // 4, (s // 2) % 2, place : place + shard, :] = product[
                                shard * s : shard * s + shard, 128 * i : 128 * i + 128
                            ]
            ff.stage0(2 + g)

        def norm_back(vector_ref, gain_ref, extra_ref, low_ref, row):
            total = jnp.zeros((1, width), F32)
            for i in range(blocks):
                rows = slice(128 * i, 128 * i + 128)
                vector = vector_ref[rows, :].astype(F32)
                scale = inverse_rms(vector)
                normed = vector * scale
                grad = acc_ref[rows, :]
                total = total + jnp.sum(grad * normed, axis=0, keepdims=True)
                inner = grad * gain_ref[...]
                result = extra_ref[rows, :].astype(F32) + scale * (
                    inner - normed * jnp.mean(inner * normed, -1, keepdims=True)
                )
                acc_ref[rows, :] = result
                low_ref[rows, :] = result.astype(LOW)
            for i in range(width // 128):
                small_own[0, row + i : row + i + 1, :] = total[:, 128 * i : 128 * i + 128]

        norm_back(resid_ref, gain_two_ref, cot_ref, d_branch_ref, 12)
        products(0)

        def share(sums, j, left_t, right):
            for k in range(2):
                half = slice(width // 2 * k, width // 2 * k + width // 2)
                product = dot(left_t, right[:, half]).astype(LOW)
                for s in range(GROUP):
                    for i in range(width // 256):
                        sums.own[2 * j + k, s % 2, s // 4, (s // 2) % 2, shard * i : shard * i + shard, :] = product[
                            shard * s : shard * s + shard, 128 * i : 128 * i + 128
                        ]
            sums.stage0(j)

        for tile in range(width // 256):
            rows = slice(256 * tile, 256 * tile + 256)
            d_att_t = dot_back(d_branch_ref[...], wo_ref[rows, :]).T
            for i in range(256 // head_dim):
                h = 256 // head_dim * tile + i
                d_att_t_ref[head_dim * h : head_dim * (h + 1), :] = (
                    d_att_t[head_dim * i : head_dim * (i + 1), :] * inverse_ref[h : h + 1, :]
                ).astype(LOW)
            for i in range(2):
                d_att_ref[2 * tile + i] = d_att_t_ref[256 * tile + 128 * i : 256 * tile + 128 * i + 128, :].T
        left_half = lax.broadcasted_iota(jnp.int32, (span, 128), 1) < head_dim
        d_probs_refs = (resid_ref, d_probs_ref)

        def put_d_probs(pair, b):
            rows = pl.ds(pl.multiple_of((2 * pair + b) * head_dim, head_dim), head_dim)
            values = v_ref[pair]
            d_att_t = zero_padded(d_att_t_ref[rows, :], b)

            def half_of(half):
                cols = slice(256 * half, 256 * half + 256)
                d_probs_refs[b][:, cols] = dot(values, d_att_t[:, cols])

            return half_of

        across = lax.broadcasted_iota(jnp.int32, (8, 128), 1)

        def put_d_scores(pair, b, slot):
            h = 2 * pair + b
            rows = pl.ds(pl.multiple_of(h * head_dim, head_dim), head_dim)
            k_t = k_t_ref[rows, :]
            sums = [None] * (2 * blocks - 1)

            def half_of(half):
                cols = slice(256 * half, 256 * half + 256)
                d_probs = d_probs_refs[b][:, cols]
                probs = probs_ref[slot, b, :, cols].astype(F32)
                inner = jnp.sum(probs * d_probs, axis=0, keepdims=True) * inverse_ref[pl.ds(h, 1), cols]
                d_scores = probs * (d_probs - inner)
                for kb in range(blocks):
                    for i in range(2):
                        d = kb - (2 * half + i) + blocks - 1
                        part = d_scores[128 * kb : 128 * kb + 128, 128 * i : 128 * i + 128]
                        sums[d] = part if sums[d] is None else sums[d] + part
                d_scores = d_scores.astype(LOW)
                for i in range(2):
                    activ_t_ref[2 * b + i, :, cols] = d_scores[256 * i : 256 * i + 256, :]
                d_q_t_ref[rows, cols] = dot(k_t, d_scores).astype(LOW)
                if half == 1:
                    for d in range(2 * blocks - 1):
                        every, low_lanes = sums[d][:8, :], sums[d][:8, :]
                        for a in range(1, 16):
                            rolled = pltpu.roll(sums[d][8 * a : 8 * a + 8, :], 128 - 8 * a, 1)
                            every = every + rolled
                            low_lanes = low_lanes + jnp.where(across < 128 - 8 * a, rolled, 0.0)
                        diag_ref[h, d] = jnp.concatenate([low_lanes, every - low_lanes], axis=1)

            return half_of

        first = put_d_probs(0, 0)
        for half in range(2):
            first(half)

        @pl.loop(0, pairs)
        def _(pair):
            slot = lax.rem(pair, 2)
            probs_copy(pair, slot, False).wait()

            @pl.when(pair < pairs - 1)
            def _():
                probs_copy(pair + 1, 1 - slot, False).start()

            for b in range(2):
                ahead = put_d_probs(pair, 1) if b == 0 else put_d_probs(jnp.minimum(pair + 1, pairs - 1), 0)
                now = put_d_scores(pair, b, slot)
                for half in range(2):
                    ahead(half)
                    now(half)
            lanes = pl.ds(pl.multiple_of(pair * 128, 128), 128)
            d_att, queries = d_att_ref[pair], q_ref[pair]
            blank = jnp.zeros_like(d_att)
            d_scores = [activ_t_ref[2 * b : 2 * b + 2].reshape(span, span) for b in range(2)]
            d_v_ref[:, lanes] = (
                dot(probs_ref[slot, 0], jnp.where(left_half, d_att, blank))
                + dot(probs_ref[slot, 1], jnp.where(left_half, blank, d_att))
            ).astype(LOW)
            d_k_ref[:, lanes] = (
                dot(d_scores[0], jnp.where(left_half, queries, blank))
                + dot(d_scores[1], jnp.where(left_half, blank, queries))
            ).astype(LOW)
            @pl.when(lax.rem(pair, 2) == 1)
            def _():
                products((pair + 1) // 2)

            @pl.when(pair == 0)
            def _():
                ff.stage1(2)
                ff.stage2(1)

            @pl.when(pair == 1)
            def _():
                ff.stage3(0)

            @pl.when(pair == 2)
            def _():
                ff.stage1(3)

            @pl.when(pair == 3)
            def _():
                ff.stage2(2)
                ff.stage3(1)

            @pl.when(pair == 4)
            def _():
                ff.stage1(4)
                ff.hop(0, 1)

            @pl.when(pair == 5)
            def _():
                ff.stage2(3)

        branch_ref[...] = d_q_t_ref[...].T
        wait(loads)
        for tile in range(width // 256):
            rows = slice(256 * tile, 256 * tile + 256)
            resid_ref[:, rows] = acc_ref[:, rows]
            acc_ref[:, rows] = (
                dot_back(branch_ref[...], wgu_ref[0, rows, :width])
                + dot_back(d_k_ref[...], wgu_ref[1, rows, :width])
                + dot_back(d_v_ref[...], wd_ref[rows, :])
            )
        ff.stage1(5)
        ff.stage3(2)
        norm_back(x_ref, gain_one_ref, resid_ref, d_back_ref, 18)
        ff.hop(1, 1)
        ff.hop(0, 2)
        start(tokens_back)
        share(att, 0, attended_t_ref[...], d_branch_ref[...])

        @pl.loop(0, blocks)
        def _(i):
            inputs = x_ref[block(i), :].astype(F32)
            hidden_t_ref[:, block(i)] = (inputs * inverse_rms(inputs) * gain_one_ref[...]).T.astype(LOW)

        ff.stage2(4)
        att.stage1(0)
        share(att, 1, hidden_t_ref[...], d_v_ref[...])
        ff.stage3(3)
        share(att, 2, hidden_t_ref[...], d_k_ref[...])
        share(att, 3, hidden_t_ref[...], branch_ref[...])

    pl.run_scoped(
        backward,
        hidden_t_ref=VMEM((width, span), LOW),
        d_att_ref=VMEM((pairs, span, 128), LOW),
        d_k_ref=VMEM((span, width), LOW),
        d_v_ref=VMEM((span, width), LOW),
        d_probs_ref=VMEM((span, span), F32),
    )

    ff.hop(2, 1)
    ff.hop(1, 2)
    ff.stage2(5)
    att.stage1(1)

    flip = (
        lax.broadcasted_iota(jnp.int32, (256, 256), 0) + lax.broadcasted_iota(jnp.int32, (256, 256), 1) == 255
    ).astype(F32)

    @pl.loop(0, heads)
    def _(h):
        tiles_ = diag_ref[h].reshape(8 * (2 * blocks - 1), 256)
        flipped = jnp.dot(tiles_, flip, precision=lax.Precision.HIGHEST, preferred_element_type=F32)
        totals = [
            jnp.sum(pltpu.roll(flipped[8 * d : 8 * d + 8, :], 0, 1, stride=1, stride_axis=0), axis=0, keepdims=True)
            for d in range(2 * blocks - 1)
        ]
        pieces = [totals[0][:, 128:]]
        for d in range(1, 2 * blocks - 1):
            pieces.append(totals[d - 1][:, :128] + totals[d][:, 128:])
        pieces.append(totals[-1][:, :128])
        offset_ref[pl.ds(h, 1), :] = jnp.concatenate(pieces, axis=1)

    one_hot = (lax.broadcasted_iota(jnp.int32, (128, buckets_wide), 0) == bucket_ref[...]).astype(F32)
    small_own[0, :12, :] = lax.dot_general(
        offset_ref[:12, :], one_hot, (((1,), (1,)), ((), ())),
        precision=lax.Precision.HIGHEST, preferred_element_type=F32,
    )
    small_peers = [at.core_peer, at.x_peer, at.y_peer]
    steps = len(small_peers)

    def small_copy(i):
        return remote(small_own.at[i], small_got.at[i], small_sems, i, small_peers[i])

    def small_row(i):
        return pltpu.make_async_remote_copy(
            src_ref=small_own.at[steps], dst_ref=small_rows.at[at.z],
            send_sem=small_row_sems.at[0, i], recv_sem=small_row_sems.at[1, i],
            device_id=at.z_peer(lax.rem(at.z + i, n_seq)), device_id_type=MESH,
        )

    def small_step(i):
        small_copy(i).wait_recv()
        small_own[i + 1] = small_own[i] + small_got[i]
        if i + 1 < steps:
            small_copy(i + 1).start()

    small_copy(0).start()
    ff.stage3(4)
    att.stage2(0)
    att.stage1(2)
    small_step(0)
    ff.stage3(5)
    att.stage2(1)
    att.stage1(3)
    att.stage3(0)
    ff.hop(3, 1)
    att.stage2(2)
    small_step(1)
    att.stage3(1)
    ff.hop(2, 2)
    ff.hop(4, 1)
    att.stage2(3)
    small_step(2)
    small_rows[at.z] = small_own[steps]
    att.stage3(2)
    ff.hop(3, 2)
    ff.hop(5, 1)
    att.stage3(3)
    for i in range(1, n_seq):
        small_row(i).start()
    ff.hop(4, 2)
    att.hop(0, 1)
    ff.hop(5, 2)
    att.hop(1, 1)
    att.hop(0, 2)
    att.hop(2, 1)
    att.hop(1, 2)
    att.hop(3, 1)
    att.hop(2, 2)
    att.hop(3, 2)

    @pl.loop(0, FF_JOBS)
    def _(j):
        ff.finish(j, ff_out, ff_out_sems)

    @pl.loop(0, ATT_JOBS)
    def _(j):
        att.finish(j, att_out, att_out_sems)

    for i in range(1, n_seq):
        small_row(i).wait_recv()
    total = small_rows[0]
    for i in range(1, n_seq):
        total = total + small_rows[i]
    small_out[...] = total
    for sums, jobs, out, sems in ((ff, FF_JOBS, ff_out, ff_out_sems), (att, ATT_JOBS, att_out, att_out_sems)):

        @pl.loop(0, jobs)
        def _(j):
            sums.drain(j, out, sems)

    for i in range(steps):
        small_copy(i).wait_send()
    for i in range(1, n_seq):
        small_row(i).wait_send()
    wait(mixed_back)
    wait(tokens_back)


def layer(n_dp, n_seq, tokens, cot, seg, buckets, gain_one, gain_two, table, weights):
    width = tokens.shape[-1]
    span = tokens.shape[0] * tokens.shape[1]
    heads = table.shape[0]
    ff_width = weights[4].shape[1]
    ff_pieces, att_pieces = 2 * FF_JOBS, 2 * ATT_JOBS
    low = lambda *shape: VMEM(shape, LOW)
    dma = pltpu.SemaphoreType.DMA
    steps = 3

    def sums(pieces, rows):
        return [
            low(pieces, 2, 2, 2, rows, 128), low(pieces, 2, 2, rows, 128), low(pieces, 2, rows, 128),
            low(pieces, rows, 128), low(pieces, rows, 128), low(pieces, rows, 128),
            dma((5, 2, pieces)), dma((pieces,)),
        ]

    pairs = low(heads // 2, span, 128)
    rows, turned = low(span, width), low(width, span)
    any_, vmem = pl.BlockSpec(memory_space=pl.ANY), pl.BlockSpec(memory_space=VMEM)
    result = lambda *shape: jax.ShapeDtypeStruct(shape, LOW)
    return pl.pallas_call(
        functools.partial(layer_kernel, n_dp, n_seq),
        out_shape=[
            result(n_seq, span // n_seq, width), result(n_seq, span // n_seq, width),
            result(ff_pieces, FF_ROWS, 128), result(att_pieces, ATT_ROWS, 128),
            jax.ShapeDtypeStruct((24, 128), F32),
            result(heads, span, span), result(ff_width // 512, 2, span, 512),
        ],
        in_specs=[any_] * 2 + [vmem] * 5 + [any_] * 7,
        out_specs=[any_] * 4 + [vmem] + [any_] * 2,
        scratch_shapes=sums(ff_pieces, FF_ROWS)
        + sums(att_pieces, ATT_ROWS)
        + [
            VMEM((steps + 1, 24, 128), F32), VMEM((steps, 24, 128), F32), VMEM((n_seq, 24, 128), F32),
            dma((2, steps)), dma((2, n_seq)),
        ]
        + [
            rows, rows, VMEM((n_seq, 8, 128), jnp.int32), VMEM((n_seq, 8, 128), jnp.int32), rows,
            low(width, width), low(2, width, 1024), low(1024, width), low(2, 2, span, span), VMEM((16, span), F32),
            low(ff_width // 256, 256, span), turned, pairs, pairs, pairs, turned, VMEM((span, width), F32),
            VMEM((span, width), F32), rows, rows, turned, turned, VMEM((16, 1024), F32),
            VMEM((heads, 2 * (span // 128) - 1, 8, 256), F32),
            dma((4,)), dma((3, 2)), dma((2,)), dma((5, 2, n_seq)), dma((5,)),
        ],
        compiler_params=pltpu.CompilerParams(
            collective_id=0, has_side_effects=True, vmem_limit_bytes=VMEM_BYTES
        ),
        name="layer",
    )(tokens, cot, seg, buckets, gain_one, gain_two, table, *weights)


def outputs_kernel(
    n_dp, mixed_ref, tokens_ref, ff_ref, att_ref, small_ref,
    mixed_out, tokens_out, gn_one_out, gq_out, gk_out, gv_out, go_out, table_out, gn_two_out, gg_out, gu_out, gd_out,
):
    mixed_out[...] = mixed_ref[...]
    tokens_out[...] = tokens_ref[...].astype(F32)
    width = mixed_ref.shape[-1]
    shard = width // GROUP
    for j, out in enumerate((go_out, gv_out, gk_out, gq_out)):
        for k in range(2):
            for i in range(width // 256):
                col = width // 2 * k + 128 * i
                out[:, col : col + 128] = att_ref[2 * j + k, shard * i : shard * i + shard, :].astype(F32)
    for p in range(4):
        for i in range(width // 128):
            gd_out[64 * p : 64 * p + 64, 128 * i : 128 * i + 128] = ff_ref[p, 64 * i : 64 * i + 64, :].astype(F32)
    for g in range(4):
        for k, out in enumerate((gg_out, gu_out)):
            for i in range(4):
                col = 512 * g + 128 * i
                out[:, col : col + 128] = ff_ref[4 + 2 * g + k, shard * i : shard * i + shard, :].astype(F32)
    table_out[...] = small_ref[: table_out.shape[0], : table_out.shape[1]]
    mine = lax.axis_index("dp") // (n_dp // GROUP)
    for row, out in ((12, gn_two_out), (18, gn_one_out)):
        gains = jnp.concatenate([small_ref[row + i : row + i + 1, :] for i in range(width // 128)], axis=1)
        total = jnp.zeros((1, shard), F32)
        for s in range(GROUP):
            total = total + jnp.where(mine == s, gains[:, shard * s : shard * s + shard], 0.0)
        out[...] = total


def outputs(n_dp, buckets, heads, mixed, tokens, ff, att, small):
    width = mixed.shape[-1]
    shard = width // GROUP
    full = lambda *shape: jax.ShapeDtypeStruct(shape, F32)
    return pl.pallas_call(
        functools.partial(outputs_kernel, n_dp),
        out_shape=[
            jax.ShapeDtypeStruct(mixed.shape, LOW), full(*tokens.shape), full(1, shard),
            full(shard, width), full(shard, width), full(shard, width), full(shard, width), full(heads, buckets),
            full(1, shard), full(shard, 2048), full(shard, 2048), full(256, width),
        ],
        compiler_params=pltpu.CompilerParams(vmem_limit_bytes=VMEM_BYTES),
        name="outputs",
    )(mixed, tokens, ff, att, small)


def solution(mesh):
    n_dp, n_seq = mesh.shape["dp"], mesh.shape["seq"]

    def on_device(
        tokens, segments, offset_buckets, norm_attn, w_query, w_key, w_value, w_output, bias_table,
        norm_ff, w_gate, w_up, w_down, cotangent,
    ):
        buckets = jnp.pad(offset_buckets, (0, 1)).reshape(1, -1)
        gain_one, gain_two = norm_attn.reshape(1, -1), norm_ff.reshape(1, -1)
        weights = (w_query, w_key, w_value, w_output, w_gate, w_up, w_down)
        sums = layer(
            n_dp, n_seq, tokens, cotangent, segments, buckets, gain_one, gain_two, bias_table.T, weights
        )[:5]
        results = list(outputs(n_dp, bias_table.shape[0], bias_table.shape[1], *sums))
        results[2], results[7], results[8] = results[2].reshape(-1), results[7].T, results[8].reshape(-1)
        rest = n_dp // GROUP
        if rest > 1:
            groups = [[i * rest + j for j in range(rest)] for i in range(GROUP)]
            for i in (2, 3, 4, 5, 6, 8, 9, 10, 11):
                results[i] = lax.psum_scatter(
                    results[i], "dp", scatter_dimension=0, axis_index_groups=groups, tiled=True
                )
            results[7] = lax.psum(results[7], "dp", axis_index_groups=groups)
        return tuple(results)

    rows, shares = P("dp", "seq", None), P("dp", None)
    return jax.shard_map(
        on_device,
        mesh=mesh,
        in_specs=(rows, P("dp", "seq")) + (P(),) * 11 + (rows,),
        out_specs=(rows, rows, P("dp"), shares, shares, shares, shares, P(), P("dp"), shares, shares, shares),
        check_vma=False,
    )
```

```python
import functools

import jax
import jax.numpy as jnp
from jax import lax
from jax.experimental import pallas as pl
from jax.experimental.pallas import tpu as pltpu
from jax.sharding import PartitionSpec as P

MESH = pl.DeviceIdType.MESH
VMEM = pltpu.VMEM
LOW = jnp.bfloat16
F32 = jnp.float32
EPSILON = 1e-06
MASKED = -1e30
GROUP = 8
VMEM_BYTES = 63 * 2**20


def dot(left, right):
    return jnp.dot(left, right, preferred_element_type=F32)


def dot_back(left, right):
    return lax.dot_general(left, right, (((1,), (1,)), ((), ())), preferred_element_type=F32)


def inverse_rms(values):
    return lax.rsqrt(jnp.mean(values * values, -1, keepdims=True) + EPSILON)


def zero_padded(block, half):
    blank = jnp.zeros_like(block)
    return jnp.concatenate([blank, block] if half else [block, blank], axis=0)


class Place:
    def __init__(self, n_dp, n_seq):
        stride = n_dp // GROUP
        dp = lax.axis_index("dp")
        z = lax.axis_index("seq")
        index = dp // stride
        self.n_seq = n_seq
        self.core, self.x, self.y, self.z = index % 2, (index // 2) % 2, index // 4, z
        self.dp = dp
        self.core_peer = (dp + stride * (1 - 2 * self.core), z)
        self.x_peer = (dp + 2 * stride * (1 - 2 * self.x), z)
        self.y_peer = (dp + 4 * stride * (1 - 2 * self.y), z)

    def z_peer(self, z):
        return (self.dp, z)

    def z_pair(self, bit):
        return (self.dp, self.z + bit * (1 - 2 * ((self.z // bit) % 2)))


def remote(src, dst, send_sem, recv_sem, peer):
    return pltpu.make_async_remote_copy(
        src_ref=src, dst_ref=dst, send_sem=send_sem, recv_sem=recv_sem, device_id=peer, device_id_type=MESH
    )


class Sums:
    def __init__(self, place, own, got0, got1, got2, low_z, high_z, send_sems, recv_sems, z_sems, out_sem):
        self.place, self.own = place, own
        self.got0, self.got1, self.got2, self.low_z, self.high_z = got0, got1, got2, low_z, high_z
        self.send_sems, self.recv_sems, self.z_sems, self.out_sem = send_sems, recv_sems, z_sems, out_sem

    def arrived(self, stage, j):
        got = (self.got0, self.got1, self.got2)[stage].at[pl.ds(2 * j, 2)]
        remote(got, got, self.send_sems.at[stage], self.recv_sems.at[stage, j], self.place.core_peer).wait_recv()

    def send0(self, j, k):
        at, p = self.place, 2 * j + k
        remote(
            self.own.at[p, 1 - at.core], self.got0.at[p], self.send_sems.at[0], self.recv_sems.at[0, j], at.core_peer
        ).start()

    def send1(self, j, k):
        at, p = self.place, 2 * j + k
        mine = self.own.at[p, at.core]
        src = mine.at[1 - at.y] if k else mine.at[:, 1 - at.x]
        remote(
            src, self.got1.at[p], self.send_sems.at[1], self.recv_sems.at[1, j], at.y_peer if k else at.x_peer
        ).start()

    def send2(self, j, k):
        at, p = self.place, 2 * j + k
        mine = self.own.at[p, at.core]
        src = mine.at[at.y, 1 - at.x] if k else mine.at[1 - at.y, at.x]
        remote(
            src, self.got2.at[p], self.send_sems.at[2], self.recv_sems.at[2, j], at.x_peer if k else at.y_peer
        ).start()

    def kept(self, p):
        at = self.place
        return self.own.at[p, at.core, at.y, at.x]

    def up(self, p, first):
        src = self.kept(p) if first else self.got2.at[p]
        return remote(
            src, self.low_z.at[p], self.send_sems.at[3], self.z_sems.at[0, p], self.place.z_peer(self.place.z + 1)
        )

    def down(self, p, first):
        src = self.kept(p) if first else self.got1.at[p, 0]
        return remote(
            src, self.high_z.at[p], self.send_sems.at[4], self.z_sems.at[1, p], self.place.z_peer(self.place.z - 1)
        )

    def stage0(self, j):
        for k in range(2):
            self.send0(j, k)

    def stage1(self, j):
        at = self.place
        self.arrived(0, j)
        for k in range(2):
            p = 2 * j + k
            for a in range(2):
                for b in range(2):
                    self.own[p, at.core, a, b] = self.own[p, at.core, a, b] + self.got0[p, a, b]
            self.send1(j, k)

    def stage2(self, j):
        at = self.place
        self.arrived(1, j)
        for k in range(2):
            p = 2 * j + k
            for a in range(2):
                if k:
                    self.own[p, at.core, at.y, a] = self.own[p, at.core, at.y, a] + self.got1[p, a]
                else:
                    self.own[p, at.core, a, at.x] = self.own[p, at.core, a, at.x] + self.got1[p, a]
            self.send2(j, k)

    def stage3(self, j):
        at = self.place
        self.arrived(2, j)
        for k in range(2):
            p = 2 * j + k
            self.own[p, at.core, at.y, at.x] = self.own[p, at.core, at.y, at.x] + self.got2[p]
        self.hop(j, 0)

    def hop(self, j, step):
        at = self.place
        last = at.n_seq - 1

        @pl.when(at.z == step)
        def _():
            for k in range(2):
                p = 2 * j + k
                if step:
                    self.up(p, False).wait_recv()
                    self.got2[p] = self.low_z[p] + self.own[p, at.core, at.y, at.x]
                self.up(p, step == 0).start()

        @pl.when(at.z == last - step)
        def _():
            for k in range(2):
                p = 2 * j + k
                if step:
                    self.down(p, False).wait_recv()
                    self.got1[p, 0] = self.high_z[p] + self.own[p, at.core, at.y, at.x]
                self.down(p, step == 0).start()

    def finish(self, j, out):
        at = self.place
        last = at.n_seq - 1
        for k in range(2):
            p = 2 * j + k

            @pl.when(at.z == last)
            def _():
                self.up(p, False).wait_recv()
                self.low_z[p] = self.low_z[p] + self.own[p, at.core, at.y, at.x]

            @pl.when(at.z == 0)
            def _():
                self.down(p, False).wait_recv()
                self.low_z[p] = self.high_z[p] + self.own[p, at.core, at.y, at.x]

            @pl.when((at.z > 0) & (at.z < last))
            def _():
                total = self.low_z[p].astype(F32) + self.high_z[p].astype(F32)
                self.low_z[p] = (total + self.own[p, at.core, at.y, at.x].astype(F32)).astype(LOW)

            pltpu.make_async_copy(self.low_z.at[p], out.at[p], self.out_sem.at[0]).start()

    def drain(self, out):
        at = self.place
        last = at.n_seq - 1

        def sent(stage, all_pieces):
            remote(
                all_pieces, all_pieces, self.send_sems.at[stage], self.recv_sems.at[0, 0], at.core_peer
            ).wait_send()

        for stage, got in enumerate((self.got0, self.got1, self.got2)):
            sent(stage, got)

        @pl.when(at.z < last)
        def _():
            sent(3, self.low_z)

        @pl.when(at.z > 0)
        def _():
            sent(4, self.high_z)

        pltpu.make_async_copy(self.low_z, out, self.out_sem.at[0]).wait()


FF_JOBS, ATT_JOBS = 6, 4
FF_ROWS, ATT_ROWS = 384, 288


def layer_kernel(
    n_dp, n_seq,
    tokens_hbm, cot_hbm, seg_ref, bucket_row, gain_one_row, gain_two_row, table_ref,
    wq_hbm, wk_hbm, wv_hbm, wo_hbm, wg_hbm, wu_hbm, wd_hbm,
    mixed_out, tokens_out, ff_out, att_out, small_out, probs_hbm, slope_hbm,
    ff_own, ff_got0, ff_got1, ff_got2, ff_low, ff_high, ff_sends, ff_recvs, ff_z_recvs, ff_out_sem,
    att_own, att_got0, att_got1, att_got2, att_low, att_high, att_sends, att_recvs, att_z_recvs, att_out_sem,
    small_own, small_got, small_rows, small_sems,
    x_ref, cot_ref, seg_send_ref, seg_rows_ref, mixed_ref,
    wo_ref, wgu_ref, wd_ref, probs_ref, inverse_ref,
    activ_t_ref, attended_t_ref, q_ref, k_ref, v_ref, k_t_ref, resid_ref, acc_ref, branch_ref, d_branch_ref,
    d_att_t_ref, d_q_t_ref, offset_ref, diag_ref, bucket_ref, gain_one_ref, gain_two_ref,
    load_sems, ff_load_sems, probs_sems, send_sems, recv_sems, token_sems, own_sems,
):
    span, width = x_ref.shape
    heads, buckets = table_ref.shape
    buckets_wide = bucket_ref.shape[1]
    head_dim = width // heads
    blocks = span // 128
    pairs = heads // 2
    tiles = wg_hbm.shape[1] // 512
    shard = width // GROUP
    at = Place(n_dp, n_seq)
    d_back_ref = cot_ref

    wq_ref, wk_ref, wv_ref = wgu_ref.at[0, :, pl.ds(0, width)], wgu_ref.at[1, :, pl.ds(0, width)], wd_ref.at[pl.ds(0, width)]
    loads = [
        pltpu.make_async_copy(src, dst, load_sems.at[i])
        for i, (src, dst) in enumerate([(wq_hbm, wq_ref), (wk_hbm, wk_ref), (wv_hbm, wv_ref)])
    ]
    output_load = pltpu.make_async_copy(wo_hbm, wo_ref, load_sems.at[3])

    def weight_loads(g, slot):
        cols = pl.ds(pl.multiple_of(g * 512, 512), 512)
        sides = [
            (wd_hbm.at[cols, :], wd_ref.at[pl.ds(pl.multiple_of(slot * 512, 512), 512)]),
            (wg_hbm.at[:, cols], wgu_ref.at[slot, :, pl.ds(0, 512)]),
            (wu_hbm.at[:, cols], wgu_ref.at[slot, :, pl.ds(512, 512)]),
        ]
        return [pltpu.make_async_copy(src, dst, ff_load_sems.at[i, slot]) for i, (src, dst) in enumerate(sides)]

    def slope_copy(g, slot, store):
        sides = (slope_hbm.at[g], probs_ref.at[slot])
        return pltpu.make_async_copy(*(sides[::-1] if store else sides), probs_sems.at[slot])

    def probs_copy(pair, slot, store):
        sides = (probs_hbm.at[pl.ds(2 * pair, 2)], probs_ref.at[slot])
        return pltpu.make_async_copy(*(sides[::-1] if store else sides), probs_sems.at[slot])

    def start(copies):
        for copy in copies:
            copy.start()

    def wait(copies):
        for copy in copies:
            copy.wait()

    start(loads)
    output_load.start()
    for i in range(n_seq):
        seg_send_ref[i] = jnp.broadcast_to(seg_ref[i : i + 1, :], (8, 128))

    barrier = pltpu.get_barrier_semaphore()
    peers = [at.core_peer, at.x_peer, at.y_peer] + [
        at.z_peer(lax.rem(at.z + i, n_seq)) for i in range(1, n_seq)
    ]
    for peer in peers:
        pl.semaphore_signal(barrier, inc=1, device_id=peer, device_id_type=MESH)
    pl.semaphore_wait(barrier, len(peers))

    ff = Sums(
        at, ff_own, ff_got0, ff_got1, ff_got2, ff_low, ff_high, ff_sends, ff_recvs, ff_z_recvs, ff_out_sem
    )
    att = Sums(
        at, att_own, att_got0, att_got1, att_got2, att_low, att_high, att_sends, att_recvs, att_z_recvs, att_out_sem
    )

    def block(z):
        return pl.ds(pl.multiple_of(z * 128, 128), 128)

    def pick(values):
        return sum(jnp.where(at.z == z, value, 0) for z, value in enumerate(values))

    nearest = [sorted(range(n_seq), key=lambda other: abs(other - z)) for z in range(n_seq)]

    def exchange(kind, src, dst, recv_of=None):
        sends = []
        for i in range(n_seq - 1):
            to = pick([near[i + 1] for near in nearest])
            recv = recv_sems.at[kind] if recv_of is None else recv_of.at[at.z]
            sends.append(remote(src(to), dst(at.z), send_sems.at[kind], recv, at.z_peer(to)))
        return sends, pltpu.make_async_copy(src(at.z), dst(at.z), own_sems.at[kind])

    def begin(exchanged):
        sends, own = exchanged
        start(sends)
        own.start()

    def arrive(kind, others, one):
        remote(others, others, send_sems.at[kind], recv_sems.at[kind], at.core_peer).wait_recv()
        pltpu.make_async_copy(one, one, own_sems.at[kind]).wait()

    def sent(kind, others):
        remote(others, others, send_sems.at[kind], recv_sems.at[kind], at.core_peer).wait_send()

    SEGS, TOKENS, COT, MIXED, BACK = range(5)
    segs = exchange(SEGS, lambda z: seg_send_ref.at[z], lambda z: seg_rows_ref.at[z])
    tokens_in = exchange(TOKENS, lambda z: tokens_hbm.at[z], lambda z: x_ref.at[block(z), :], token_sems)
    cot_in = exchange(COT, lambda z: cot_hbm.at[z], lambda z: cot_ref.at[block(z), :])
    mixed_back = exchange(MIXED, lambda z: mixed_ref.at[block(z), :], lambda z: mixed_out.at[z])
    tokens_back = [
        exchange(
            BACK,
            lambda z, part=part: d_back_ref.at[pl.ds(pl.multiple_of(z * 128 + 32 * part, 32), 32), :],
            lambda z, part=part: tokens_out.at[z, pl.ds(32 * part, 32), :],
        )
        for part in range(4)
    ]
    three_segs, one_seg = seg_rows_ref.at[pl.ds(0, n_seq - 1)], seg_rows_ref.at[0]
    three_blocks, one_block = x_ref.at[pl.ds(0, 128 * (n_seq - 1)), :], x_ref.at[pl.ds(0, 128), :]
    begin(segs)
    bucket_ref[...] = jnp.zeros_like(bucket_ref)
    bucket_ref[:, : bucket_row.shape[0]] = bucket_row[...].reshape(1, -1)
    gain_one_ref[...] = gain_one_row[...].reshape(1, -1)
    gain_two_ref[...] = gain_two_row[...].reshape(1, -1)
    begin(tokens_in)
    def forward(bias_ref, key_seg_ref, query_seg_ref):
        one_hot = (lax.broadcasted_iota(jnp.int32, (buckets, buckets_wide), 0) == bucket_ref[...]).astype(F32)
        offset_ref[:heads, :] = lax.dot_general(
            table_ref[...], one_hot, (((1,), (0,)), ((), ())),
            precision=lax.Precision.HIGHEST, preferred_element_type=F32,
        )

        @pl.loop(0, heads)
        def _(h):
            row = offset_ref[pl.ds(h, 1), :]
            for d in range(2 * blocks - 1):
                window = jnp.broadcast_to(row[:, 128 * d : 128 * d + 256], (128, 256))
                bias_ref[h, d] = pltpu.roll(window, 129, 1, stride=1, stride_axis=0)[:, :128].T

        arrive(SEGS, three_segs, one_seg)
        seg_rows = [seg_rows_ref[i, 0:1, :].astype(F32) for i in range(blocks)]
        for i in range(blocks):
            column = jnp.broadcast_to(seg_rows[i], (128, 128)).T
            across = lax.broadcasted_iota(jnp.int32, (128, 128), 1).astype(F32)
            along = lax.broadcasted_iota(jnp.int32, (128, 128), 0).astype(F32)
            key_seg_ref[128 * i : 128 * i + 128, :] = jnp.where(column == across, 1.0, 0.0).astype(LOW)
            query_seg_ref[:, 128 * i : 128 * i + 128] = jnp.where(seg_rows[i] == along, 0.0, MASKED).astype(LOW)
        wait(loads)
        q_t_ref, v_t_ref = d_att_t_ref, d_q_t_ref

        @pl.loop(0, n_seq)
        def _(i):
            source = pick([jnp.where(i == 0, z, 0) for z in range(n_seq)])
            for j in range(1, n_seq):
                source = source + jnp.where(i == j, pick([near[j] for near in nearest]), 0)

            @pl.when(i == 0)
            def _():
                tokens_in[1].wait()

            @pl.when(i > 0)
            def _():
                arrived = x_ref.at[block(source), :]
                remote(
                    arrived, arrived, send_sems.at[TOKENS], token_sems.at[source], at.z_peer(source)
                ).wait_recv()

            @pl.when(i == n_seq - 1)
            def _():
                begin(cot_in)

            rows = block(source)
            inputs = x_ref[rows, :].astype(F32)
            hidden = (inputs * inverse_rms(inputs) * gain_one_ref[...]).astype(LOW)
            for tile in range(width // 256):
                cols = slice(256 * tile, 256 * tile + 256)
                q, k, v = [dot(hidden, ref[:, cols]) for ref in (wq_ref, wk_ref, wv_ref)]
                q_t_ref[cols, rows] = q.T.astype(LOW)
                k_t_ref[cols, rows] = k.T.astype(LOW)
                v_t_ref[cols, rows] = v.T.astype(LOW)
                for b in range(2):
                    lanes = slice(128 * b, 128 * b + 128)
                    q_ref[2 * tile + b, rows, :] = q[:, lanes].astype(LOW)
                    k_ref[2 * tile + b, rows, :] = k[:, lanes].astype(LOW)
                    v_ref[2 * tile + b, rows, :] = v[:, lanes].astype(LOW)

        start(weight_loads(0, 0))
        score_refs = (acc_ref, resid_ref)

        def put_scores(pair, b):
            rows = pl.ds(pl.multiple_of((2 * pair + b) * head_dim, head_dim), head_dim)
            keys = jnp.concatenate([k_ref[pair], key_seg_ref[...]], axis=1)
            q_t = jnp.concatenate([zero_padded(q_t_ref[rows, :], b), query_seg_ref[...]], axis=0)

            def half_of(half):
                cols = slice(256 * half, 256 * half + 256)
                score_refs[b][:, cols] = dot(keys, q_t[:, cols])

            return half_of

        def put_attended(pair, b, slot):
            h = 2 * pair + b
            rows = pl.ds(pl.multiple_of(h * head_dim, head_dim), head_dim)
            v_t = v_t_ref[rows, :]

            def half_of(half):
                cols = slice(256 * half, 256 * half + 256)
                bias = jnp.concatenate(
                    [
                        jnp.concatenate(
                            [bias_ref[h, kb - qb + blocks - 1] for qb in (2 * half, 2 * half + 1)], axis=1
                        )
                        for kb in range(blocks)
                    ],
                    axis=0,
                )
                scores = score_refs[b][:, cols] + bias
                powers = jnp.exp(scores - jnp.max(scores, axis=0, keepdims=True))
                inverse = 1.0 / jnp.sum(powers, axis=0, keepdims=True)
                probs = powers.astype(LOW)
                probs_ref[slot, b, :, cols] = probs
                attended_t_ref[rows, cols] = (dot(v_t, probs) * inverse).astype(LOW)
                inverse_ref[pl.ds(h, 1), cols] = inverse

            return half_of

        first = put_scores(0, 0)
        for half in range(2):
            first(half)

        @pl.loop(0, pairs)
        def _(pair):
            slot = lax.rem(pair, 2)

            @pl.when(pair >= 2)
            def _():
                probs_copy(pair - 2, slot, True).wait()

            for b in range(2):
                ahead = put_scores(pair, 1) if b == 0 else put_scores(jnp.minimum(pair + 1, pairs - 1), 0)
                now = put_attended(pair, b, slot)
                for half in range(2):
                    ahead(half)
                    now(half)
            probs_copy(pair, slot, True).start()

        output_load.wait()
        attended = attended_t_ref[...].T
        for tile in range(width // 256):
            cols = slice(256 * tile, 256 * tile + 256)
            resid_ref[:, cols] = x_ref[:, cols].astype(F32) + dot(attended, wo_ref[:, cols])

        @pl.loop(0, blocks)
        def _(i):
            resid = resid_ref[block(i), :]
            branch_ref[block(i), :] = (resid * inverse_rms(resid) * gain_two_ref[...]).astype(LOW)
            acc_ref[block(i), :] = resid

        for pair in (pairs - 2, pairs - 1):
            probs_copy(pair, pair % 2, True).wait()

        @pl.loop(0, tiles)
        def _(g):
            slot = lax.rem(g, 2)

            @pl.when(g >= 2)
            def _():
                slope_copy(g - 2, slot, True).wait()

            wait(weight_loads(g, slot))

            @pl.when(g < tiles - 1)
            def _():
                start(weight_loads(g + 1, 1 - slot))

            gates = [dot(branch_ref[...], wgu_ref[slot, :, 256 * i : 256 * i + 256]) for i in range(4)]
            activs = []
            for sub in range(2):
                gate, upper = gates[sub], gates[2 + sub]
                lanes = slice(256 * sub, 256 * sub + 256)
                square = gate * gate
                curve = jnp.tanh(0.7978845608028654 * gate * (1.0 + 0.044715 * square))
                gelu = 0.5 * gate * (1.0 + curve)
                slope = 0.5 * (1.0 + curve) + 0.5 * gate * (1.0 - curve * curve) * (
                    0.7978845608028654 * (1.0 + 3 * 0.044715 * square)
                )
                activ = gelu * upper
                probs_ref[slot, 0, :, lanes] = gelu.astype(LOW)
                probs_ref[slot, 1, :, lanes] = (upper * slope).astype(LOW)
                activ_t_ref[2 * g + sub] = activ.T.astype(LOW)
                activs.append(activ.astype(LOW))
            down = wd_ref[pl.ds(pl.multiple_of(slot * 512, 512), 512)]
            acc_ref[...] += dot(jnp.concatenate(activs, axis=1), down)

            @pl.when(g < tiles - 2)
            def _():
                slope_copy(g, slot, True).start()


        mixed_ref[...] = acc_ref[...].astype(LOW)

    pl.run_scoped(
        forward,
        bias_ref=VMEM((heads, 2 * blocks - 1, 128, 128), F32),
        key_seg_ref=VMEM((span, 128), LOW),
        query_seg_ref=VMEM((128, span), LOW),
    )
    arrive(COT, three_blocks, one_block)

    def backward(hidden_t_ref, d_att_ref, d_k_ref, d_v_ref, d_probs_ref):
        for s in range(GROUP):
            product = dot(activ_t_ref[s], cot_ref[...]).astype(LOW)
            for p in range(4):
                for i in range(width // 128):
                    ff_own[p, s % 2, s // 4, (s // 2) % 2, 64 * i : 64 * i + 64, :] = product[
                        64 * p : 64 * p + 64, 128 * i : 128 * i + 128
                    ]
        ff.stage0(0)
        ff.stage0(1)
        sent(COT, three_blocks)
        begin(mixed_back)

        acc_ref[...] = jnp.zeros_like(acc_ref)

        def d_slot(g, k, lanes, half):
            n = 2 * lanes + half
            return att_own.at[2 * g + k, n // 4, (n // 2) % 2, n % 2, pl.ds(0, 256), :]

        @pl.loop(0, tiles)
        def _(step):
            g = tiles - 1 - step
            slot = lax.rem(g, 2)

            @pl.when(step >= 2)
            def _():
                wait(weight_loads(g, slot))
                slope_copy(g, slot, False).wait()

            d_sides = [[], []]
            for sub in range(2):
                lanes = slice(256 * sub, 256 * sub + 256)
                down = wd_ref[pl.ds(pl.multiple_of(slot * 512 + 256 * sub, 256), 256)]
                d_act = dot_back(cot_ref[...], down)
                for k in range(2):
                    d_side = (d_act * probs_ref[slot, 1 - k, :, lanes].astype(F32)).astype(LOW)
                    d_sides[k].append(d_side)
                    for i in range(2):
                        for half in range(2):
                            d_slot(g, k, 2 * sub + i, half)[...] = d_side[
                                256 * half : 256 * half + 256, 128 * i : 128 * i + 128
                            ]
            resid = resid_ref[block(step), :]
            hidden_t_ref[:, block(step)] = (resid * inverse_rms(resid) * gain_two_ref[...]).T.astype(LOW)
            d_both = jnp.concatenate(d_sides[0] + d_sides[1], axis=1)
            for tile in range(width // 256):
                cols = slice(256 * tile, 256 * tile + 256)
                acc_ref[:, cols] += dot_back(d_both, wgu_ref[slot, cols, :])

            @pl.when(step <= 1)
            def _():
                start(weight_loads(g - 2, slot))
                slope_copy(g - 2, slot, False).start()


            @pl.when(step == 0)
            def _():
                ff.stage1(0)

        start(loads)
        probs_copy(0, 0, False).start()


        def product(g, k, sub):
            right = jnp.concatenate(
                [
                    jnp.concatenate([d_slot(g, k, 2 * sub + i, half)[...] for half in range(2)], axis=0)
                    for i in range(2)
                ],
                axis=1,
            )
            result = dot(hidden_t_ref[...], right).astype(LOW)
            for s in range(GROUP):
                for i in range(2):
                    place = shard * (2 * sub + i)
                    ff_own[4 + 2 * g + k, s % 2, s // 4, (s // 2) % 2, place : place + shard, :] = result[
                        shard * s : shard * s + shard, 128 * i : 128 * i + 128
                    ]

        def norm_back(grad_ref, vector_ref, gain_ref, extra_ref, out_ref, low_ref, row):
            total = jnp.zeros((1, width), F32)
            for i in range(blocks):
                rows = slice(128 * i, 128 * i + 128)
                vector = vector_ref[rows, :].astype(F32)
                scale = inverse_rms(vector)
                normed = vector * scale
                grad = grad_ref[rows, :]
                total = total + jnp.sum(grad * normed, axis=0, keepdims=True)
                inner = grad * gain_ref[...]
                result = extra_ref[rows, :].astype(F32) + scale * (
                    inner - normed * jnp.mean(inner * normed, -1, keepdims=True)
                )
                if out_ref is not None:
                    out_ref[rows, :] = result
                low_ref[rows, :] = result.astype(LOW)
            for i in range(width // 128):
                small_own[0, row + i : row + i + 1, :] = total[:, 128 * i : 128 * i + 128]

        norm_back(acc_ref, resid_ref, gain_two_ref, cot_ref, acc_ref, d_branch_ref, 12)

        def share(sums, j, left_t, right):
            for k in range(2):
                half = slice(width // 2 * k, width // 2 * k + width // 2)
                product = dot(left_t, right[:, half]).astype(LOW)
                for s in range(GROUP):
                    for i in range(width // 256):
                        sums.own[2 * j + k, s % 2, s // 4, (s // 2) % 2, shard * i : shard * i + shard, :] = product[
                            shard * s : shard * s + shard, 128 * i : 128 * i + 128
                        ]
            sums.stage0(j)

        for tile in range(width // 256):
            rows = slice(256 * tile, 256 * tile + 256)
            d_att_t = dot_back(d_branch_ref[...], wo_ref[rows, :]).T
            for i in range(256 // head_dim):
                h = 256 // head_dim * tile + i
                d_att_t_ref[head_dim * h : head_dim * (h + 1), :] = (
                    d_att_t[head_dim * i : head_dim * (i + 1), :] * inverse_ref[h : h + 1, :]
                ).astype(LOW)
            for i in range(2):
                d_att_ref[2 * tile + i] = d_att_t_ref[256 * tile + 128 * i : 256 * tile + 128 * i + 128, :].T
        left_half = lax.broadcasted_iota(jnp.int32, (span, 128), 1) < head_dim
        d_probs_refs = (resid_ref, d_probs_ref)

        def put_d_probs(pair, b):
            rows = pl.ds(pl.multiple_of((2 * pair + b) * head_dim, head_dim), head_dim)
            values = v_ref[pair]
            d_att_t = zero_padded(d_att_t_ref[rows, :], b)

            def half_of(half):
                cols = slice(256 * half, 256 * half + 256)
                d_probs_refs[b][:, cols] = dot(values, d_att_t[:, cols])

            return half_of

        across = lax.broadcasted_iota(jnp.int32, (8, 128), 1)

        def put_d_scores(pair, b, slot):
            h = 2 * pair + b
            rows = pl.ds(pl.multiple_of(h * head_dim, head_dim), head_dim)
            k_t = k_t_ref[rows, :]
            sums = [None] * (2 * blocks - 1)

            def half_of(half):
                cols = slice(256 * half, 256 * half + 256)
                d_probs = d_probs_refs[b][:, cols]
                probs = probs_ref[slot, b, :, cols].astype(F32)
                inner = jnp.sum(probs * d_probs, axis=0, keepdims=True) * inverse_ref[pl.ds(h, 1), cols]
                d_scores = probs * (d_probs - inner)
                for kb in range(blocks):
                    for i in range(2):
                        d = kb - (2 * half + i) + blocks - 1
                        part = d_scores[128 * kb : 128 * kb + 128, 128 * i : 128 * i + 128]
                        sums[d] = part if sums[d] is None else sums[d] + part
                d_scores = d_scores.astype(LOW)
                for i in range(2):
                    activ_t_ref[2 * b + i, :, cols] = d_scores[256 * i : 256 * i + 256, :]
                d_q_t_ref[rows, cols] = dot(k_t, d_scores).astype(LOW)
                if half == 1:
                    for d in range(2 * blocks - 1):
                        every, low_lanes = sums[d][:8, :], sums[d][:8, :]
                        for a in range(1, 16):
                            rolled = pltpu.roll(sums[d][8 * a : 8 * a + 8, :], 128 - 8 * a, 1)
                            every = every + rolled
                            low_lanes = low_lanes + jnp.where(across < 128 - 8 * a, rolled, 0.0)
                        diag_ref[h, d] = jnp.concatenate([low_lanes, every - low_lanes], axis=1)

            return half_of

        ff.stage2(0)
        ff.stage1(1)
        first = put_d_probs(0, 0)
        for half in range(2):
            first(half)

        def attention_back(pair, with_products):
            slot = lax.rem(pair, 2)
            probs_copy(pair, slot, False).wait()

            @pl.when(pair < pairs - 1)
            def _():
                probs_copy(pair + 1, 1 - slot, False).start()

            for b in range(2):
                ahead = put_d_probs(pair, 1) if b == 0 else put_d_probs(jnp.minimum(pair + 1, pairs - 1), 0)
                now = put_d_scores(pair, b, slot)
                for half in range(2):
                    ahead(half)
                    if with_products:
                        product(pair, b, half)
                    now(half)
            lanes = pl.ds(pl.multiple_of(pair * 128, 128), 128)
            d_att, queries = d_att_ref[pair], q_ref[pair]
            blank = jnp.zeros_like(d_att)
            d_scores = [activ_t_ref[2 * b : 2 * b + 2].reshape(span, span) for b in range(2)]
            d_v_ref[:, lanes] = (
                dot(probs_ref[slot, 0], jnp.where(left_half, d_att, blank))
                + dot(probs_ref[slot, 1], jnp.where(left_half, blank, d_att))
            ).astype(LOW)
            d_k_ref[:, lanes] = (
                dot(d_scores[0], jnp.where(left_half, queries, blank))
                + dot(d_scores[1], jnp.where(left_half, blank, queries))
            ).astype(LOW)

        @pl.loop(0, tiles)
        def _(pair):
            attention_back(pair, True)
            ff.stage0(2 + pair)

            @pl.when(pair == 0)
            def _():
                ff.stage3(0)

            @pl.when(pair == 1)
            def _():
                ff.stage1(2)

            @pl.when(pair == 2)
            def _():
                ff.stage2(1)
                ff.stage1(3)
                ff.hop(0, 1)

        @pl.loop(tiles, pairs)
        def _(pair):
            attention_back(pair, False)

            @pl.when(pair == tiles)
            def _():
                ff.stage2(2)
                ff.stage1(4)
                ff.stage3(1)

        branch_ref[...] = d_q_t_ref[...].T
        wait(loads)
        for tile in range(width // 256):
            rows = slice(256 * tile, 256 * tile + 256)
            resid_ref[:, rows] = (
                dot_back(branch_ref[...], wgu_ref[0, rows, :width])
                + dot_back(d_k_ref[...], wgu_ref[1, rows, :width])
                + dot_back(d_v_ref[...], wd_ref[rows, :])
            )
        ff.stage2(3)
        ff.stage1(5)
        norm_back(resid_ref, x_ref, gain_one_ref, acc_ref, None, d_back_ref, 18)
        ff.hop(1, 1)
        ff.stage3(2)
        begin(tokens_back[0])
        share(att, 0, attended_t_ref[...], d_branch_ref[...])
        ff.hop(0, 2)

        @pl.loop(0, blocks)
        def _(i):
            inputs = x_ref[block(i), :].astype(F32)
            hidden_t_ref[:, block(i)] = (inputs * inverse_rms(inputs) * gain_one_ref[...]).T.astype(LOW)

        share(att, 1, hidden_t_ref[...], d_v_ref[...])
        share(att, 2, hidden_t_ref[...], d_k_ref[...])
        ff.stage2(4)
        att.stage1(0)
        share(att, 3, hidden_t_ref[...], branch_ref[...])
        ff.hop(2, 1)
        begin(tokens_back[1])
        ff.stage3(3)

    pl.run_scoped(
        backward,
        hidden_t_ref=VMEM((width, span), LOW),
        d_att_ref=VMEM((pairs, span, 128), LOW),
        d_k_ref=VMEM((span, width), LOW),
        d_v_ref=VMEM((span, width), LOW),
        d_probs_ref=VMEM((span, span), F32),
    )

    flip = (
        lax.broadcasted_iota(jnp.int32, (256, 256), 0) + lax.broadcasted_iota(jnp.int32, (256, 256), 1) == 255
    ).astype(F32)

    @pl.loop(0, heads)
    def _(h):
        tiles_ = diag_ref[h].reshape(8 * (2 * blocks - 1), 256)
        flipped = jnp.dot(tiles_, flip, precision=lax.Precision.HIGHEST, preferred_element_type=F32)
        totals = [
            jnp.sum(pltpu.roll(flipped[8 * d : 8 * d + 8, :], 0, 1, stride=1, stride_axis=0), axis=0, keepdims=True)
            for d in range(2 * blocks - 1)
        ]
        pieces = [totals[0][:, 128:]]
        for d in range(1, 2 * blocks - 1):
            pieces.append(totals[d - 1][:, :128] + totals[d][:, 128:])
        pieces.append(totals[-1][:, :128])
        offset_ref[pl.ds(h, 1), :] = jnp.concatenate(pieces, axis=1)

    one_hot = (lax.broadcasted_iota(jnp.int32, (128, buckets_wide), 0) == bucket_ref[...]).astype(F32)
    small_own[0, :12, :] = lax.dot_general(
        offset_ref[:12, :], one_hot, (((1,), (1,)), ((), ())),
        precision=lax.Precision.HIGHEST, preferred_element_type=F32,
    )
    small_peers = [at.core_peer, at.x_peer, at.y_peer]
    steps = len(small_peers)

    def small_copy(i):
        return remote(small_own.at[i], small_got.at[i], small_sems.at[3], small_sems.at[i], small_peers[i])

    def small_row(i):
        return remote(
            small_own.at[steps], small_rows.at[at.z], small_sems.at[4], small_sems.at[5],
            at.z_peer(lax.rem(at.z + i, n_seq)),
        )

    def small_step(i):
        small_copy(i).wait_recv()
        small_own[i + 1] = small_own[i] + small_got[i]
        if i + 1 < steps:
            small_copy(i + 1).start()

    inner = (at.z > 0) & (at.z < n_seq - 1)
    small_copy(0).start()
    ff.stage2(5)
    att.stage1(1)
    ff.stage3(4)
    small_step(0)
    ff.hop(1, 2)
    att.stage2(0)
    att.stage1(2)
    ff.hop(3, 1)
    begin(tokens_back[2])
    ff.stage3(5)
    att.stage2(1)
    att.stage1(3)
    ff.hop(4, 1)
    ff.hop(2, 2)
    att.stage3(0)
    small_step(1)
    att.stage2(2)
    ff.hop(5, 1)
    ff.hop(3, 2)
    att.stage3(1)
    att.hop(0, 1)
    att.stage2(3)
    ff.hop(4, 2)
    small_step(2)
    small_rows[at.z] = small_own[steps]
    att.stage3(2)
    att.hop(1, 1)
    att.stage3(3)
    for i in range(1, n_seq):
        small_row(i).start()
    ff.hop(5, 2)
    att.hop(0, 2)
    att.hop(2, 1)
    att.hop(3, 1)

    @pl.when(inner)
    def _():
        begin(tokens_back[3])

    att.hop(1, 2)
    att.hop(2, 2)
    att.hop(3, 2)

    @pl.loop(0, FF_JOBS)
    def _(j):
        ff.finish(j, ff_out)

    @pl.when(jnp.logical_not(inner))
    def _():
        begin(tokens_back[3])

    @pl.loop(0, ATT_JOBS)
    def _(j):
        att.finish(j, att_out)

    three_rows = small_rows.at[pl.ds(0, n_seq - 1)]
    remote(three_rows, three_rows, small_sems.at[4], small_sems.at[5], at.core_peer).wait_recv()
    total = small_rows[0]
    for i in range(1, n_seq):
        total = total + small_rows[i]
    small_rows[0] = total
    small_store = pltpu.make_async_copy(small_rows.at[0], small_out, own_sems.at[5])
    small_store.start()
    ff.drain(ff_out)
    att.drain(att_out)
    three_steps = small_own.at[pl.ds(0, steps)]
    remote(three_steps, three_steps, small_sems.at[3], small_sems.at[0], at.core_peer).wait_send()
    remote(three_rows, three_rows, small_sems.at[4], small_sems.at[5], at.core_peer).wait_send()
    sent(SEGS, three_segs)
    for kind in (TOKENS, MIXED, BACK):
        sent(kind, three_blocks)
    for kind in (MIXED, BACK):
        arrive(kind, three_blocks, one_block)
    small_store.wait()


def layer(n_dp, n_seq, tokens, cot, seg, buckets, gain_one, gain_two, table, weights):
    width = tokens.shape[-1]
    span = tokens.shape[0] * tokens.shape[1]
    heads = table.shape[0]
    ff_width = weights[4].shape[1]
    ff_pieces, att_pieces = 2 * FF_JOBS, 2 * ATT_JOBS
    low = lambda *shape: VMEM(shape, LOW)
    dma = pltpu.SemaphoreType.DMA
    steps = 3

    def sums(pieces, rows):
        return [
            low(pieces, 2, 2, 2, rows, 128), low(pieces, 2, 2, rows, 128), low(pieces, 2, rows, 128),
            low(pieces, rows, 128), low(pieces, rows, 128), low(pieces, rows, 128),
            dma((5,)), dma((3, pieces // 2)), dma((2, pieces)), dma((1,)),
        ]

    pairs = low(heads // 2, span, 128)
    rows, turned = low(span, width), low(width, span)
    any_, vmem = pl.BlockSpec(memory_space=pl.ANY), pl.BlockSpec(memory_space=VMEM)
    result = lambda *shape: jax.ShapeDtypeStruct(shape, LOW)
    return pl.pallas_call(
        functools.partial(layer_kernel, n_dp, n_seq),
        out_shape=[
            result(n_seq, span // n_seq, width), result(n_seq, span // n_seq, width),
            result(ff_pieces, FF_ROWS, 128), result(att_pieces, ATT_ROWS, 128),
            jax.ShapeDtypeStruct((24, 128), F32),
            result(heads, span, span), result(ff_width // 512, 2, span, 512),
        ],
        in_specs=[any_] * 2 + [vmem] * 5 + [any_] * 7,
        out_specs=[any_] * 7,
        scratch_shapes=sums(ff_pieces, FF_ROWS)
        + sums(att_pieces, ATT_ROWS)
        + [
            VMEM((steps + 1, 24, 128), F32), VMEM((steps, 24, 128), F32), VMEM((n_seq, 24, 128), F32),
            dma((6,)),
        ]
        + [
            rows, rows, VMEM((n_seq, 8, 128), jnp.int32), VMEM((n_seq, 8, 128), jnp.int32), rows,
            low(width, width), low(2, width, 1024), low(1024, width), low(2, 2, span, span), VMEM((16, span), F32),
            low(ff_width // 256, 256, span), turned, pairs, pairs, pairs, turned, VMEM((span, width), F32),
            VMEM((span, width), F32), rows, rows, turned, turned, VMEM((16, 1024), F32),
            VMEM((heads, 2 * (span // 128) - 1, 8, 256), F32),
            VMEM((1, 1024), jnp.int32), VMEM((1, width), F32), VMEM((1, width), F32),
            dma((4,)), dma((3, 2)), dma((2,)), dma((5,)), dma((5,)), dma((n_seq,)), dma((6,)),
        ],
        compiler_params=pltpu.CompilerParams(
            collective_id=0, has_side_effects=True, vmem_limit_bytes=VMEM_BYTES
        ),
        name="layer",
    )(tokens, cot, seg, buckets, gain_one, gain_two, table, *weights)


def outputs_kernel(
    n_dp, mixed_ref, tokens_ref, ff_ref, att_ref, small_ref,
    mixed_out, tokens_out, gn_one_out, gq_out, gk_out, gv_out, go_out, table_out, gn_two_out, gg_out, gu_out, gd_out,
    mixed_in, tokens_in, ff_in, att_in, small_in, gn_one, gq, gk, gv, go, table, gn_two, gg, gu, gd, tokens, sems,
):
    copies = [
        pltpu.make_async_copy(src, dst, sems.at[i])
        for i, (src, dst) in enumerate(
            [(small_ref, small_in), (tokens_ref, tokens_in), (ff_ref, ff_in), (att_ref, att_in), (mixed_ref, mixed_in)]
        )
    ]
    for copy in copies:
        copy.start()
    stores = []

    def store(src, dst):
        stores.append(pltpu.make_async_copy(src, dst, sems.at[len(copies) + len(stores)]))
        stores[-1].start()

    width = mixed_ref.shape[-1]
    shard = width // GROUP
    copies[0].wait()
    table[...] = small_in[: table.shape[0], : table.shape[1]]
    store(table, table_out)
    mine = lax.axis_index("dp") // (n_dp // GROUP)
    for row, part, out in ((12, gn_two, gn_two_out), (18, gn_one, gn_one_out)):
        gains = jnp.concatenate([small_in[row + i : row + i + 1, :] for i in range(width // 128)], axis=1)
        total = jnp.zeros((1, shard), F32)
        for s in range(GROUP):
            total = total + jnp.where(mine == s, gains[:, shard * s : shard * s + shard], 0.0)
        part[...] = total
        store(part, out)
    copies[1].wait()
    tokens[...] = tokens_in[...].astype(F32)
    store(tokens, tokens_out)
    copies[2].wait()
    for k, (part, out) in enumerate(((gg, gg_out), (gu, gu_out))):
        for g in range(4):
            for i in range(4):
                col = 512 * g + 128 * i
                part[:, col : col + 128] = ff_in[4 + 2 * g + k, shard * i : shard * i + shard, :].astype(F32)
        store(part, out)
    for p in range(4):
        for i in range(width // 128):
            gd[64 * p : 64 * p + 64, 128 * i : 128 * i + 128] = ff_in[p, 64 * i : 64 * i + 64, :].astype(F32)
    store(gd, gd_out)
    copies[3].wait()
    for j, (part, out) in enumerate(((go, go_out), (gv, gv_out), (gk, gk_out), (gq, gq_out))):
        for k in range(2):
            for i in range(width // 256):
                col = width // 2 * k + 128 * i
                part[:, col : col + 128] = att_in[2 * j + k, shard * i : shard * i + shard, :].astype(F32)
        store(part, out)
    copies[4].wait()
    store(mixed_in, mixed_out)
    for copy in stores:
        copy.wait()


def outputs(n_dp, buckets, heads, mixed, tokens, ff, att, small):
    width = mixed.shape[-1]
    shard = width // GROUP
    full = lambda *shape: jax.ShapeDtypeStruct(shape, F32)
    square, wide = full(shard, width), full(shard, 2048)
    results = [
        jax.ShapeDtypeStruct(mixed.shape, LOW), full(*tokens.shape), full(1, shard), square, square, square, square,
        full(heads, buckets), full(1, shard), wide, wide, full(256, width),
    ]
    any_ = pl.BlockSpec(memory_space=pl.ANY)
    return pl.pallas_call(
        functools.partial(outputs_kernel, n_dp),
        out_shape=results,
        in_specs=[any_] * 5,
        out_specs=[any_] * len(results),
        scratch_shapes=[VMEM(a.shape, a.dtype) for a in [mixed, tokens, ff, att, small] + results[2:] + results[1:2]]
        + [pltpu.SemaphoreType.DMA((5 + len(results),))],
        compiler_params=pltpu.CompilerParams(vmem_limit_bytes=VMEM_BYTES),
        name="outputs",
    )(mixed, tokens, ff, att, small)


def solution(mesh):
    n_dp, n_seq = mesh.shape["dp"], mesh.shape["seq"]

    def on_device(
        tokens, segments, offset_buckets, norm_attn, w_query, w_key, w_value, w_output, bias_table,
        norm_ff, w_gate, w_up, w_down, cotangent,
    ):
        weights = (w_query, w_key, w_value, w_output, w_gate, w_up, w_down)
        sums = layer(
            n_dp, n_seq, tokens, cotangent, segments, offset_buckets, norm_attn, norm_ff, bias_table.T, weights
        )[:5]
        results = list(outputs(n_dp, bias_table.shape[0], bias_table.shape[1], *sums))
        results[2], results[7], results[8] = results[2].reshape(-1), results[7].T, results[8].reshape(-1)
        rest = n_dp // GROUP
        if rest > 1:
            groups = [[i * rest + j for j in range(rest)] for i in range(GROUP)]
            for i in (2, 3, 4, 5, 6, 8, 9, 10, 11):
                results[i] = lax.psum_scatter(
                    results[i], "dp", scatter_dimension=0, axis_index_groups=groups, tiled=True
                )
            results[7] = lax.psum(results[7], "dp", axis_index_groups=groups)
        return tuple(results)

    rows, shares = P("dp", "seq", None), P("dp", None)
    return jax.shard_map(
        on_device,
        mesh=mesh,
        in_specs=(rows, P("dp", "seq")) + (P(),) * 11 + (rows,),
        out_specs=(rows, rows, P("dp"), shares, shares, shares, shares, P(), P("dp"), shares, shares, shares),
        check_vma=False,
    )
```

```python
import functools

import jax
import jax.numpy as jnp
from jax import lax
from jax.experimental import pallas as pl
from jax.experimental.pallas import tpu as pltpu
from jax.sharding import PartitionSpec as P

MESH = pl.DeviceIdType.MESH
VMEM = pltpu.VMEM
LOW = jnp.bfloat16
F32 = jnp.float32
EPSILON = 1e-06
MASKED = -1e30
GROUP = 8
VMEM_BYTES = 63 * 2**20


def dot(left, right):
    return jnp.dot(left, right, preferred_element_type=F32)


def dot_back(left, right):
    return lax.dot_general(left, right, (((1,), (1,)), ((), ())), preferred_element_type=F32)


def inverse_rms(values):
    return lax.rsqrt(jnp.mean(values * values, -1, keepdims=True) + EPSILON)


def zero_padded(block, half):
    blank = jnp.zeros_like(block)
    return jnp.concatenate([blank, block] if half else [block, blank], axis=0)


class Place:
    def __init__(self, n_dp, n_seq):
        stride = n_dp // GROUP
        dp = lax.axis_index("dp")
        z = lax.axis_index("seq")
        index = dp // stride
        self.n_seq = n_seq
        self.core, self.x, self.y, self.z = index % 2, (index // 2) % 2, index // 4, z
        self.dp = dp
        self.core_peer = (dp + stride * (1 - 2 * self.core), z)
        self.x_peer = (dp + 2 * stride * (1 - 2 * self.x), z)
        self.y_peer = (dp + 4 * stride * (1 - 2 * self.y), z)

    def z_peer(self, z):
        return (self.dp, z)

    def z_pair(self, bit):
        return (self.dp, self.z + bit * (1 - 2 * ((self.z // bit) % 2)))


def remote(src, dst, send_sem, recv_sem, peer):
    return pltpu.make_async_remote_copy(
        src_ref=src, dst_ref=dst, send_sem=send_sem, recv_sem=recv_sem, device_id=peer, device_id_type=MESH
    )


class Sums:
    def __init__(self, place, own, got0, got1, got2, low_z, high_z, send_sems, recv_sems, z_sems, out_sem):
        self.place, self.own = place, own
        self.got0, self.got1, self.got2, self.low_z, self.high_z = got0, got1, got2, low_z, high_z
        self.send_sems, self.recv_sems, self.z_sems, self.out_sem = send_sems, recv_sems, z_sems, out_sem

    def arrived(self, stage, j):
        got = (self.got0, self.got1, self.got2)[stage].at[pl.ds(2 * j, 2)]
        remote(got, got, self.send_sems.at[stage], self.recv_sems.at[stage, j], self.place.core_peer).wait_recv()

    def send0(self, j, k):
        at, p = self.place, 2 * j + k
        remote(
            self.own.at[p, 1 - at.core], self.got0.at[p], self.send_sems.at[0], self.recv_sems.at[0, j], at.core_peer
        ).start()

    def send1(self, j, k):
        at, p = self.place, 2 * j + k
        mine = self.own.at[p, at.core]
        src = mine.at[1 - at.y] if k else mine.at[:, 1 - at.x]
        remote(
            src, self.got1.at[p], self.send_sems.at[1], self.recv_sems.at[1, j], at.y_peer if k else at.x_peer
        ).start()

    def send2(self, j, k):
        at, p = self.place, 2 * j + k
        mine = self.own.at[p, at.core]
        src = mine.at[at.y, 1 - at.x] if k else mine.at[1 - at.y, at.x]
        remote(
            src, self.got2.at[p], self.send_sems.at[2], self.recv_sems.at[2, j], at.x_peer if k else at.y_peer
        ).start()

    def kept(self, p):
        at = self.place
        return self.own.at[p, at.core, at.y, at.x]

    def up(self, p, first):
        src = self.kept(p) if first else self.got2.at[p]
        return remote(
            src, self.low_z.at[p], self.send_sems.at[3], self.z_sems.at[0, p], self.place.z_peer(self.place.z + 1)
        )

    def down(self, p, first):
        src = self.kept(p) if first else self.got1.at[p, 0]
        return remote(
            src, self.high_z.at[p], self.send_sems.at[4], self.z_sems.at[1, p], self.place.z_peer(self.place.z - 1)
        )

    def stage0(self, j):
        for k in range(2):
            self.send0(j, k)

    def stage1(self, j):
        at = self.place
        self.arrived(0, j)
        for k in range(2):
            p = 2 * j + k
            for a in range(2):
                for b in range(2):
                    self.own[p, at.core, a, b] = self.own[p, at.core, a, b] + self.got0[p, a, b]
            self.send1(j, k)

    def stage2(self, j):
        at = self.place
        self.arrived(1, j)
        for k in range(2):
            p = 2 * j + k
            for a in range(2):
                if k:
                    self.own[p, at.core, at.y, a] = self.own[p, at.core, at.y, a] + self.got1[p, a]
                else:
                    self.own[p, at.core, a, at.x] = self.own[p, at.core, a, at.x] + self.got1[p, a]
            self.send2(j, k)

    def stage3(self, j):
        at = self.place
        self.arrived(2, j)
        for k in range(2):
            p = 2 * j + k
            self.own[p, at.core, at.y, at.x] = self.own[p, at.core, at.y, at.x] + self.got2[p]
        self.hop(j, 0)

    def hop(self, j, step):
        at = self.place
        last = at.n_seq - 1

        @pl.when(at.z == step)
        def _():
            for k in range(2):
                p = 2 * j + k
                if step:
                    self.up(p, False).wait_recv()
                    self.got2[p] = self.low_z[p] + self.own[p, at.core, at.y, at.x]
                self.up(p, step == 0).start()

        @pl.when(at.z == last - step)
        def _():
            for k in range(2):
                p = 2 * j + k
                if step:
                    self.down(p, False).wait_recv()
                    self.got1[p, 0] = self.high_z[p] + self.own[p, at.core, at.y, at.x]
                self.down(p, step == 0).start()

    def finish(self, j, out):
        at = self.place
        last = at.n_seq - 1
        for k in range(2):
            p = 2 * j + k

            @pl.when(at.z == last)
            def _():
                self.up(p, False).wait_recv()
                self.low_z[p] = self.low_z[p] + self.own[p, at.core, at.y, at.x]

            @pl.when(at.z == 0)
            def _():
                self.down(p, False).wait_recv()
                self.low_z[p] = self.high_z[p] + self.own[p, at.core, at.y, at.x]

            @pl.when((at.z > 0) & (at.z < last))
            def _():
                total = self.low_z[p].astype(F32) + self.high_z[p].astype(F32)
                self.low_z[p] = (total + self.own[p, at.core, at.y, at.x].astype(F32)).astype(LOW)

            pltpu.make_async_copy(self.low_z.at[p], out.at[p], self.out_sem.at[0]).start()

    def drain(self, out):
        at = self.place
        last = at.n_seq - 1

        def sent(stage, all_pieces):
            remote(
                all_pieces, all_pieces, self.send_sems.at[stage], self.recv_sems.at[0, 0], at.core_peer
            ).wait_send()

        for stage, got in enumerate((self.got0, self.got1, self.got2)):
            sent(stage, got)

        @pl.when(at.z < last)
        def _():
            sent(3, self.low_z)

        @pl.when(at.z > 0)
        def _():
            sent(4, self.high_z)

        pltpu.make_async_copy(self.low_z, out, self.out_sem.at[0]).wait()


FF_JOBS, ATT_JOBS = 6, 4
FF_ROWS, ATT_ROWS = 384, 288


def layer_kernel(
    n_dp, n_seq,
    tokens_hbm, cot_hbm, seg_ref, bucket_row, gain_one_row, gain_two_row, table_ref,
    wq_hbm, wk_hbm, wv_hbm, wo_hbm, wg_hbm, wu_hbm, wd_hbm,
    mixed_out, tokens_out, ff_out, att_out, small_out, probs_hbm, slope_hbm,
    ff_own, ff_got0, ff_got1, ff_got2, ff_low, ff_high, ff_sends, ff_recvs, ff_z_recvs, ff_out_sem,
    att_own, att_got0, att_got1, att_got2, att_low, att_high, att_sends, att_recvs, att_z_recvs, att_out_sem,
    small_own, small_got, small_rows, small_sems,
    x_ref, cot_ref, seg_send_ref, seg_rows_ref, mixed_ref,
    wo_ref, wgu_ref, wd_ref, probs_ref, inverse_ref,
    activ_t_ref, attended_t_ref, q_ref, k_ref, v_ref, k_t_ref, resid_ref, acc_ref, branch_ref, d_branch_ref,
    d_att_t_ref, d_q_t_ref, offset_ref, diag_ref, bucket_ref, gain_one_ref, gain_two_ref,
    load_sems, ff_load_sems, probs_sems, send_sems, recv_sems, token_sems, own_sems,
):
    span, width = x_ref.shape
    heads, buckets = table_ref.shape
    buckets_wide = bucket_ref.shape[1]
    head_dim = width // heads
    blocks = span // 128
    pairs = heads // 2
    tiles = wg_hbm.shape[1] // 512
    shard = width // GROUP
    at = Place(n_dp, n_seq)
    d_back_ref = cot_ref

    wq_ref, wk_ref, wv_ref = wgu_ref.at[0, :, pl.ds(0, width)], wgu_ref.at[1, :, pl.ds(0, width)], wd_ref.at[pl.ds(0, width)]
    loads = [
        pltpu.make_async_copy(src, dst, load_sems.at[i])
        for i, (src, dst) in enumerate([(wq_hbm, wq_ref), (wk_hbm, wk_ref), (wv_hbm, wv_ref)])
    ]
    output_load = pltpu.make_async_copy(wo_hbm, wo_ref, load_sems.at[3])

    def weight_loads(g, slot):
        cols = pl.ds(pl.multiple_of(g * 512, 512), 512)
        sides = [
            (wd_hbm.at[cols, :], wd_ref.at[pl.ds(pl.multiple_of(slot * 512, 512), 512)]),
            (wg_hbm.at[:, cols], wgu_ref.at[slot, :, pl.ds(0, 512)]),
            (wu_hbm.at[:, cols], wgu_ref.at[slot, :, pl.ds(512, 512)]),
        ]
        return [pltpu.make_async_copy(src, dst, ff_load_sems.at[i, slot]) for i, (src, dst) in enumerate(sides)]

    def slope_copy(g, slot, store):
        sides = (slope_hbm.at[g], probs_ref.at[slot])
        return pltpu.make_async_copy(*(sides[::-1] if store else sides), probs_sems.at[slot])

    def probs_copy(pair, slot, store):
        sides = (probs_hbm.at[pl.ds(2 * pair, 2)], probs_ref.at[slot])
        return pltpu.make_async_copy(*(sides[::-1] if store else sides), probs_sems.at[slot])

    def start(copies):
        for copy in copies:
            copy.start()

    def wait(copies):
        for copy in copies:
            copy.wait()

    barrier = pltpu.get_barrier_semaphore()
    peers = [at.core_peer, at.x_peer, at.y_peer] + [
        at.z_peer(lax.rem(at.z + i, n_seq)) for i in range(1, n_seq)
    ]
    for peer in peers:
        pl.semaphore_signal(barrier, inc=1, device_id=peer, device_id_type=MESH)
    start(loads)
    output_load.start()
    for i in range(n_seq):
        seg_send_ref[i] = jnp.broadcast_to(seg_ref[i : i + 1, :], (8, 128))

    pl.semaphore_wait(barrier, len(peers))

    ff = Sums(
        at, ff_own, ff_got0, ff_got1, ff_got2, ff_low, ff_high, ff_sends, ff_recvs, ff_z_recvs, ff_out_sem
    )
    att = Sums(
        at, att_own, att_got0, att_got1, att_got2, att_low, att_high, att_sends, att_recvs, att_z_recvs, att_out_sem
    )

    def block(z):
        return pl.ds(pl.multiple_of(z * 128, 128), 128)

    def pick(values):
        return sum(jnp.where(at.z == z, value, 0) for z, value in enumerate(values))

    nearest = [sorted(range(n_seq), key=lambda other: abs(other - z)) for z in range(n_seq)]

    def exchange(kind, src, dst, recv_of=None):
        sends = []
        for i in range(n_seq - 1):
            to = pick([near[i + 1] for near in nearest])
            recv = recv_sems.at[kind] if recv_of is None else recv_of.at[at.z]
            sends.append(remote(src(to), dst(at.z), send_sems.at[kind], recv, at.z_peer(to)))
        return sends, pltpu.make_async_copy(src(at.z), dst(at.z), own_sems.at[kind])

    def begin(exchanged):
        sends, own = exchanged
        start(sends)
        own.start()

    def arrive(kind, others, one):
        remote(others, others, send_sems.at[kind], recv_sems.at[kind], at.core_peer).wait_recv()
        pltpu.make_async_copy(one, one, own_sems.at[kind]).wait()

    def sent(kind, others):
        remote(others, others, send_sems.at[kind], recv_sems.at[kind], at.core_peer).wait_send()

    SEGS, TOKENS, COT, MIXED, BACK = range(5)
    segs = exchange(SEGS, lambda z: seg_send_ref.at[z], lambda z: seg_rows_ref.at[z])
    tokens_in = exchange(TOKENS, lambda z: tokens_hbm.at[z], lambda z: x_ref.at[block(z), :], token_sems)
    cot_in = exchange(COT, lambda z: cot_hbm.at[z], lambda z: cot_ref.at[block(z), :])
    mixed_back = exchange(MIXED, lambda z: mixed_ref.at[block(z), :], lambda z: mixed_out.at[z])
    tokens_back = [
        exchange(
            BACK,
            lambda z, part=part: d_back_ref.at[pl.ds(pl.multiple_of(z * 128 + 32 * part, 32), 32), :],
            lambda z, part=part: tokens_out.at[z, pl.ds(32 * part, 32), :],
        )
        for part in range(4)
    ]
    three_segs, one_seg = seg_rows_ref.at[pl.ds(0, n_seq - 1)], seg_rows_ref.at[0]
    three_blocks, one_block = x_ref.at[pl.ds(0, 128 * (n_seq - 1)), :], x_ref.at[pl.ds(0, 128), :]
    begin(segs)
    bucket_ref[...] = jnp.zeros_like(bucket_ref)
    bucket_ref[:, : bucket_row.shape[0]] = bucket_row[...].reshape(1, -1)
    gain_one_ref[...] = gain_one_row[...].reshape(1, -1)
    gain_two_ref[...] = gain_two_row[...].reshape(1, -1)
    begin(tokens_in)
    def forward(bias_ref, key_seg_ref, query_seg_ref):
        one_hot = (lax.broadcasted_iota(jnp.int32, (buckets, buckets_wide), 0) == bucket_ref[...]).astype(F32)
        offset_ref[:heads, :] = lax.dot_general(
            table_ref[...], one_hot, (((1,), (0,)), ((), ())),
            precision=lax.Precision.HIGHEST, preferred_element_type=F32,
        )

        @pl.loop(0, heads)
        def _(h):
            row = offset_ref[pl.ds(h, 1), :]
            for d in range(2 * blocks - 1):
                window = jnp.broadcast_to(row[:, 128 * d : 128 * d + 256], (128, 256))
                bias_ref[h, d] = pltpu.roll(window, 129, 1, stride=1, stride_axis=0)[:, :128].T

        arrive(SEGS, three_segs, one_seg)
        seg_rows = [seg_rows_ref[i, 0:1, :].astype(F32) for i in range(blocks)]
        for i in range(blocks):
            column = jnp.broadcast_to(seg_rows[i], (128, 128)).T
            across = lax.broadcasted_iota(jnp.int32, (128, 128), 1).astype(F32)
            along = lax.broadcasted_iota(jnp.int32, (128, 128), 0).astype(F32)
            key_seg_ref[128 * i : 128 * i + 128, :] = jnp.where(column == across, 1.0, 0.0).astype(LOW)
            query_seg_ref[:, 128 * i : 128 * i + 128] = jnp.where(seg_rows[i] == along, 0.0, MASKED).astype(LOW)
        wait(loads)
        q_t_ref, v_t_ref = d_att_t_ref, d_q_t_ref

        @pl.loop(0, n_seq)
        def _(i):
            source = pick([jnp.where(i == 0, z, 0) for z in range(n_seq)])
            for j in range(1, n_seq):
                source = source + jnp.where(i == j, pick([near[j] for near in nearest]), 0)

            @pl.when(i == 0)
            def _():
                tokens_in[1].wait()

            @pl.when(i > 0)
            def _():
                arrived = x_ref.at[block(source), :]
                remote(
                    arrived, arrived, send_sems.at[TOKENS], token_sems.at[source], at.z_peer(source)
                ).wait_recv()

            @pl.when(i == n_seq - 1)
            def _():
                begin(cot_in)

            rows = block(source)
            inputs = x_ref[rows, :].astype(F32)
            hidden = (inputs * inverse_rms(inputs) * gain_one_ref[...]).astype(LOW)
            for tile in range(width // 256):
                cols = slice(256 * tile, 256 * tile + 256)
                q, k, v = [dot(hidden, ref[:, cols]) for ref in (wq_ref, wk_ref, wv_ref)]
                q_t_ref[cols, rows] = q.T.astype(LOW)
                k_t_ref[cols, rows] = k.T.astype(LOW)
                v_t_ref[cols, rows] = v.T.astype(LOW)
                for b in range(2):
                    lanes = slice(128 * b, 128 * b + 128)
                    q_ref[2 * tile + b, rows, :] = q[:, lanes].astype(LOW)
                    k_ref[2 * tile + b, rows, :] = k[:, lanes].astype(LOW)
                    v_ref[2 * tile + b, rows, :] = v[:, lanes].astype(LOW)

        start(weight_loads(0, 0))
        score_refs = (acc_ref, resid_ref)

        def put_scores(pair, b):
            rows = pl.ds(pl.multiple_of((2 * pair + b) * head_dim, head_dim), head_dim)
            keys = jnp.concatenate([k_ref[pair], key_seg_ref[...]], axis=1)
            q_t = jnp.concatenate([zero_padded(q_t_ref[rows, :], b), query_seg_ref[...]], axis=0)

            def half_of(half):
                cols = slice(256 * half, 256 * half + 256)
                score_refs[b][:, cols] = dot(keys, q_t[:, cols])

            return half_of

        def put_attended(pair, b, slot):
            h = 2 * pair + b
            rows = pl.ds(pl.multiple_of(h * head_dim, head_dim), head_dim)
            v_t = v_t_ref[rows, :]

            def half_of(half):
                cols = slice(256 * half, 256 * half + 256)
                bias = jnp.concatenate(
                    [
                        jnp.concatenate(
                            [bias_ref[h, kb - qb + blocks - 1] for qb in (2 * half, 2 * half + 1)], axis=1
                        )
                        for kb in range(blocks)
                    ],
                    axis=0,
                )
                scores = score_refs[b][:, cols] + bias
                powers = jnp.exp(scores - jnp.max(scores, axis=0, keepdims=True))
                inverse = 1.0 / jnp.sum(powers, axis=0, keepdims=True)
                probs = powers.astype(LOW)
                probs_ref[slot, b, :, cols] = probs
                attended_t_ref[rows, cols] = (dot(v_t, probs) * inverse).astype(LOW)
                inverse_ref[pl.ds(h, 1), cols] = inverse

            return half_of

        first = put_scores(0, 0)
        for half in range(2):
            first(half)

        @pl.loop(0, pairs)
        def _(pair):
            slot = lax.rem(pair, 2)

            @pl.when(pair >= 2)
            def _():
                probs_copy(pair - 2, slot, True).wait()

            for b in range(2):
                ahead = put_scores(pair, 1) if b == 0 else put_scores(jnp.minimum(pair + 1, pairs - 1), 0)
                now = put_attended(pair, b, slot)
                for half in range(2):
                    ahead(half)
                    now(half)
            probs_copy(pair, slot, True).start()

        output_load.wait()
        attended = attended_t_ref[...].T
        for tile in range(width // 256):
            cols = slice(256 * tile, 256 * tile + 256)
            resid_ref[:, cols] = x_ref[:, cols].astype(F32) + dot(attended, wo_ref[:, cols])

        @pl.loop(0, blocks)
        def _(i):
            resid = resid_ref[block(i), :]
            branch_ref[block(i), :] = (resid * inverse_rms(resid) * gain_two_ref[...]).astype(LOW)
            acc_ref[block(i), :] = resid

        for pair in (pairs - 2, pairs - 1):
            probs_copy(pair, pair % 2, True).wait()

        @pl.loop(0, tiles)
        def _(g):
            slot = lax.rem(g, 2)

            @pl.when(g >= 2)
            def _():
                slope_copy(g - 2, slot, True).wait()

            wait(weight_loads(g, slot))

            @pl.when(g < tiles - 1)
            def _():
                start(weight_loads(g + 1, 1 - slot))

            gates = [dot(branch_ref[...], wgu_ref[slot, :, 256 * i : 256 * i + 256]) for i in range(4)]
            activs = []
            for sub in range(2):
                gate, upper = gates[sub], gates[2 + sub]
                lanes = slice(256 * sub, 256 * sub + 256)
                square = gate * gate
                curve = jnp.tanh(0.7978845608028654 * gate * (1.0 + 0.044715 * square))
                gelu = 0.5 * gate * (1.0 + curve)
                slope = 0.5 * (1.0 + curve) + 0.5 * gate * (1.0 - curve * curve) * (
                    0.7978845608028654 * (1.0 + 3 * 0.044715 * square)
                )
                activ = gelu * upper
                probs_ref[slot, 0, :, lanes] = gelu.astype(LOW)
                probs_ref[slot, 1, :, lanes] = (upper * slope).astype(LOW)
                activ_t_ref[2 * g + sub] = activ.T.astype(LOW)
                activs.append(activ.astype(LOW))
            down = wd_ref[pl.ds(pl.multiple_of(slot * 512, 512), 512)]
            acc_ref[...] += dot(jnp.concatenate(activs, axis=1), down)

            @pl.when(g < tiles - 2)
            def _():
                slope_copy(g, slot, True).start()


        mixed_ref[...] = acc_ref[...].astype(LOW)

    pl.run_scoped(
        forward,
        bias_ref=VMEM((heads, 2 * blocks - 1, 128, 128), F32),
        key_seg_ref=VMEM((span, 128), LOW),
        query_seg_ref=VMEM((128, span), LOW),
    )
    arrive(COT, three_blocks, one_block)

    def backward(hidden_t_ref, d_att_ref, d_k_ref, d_v_ref, d_probs_ref):
        for s in range(GROUP):
            product = dot(activ_t_ref[s], cot_ref[...]).astype(LOW)
            for p in range(4):
                for i in range(width // 128):
                    ff_own[p, s % 2, s // 4, (s // 2) % 2, 64 * i : 64 * i + 64, :] = product[
                        64 * p : 64 * p + 64, 128 * i : 128 * i + 128
                    ]
        ff.stage0(0)
        ff.stage0(1)
        sent(COT, three_blocks)
        begin(mixed_back)

        def d_slot(g, k, lanes, half):
            n = 2 * lanes + half
            return att_own.at[2 * g + k, n // 4, (n // 2) % 2, n % 2, pl.ds(0, 256), :]

        def put_d_sides(g):
            slot = g % 2
            for sub in range(2):
                lanes = slice(256 * sub, 256 * sub + 256)
                d_act = dot_back(cot_ref[...], wd_ref[512 * slot + 256 * sub : 512 * slot + 256 * sub + 256, :])
                for k in range(2):
                    d_side = (d_act * probs_ref[slot, 1 - k, :, lanes].astype(F32)).astype(LOW)
                    for i in range(2):
                        for half in range(2):
                            d_slot(g, k, 2 * sub + i, half)[...] = d_side[
                                256 * half : 256 * half + 256, 128 * i : 128 * i + 128
                            ]

        def add_d_hidden(g, first):
            slot = g % 2
            d_both = jnp.concatenate(
                [
                    jnp.concatenate([d_slot(g, k, lanes, half)[...] for half in range(2)], axis=0)
                    for k in range(2)
                    for lanes in range(4)
                ],
                axis=1,
            )
            for tile in range(width // 256):
                cols = slice(256 * tile, 256 * tile + 256)
                term = dot_back(d_both, wgu_ref[slot, cols, :])
                acc_ref[:, cols] = term if first else acc_ref[:, cols] + term

        steps_back = list(range(tiles - 1, -1, -1))
        put_d_sides(steps_back[0])
        for i, g in enumerate(steps_back):
            if g >= 2:
                weight_loads(g - 2, g % 2)[0].start()
                slope_copy(g - 2, g % 2, False).start()
            if i >= 2:
                wait(weight_loads(g, g % 2)[1:])
            if g >= 1:
                if i >= 1:
                    weight_loads(g - 1, (g - 1) % 2)[0].wait()
                    slope_copy(g - 1, (g - 1) % 2, False).wait()
                put_d_sides(g - 1)
            rows = slice(128 * i, 128 * i + 128)
            resid = resid_ref[rows, :]
            hidden_t_ref[:, rows] = (resid * inverse_rms(resid) * gain_two_ref[...]).T.astype(LOW)
            add_d_hidden(g, i == 0)
            if g >= 2:
                start(weight_loads(g - 2, g % 2)[1:])
            if i <= 1:
                ff.stage1(i)

        start(loads)
        probs_copy(0, 0, False).start()


        def product(g, k, sub):
            right = jnp.concatenate(
                [
                    jnp.concatenate([d_slot(g, k, 2 * sub + i, half)[...] for half in range(2)], axis=0)
                    for i in range(2)
                ],
                axis=1,
            )
            result = dot(hidden_t_ref[...], right).astype(LOW)
            for s in range(GROUP):
                for i in range(2):
                    place = shard * (2 * sub + i)
                    ff_own[4 + 2 * g + k, s % 2, s // 4, (s // 2) % 2, place : place + shard, :] = result[
                        shard * s : shard * s + shard, 128 * i : 128 * i + 128
                    ]

        def norm_back(grad_ref, vector_ref, gain_ref, extra_ref, out_ref, low_ref, row):
            total = jnp.zeros((1, width), F32)
            for i in range(blocks):
                rows = slice(128 * i, 128 * i + 128)
                vector = vector_ref[rows, :].astype(F32)
                scale = inverse_rms(vector)
                normed = vector * scale
                grad = grad_ref[rows, :]
                total = total + jnp.sum(grad * normed, axis=0, keepdims=True)
                inner = grad * gain_ref[...]
                result = extra_ref[rows, :].astype(F32) + scale * (
                    inner - normed * jnp.mean(inner * normed, -1, keepdims=True)
                )
                if out_ref is not None:
                    out_ref[rows, :] = result
                low_ref[rows, :] = result.astype(LOW)
            for i in range(width // 128):
                small_own[0, row + i : row + i + 1, :] = total[:, 128 * i : 128 * i + 128]

        norm_back(acc_ref, resid_ref, gain_two_ref, cot_ref, acc_ref, d_branch_ref, 12)

        def share(sums, j, left_t, right):
            for k in range(2):
                half = slice(width // 2 * k, width // 2 * k + width // 2)
                product = dot(left_t, right[:, half]).astype(LOW)
                for s in range(GROUP):
                    for i in range(width // 256):
                        sums.own[2 * j + k, s % 2, s // 4, (s // 2) % 2, shard * i : shard * i + shard, :] = product[
                            shard * s : shard * s + shard, 128 * i : 128 * i + 128
                        ]
            sums.stage0(j)

        for tile in range(width // 256):
            rows = slice(256 * tile, 256 * tile + 256)
            d_att_t = dot_back(d_branch_ref[...], wo_ref[rows, :]).T
            for i in range(256 // head_dim):
                h = 256 // head_dim * tile + i
                d_att_t_ref[head_dim * h : head_dim * (h + 1), :] = (
                    d_att_t[head_dim * i : head_dim * (i + 1), :] * inverse_ref[h : h + 1, :]
                ).astype(LOW)
            for i in range(2):
                d_att_ref[2 * tile + i] = d_att_t_ref[256 * tile + 128 * i : 256 * tile + 128 * i + 128, :].T
        left_half = lax.broadcasted_iota(jnp.int32, (span, 128), 1) < head_dim
        d_probs_refs = (resid_ref, d_probs_ref)

        def put_d_probs(pair, b):
            rows = pl.ds(pl.multiple_of((2 * pair + b) * head_dim, head_dim), head_dim)
            values = v_ref[pair]
            d_att_t = zero_padded(d_att_t_ref[rows, :], b)

            def half_of(half):
                cols = slice(256 * half, 256 * half + 256)
                d_probs_refs[b][:, cols] = dot(values, d_att_t[:, cols])

            return half_of

        across = lax.broadcasted_iota(jnp.int32, (8, 128), 1)

        def put_d_scores(pair, b, slot):
            h = 2 * pair + b
            rows = pl.ds(pl.multiple_of(h * head_dim, head_dim), head_dim)
            k_t = k_t_ref[rows, :]
            sums = [None] * (2 * blocks - 1)

            def half_of(half):
                cols = slice(256 * half, 256 * half + 256)
                d_probs = d_probs_refs[b][:, cols]
                probs = probs_ref[slot, b, :, cols].astype(F32)
                inner = jnp.sum(probs * d_probs, axis=0, keepdims=True) * inverse_ref[pl.ds(h, 1), cols]
                d_scores = probs * (d_probs - inner)
                for kb in range(blocks):
                    for i in range(2):
                        d = kb - (2 * half + i) + blocks - 1
                        part = d_scores[128 * kb : 128 * kb + 128, 128 * i : 128 * i + 128]
                        sums[d] = part if sums[d] is None else sums[d] + part
                d_scores = d_scores.astype(LOW)
                for i in range(2):
                    activ_t_ref[2 * b + i, :, cols] = d_scores[256 * i : 256 * i + 256, :]
                d_q_t_ref[rows, cols] = dot(k_t, d_scores).astype(LOW)
                if half == 1:
                    for d in range(2 * blocks - 1):
                        every, low_lanes = sums[d][:8, :], sums[d][:8, :]
                        for a in range(1, 16):
                            rolled = pltpu.roll(sums[d][8 * a : 8 * a + 8, :], 128 - 8 * a, 1)
                            every = every + rolled
                            low_lanes = low_lanes + jnp.where(across < 128 - 8 * a, rolled, 0.0)
                        diag_ref[h, d] = jnp.concatenate([low_lanes, every - low_lanes], axis=1)

            return half_of

        ff.stage2(0)
        first = put_d_probs(0, 0)
        for half in range(2):
            first(half)

        def attention_back(pair, with_products):
            slot = lax.rem(pair, 2)
            probs_copy(pair, slot, False).wait()

            @pl.when(pair < pairs - 1)
            def _():
                probs_copy(pair + 1, 1 - slot, False).start()

            for b in range(2):
                ahead = put_d_probs(pair, 1) if b == 0 else put_d_probs(jnp.minimum(pair + 1, pairs - 1), 0)
                now = put_d_scores(pair, b, slot)
                for half in range(2):
                    ahead(half)
                    if with_products:
                        product(pair, b, half)
                    now(half)
            lanes = pl.ds(pl.multiple_of(pair * 128, 128), 128)
            d_att, queries = d_att_ref[pair], q_ref[pair]
            blank = jnp.zeros_like(d_att)
            d_scores = [activ_t_ref[2 * b : 2 * b + 2].reshape(span, span) for b in range(2)]
            d_v_ref[:, lanes] = (
                dot(probs_ref[slot, 0], jnp.where(left_half, d_att, blank))
                + dot(probs_ref[slot, 1], jnp.where(left_half, blank, d_att))
            ).astype(LOW)
            d_k_ref[:, lanes] = (
                dot(d_scores[0], jnp.where(left_half, queries, blank))
                + dot(d_scores[1], jnp.where(left_half, blank, queries))
            ).astype(LOW)

        @pl.loop(0, tiles)
        def _(pair):
            attention_back(pair, True)
            ff.stage0(2 + pair)

            @pl.when(pair == 1)
            def _():
                ff.stage2(1)
                ff.stage1(2)
                ff.stage3(0)

            @pl.when(pair == 2)
            def _():
                ff.stage1(3)

            @pl.when(pair == 3)
            def _():
                ff.stage3(1)

        @pl.loop(tiles, pairs)
        def _(pair):
            attention_back(pair, False)

            @pl.when(pair == tiles)
            def _():
                ff.hop(0, 1)

        ff.stage2(2)
        ff.stage1(4)
        branch_ref[...] = d_q_t_ref[...].T
        wait(loads)
        for tile in range(width // 256):
            rows = slice(256 * tile, 256 * tile + 256)
            resid_ref[:, rows] = (
                dot_back(branch_ref[...], wgu_ref[0, rows, :width])
                + dot_back(d_k_ref[...], wgu_ref[1, rows, :width])
                + dot_back(d_v_ref[...], wd_ref[rows, :])
            )
        norm_back(resid_ref, x_ref, gain_one_ref, acc_ref, None, d_back_ref, 18)
        ff.hop(1, 1)
        begin(tokens_back[0])
        ff.stage2(3)
        ff.stage1(5)
        ff.stage3(2)
        begin(tokens_back[1])
        share(att, 0, attended_t_ref[...], d_branch_ref[...])
        ff.hop(0, 2)

        @pl.loop(0, blocks)
        def _(i):
            inputs = x_ref[block(i), :].astype(F32)
            hidden_t_ref[:, block(i)] = (inputs * inverse_rms(inputs) * gain_one_ref[...]).T.astype(LOW)

        share(att, 1, hidden_t_ref[...], d_v_ref[...])
        share(att, 2, hidden_t_ref[...], d_k_ref[...])
        ff.stage2(4)
        att.stage1(0)
        share(att, 3, hidden_t_ref[...], branch_ref[...])
        ff.hop(2, 1)
        begin(tokens_back[2])
        ff.stage3(3)

    pl.run_scoped(
        backward,
        hidden_t_ref=VMEM((width, span), LOW),
        d_att_ref=VMEM((pairs, span, 128), LOW),
        d_k_ref=VMEM((span, width), LOW),
        d_v_ref=VMEM((span, width), LOW),
        d_probs_ref=VMEM((span, span), F32),
    )

    flip = (
        lax.broadcasted_iota(jnp.int32, (256, 256), 0) + lax.broadcasted_iota(jnp.int32, (256, 256), 1) == 255
    ).astype(F32)

    @pl.loop(0, heads)
    def _(h):
        tiles_ = diag_ref[h].reshape(8 * (2 * blocks - 1), 256)
        flipped = jnp.dot(tiles_, flip, precision=lax.Precision.HIGHEST, preferred_element_type=F32)
        totals = [
            jnp.sum(pltpu.roll(flipped[8 * d : 8 * d + 8, :], 0, 1, stride=1, stride_axis=0), axis=0, keepdims=True)
            for d in range(2 * blocks - 1)
        ]
        pieces = [totals[0][:, 128:]]
        for d in range(1, 2 * blocks - 1):
            pieces.append(totals[d - 1][:, :128] + totals[d][:, 128:])
        pieces.append(totals[-1][:, :128])
        offset_ref[pl.ds(h, 1), :] = jnp.concatenate(pieces, axis=1)

    one_hot = (lax.broadcasted_iota(jnp.int32, (128, buckets_wide), 0) == bucket_ref[...]).astype(F32)
    small_own[0, :12, :] = lax.dot_general(
        offset_ref[:12, :], one_hot, (((1,), (1,)), ((), ())),
        precision=lax.Precision.HIGHEST, preferred_element_type=F32,
    )
    small_peers = [at.core_peer, at.x_peer, at.y_peer]
    steps = len(small_peers)

    def small_copy(i):
        return remote(small_own.at[i], small_got.at[i], small_sems.at[3], small_sems.at[i], small_peers[i])

    def small_row(i):
        return remote(
            small_own.at[steps], small_rows.at[at.z], small_sems.at[4], small_sems.at[5],
            at.z_peer(lax.rem(at.z + i, n_seq)),
        )

    def small_step(i):
        small_copy(i).wait_recv()
        small_own[i + 1] = small_own[i] + small_got[i]
        if i + 1 < steps:
            small_copy(i + 1).start()

    inner = (at.z > 0) & (at.z < n_seq - 1)
    small_copy(0).start()
    ff.stage2(5)
    att.stage1(1)
    ff.stage3(4)
    small_step(0)
    ff.hop(1, 2)
    att.stage2(0)
    att.stage1(2)
    ff.hop(3, 1)
    begin(tokens_back[3])
    ff.stage3(5)
    ff.hop(2, 2)
    att.stage2(1)
    att.stage1(3)
    ff.hop(4, 1)
    ff.hop(3, 2)
    att.stage3(0)
    small_step(1)
    att.stage2(2)
    ff.hop(5, 1)
    ff.hop(4, 2)
    att.stage3(1)
    att.stage2(3)
    att.hop(0, 1)
    ff.hop(5, 2)
    small_step(2)
    small_rows[at.z] = small_own[steps]
    att.stage3(2)
    att.hop(1, 1)
    att.hop(0, 2)
    att.stage3(3)
    for i in range(1, n_seq):
        small_row(i).start()
    att.hop(2, 1)
    att.hop(1, 2)
    att.hop(3, 1)
    att.hop(2, 2)
    att.hop(3, 2)

    @pl.loop(0, FF_JOBS)
    def _(j):
        ff.finish(j, ff_out)

    @pl.loop(0, ATT_JOBS)
    def _(j):
        att.finish(j, att_out)


    three_rows = small_rows.at[pl.ds(0, n_seq - 1)]
    remote(three_rows, three_rows, small_sems.at[4], small_sems.at[5], at.core_peer).wait_recv()
    total = small_rows[0]
    for i in range(1, n_seq):
        total = total + small_rows[i]
    small_rows[0] = total
    small_store = pltpu.make_async_copy(small_rows.at[0], small_out, own_sems.at[5])
    small_store.start()
    ff.drain(ff_out)
    att.drain(att_out)
    three_steps = small_own.at[pl.ds(0, steps)]
    remote(three_steps, three_steps, small_sems.at[3], small_sems.at[0], at.core_peer).wait_send()
    remote(three_rows, three_rows, small_sems.at[4], small_sems.at[5], at.core_peer).wait_send()
    sent(SEGS, three_segs)
    for kind in (TOKENS, MIXED, BACK):
        sent(kind, three_blocks)
    for kind in (MIXED, BACK):
        arrive(kind, three_blocks, one_block)
    small_store.wait()


def layer(n_dp, n_seq, tokens, cot, seg, buckets, gain_one, gain_two, table, weights):
    width = tokens.shape[-1]
    span = tokens.shape[0] * tokens.shape[1]
    heads = table.shape[0]
    ff_width = weights[4].shape[1]
    ff_pieces, att_pieces = 2 * FF_JOBS, 2 * ATT_JOBS
    low = lambda *shape: VMEM(shape, LOW)
    dma = pltpu.SemaphoreType.DMA
    steps = 3

    def sums(pieces, rows):
        return [
            low(pieces, 2, 2, 2, rows, 128), low(pieces, 2, 2, rows, 128), low(pieces, 2, rows, 128),
            low(pieces, rows, 128), low(pieces, rows, 128), low(pieces, rows, 128),
            dma((5,)), dma((3, pieces // 2)), dma((2, pieces)), dma((1,)),
        ]

    pairs = low(heads // 2, span, 128)
    rows, turned = low(span, width), low(width, span)
    any_, vmem = pl.BlockSpec(memory_space=pl.ANY), pl.BlockSpec(memory_space=VMEM)
    result = lambda *shape: jax.ShapeDtypeStruct(shape, LOW)
    return pl.pallas_call(
        functools.partial(layer_kernel, n_dp, n_seq),
        out_shape=[
            result(n_seq, span // n_seq, width), result(n_seq, span // n_seq, width),
            result(ff_pieces, FF_ROWS, 128), result(att_pieces, ATT_ROWS, 128),
            jax.ShapeDtypeStruct((24, 128), F32),
            result(heads, span, span), result(ff_width // 512, 2, span, 512),
        ],
        in_specs=[any_] * 2 + [vmem] * 5 + [any_] * 7,
        out_specs=[any_] * 7,
        scratch_shapes=sums(ff_pieces, FF_ROWS)
        + sums(att_pieces, ATT_ROWS)
        + [
            VMEM((steps + 1, 24, 128), F32), VMEM((steps, 24, 128), F32), VMEM((n_seq, 24, 128), F32),
            dma((6,)),
        ]
        + [
            rows, rows, VMEM((n_seq, 8, 128), jnp.int32), VMEM((n_seq, 8, 128), jnp.int32), rows,
            low(width, width), low(2, width, 1024), low(1024, width), low(2, 2, span, span), VMEM((16, span), F32),
            low(ff_width // 256, 256, span), turned, pairs, pairs, pairs, turned, VMEM((span, width), F32),
            VMEM((span, width), F32), rows, rows, turned, turned, VMEM((16, 1024), F32),
            VMEM((heads, 2 * (span // 128) - 1, 8, 256), F32),
            VMEM((1, 1024), jnp.int32), VMEM((1, width), F32), VMEM((1, width), F32),
            dma((4,)), dma((3, 2)), dma((2,)), dma((5,)), dma((5,)), dma((n_seq,)), dma((6,)),
        ],
        compiler_params=pltpu.CompilerParams(
            collective_id=0, has_side_effects=True, vmem_limit_bytes=VMEM_BYTES
        ),
        name="layer",
    )(tokens, cot, seg, buckets, gain_one, gain_two, table, *weights)


def outputs_kernel(
    n_dp, mixed_ref, tokens_ref, ff_ref, att_ref, small_ref,
    mixed_out, tokens_out, gn_one_out, gq_out, gk_out, gv_out, go_out, table_out, gn_two_out, gg_out, gu_out, gd_out,
    mixed_in, tokens_in, ff_in, att_in, small_in, gn_one, gq, gk, gv, go, table, gn_two, gg, gu, gd, tokens, sems,
):
    copies = [
        pltpu.make_async_copy(src, dst, sems.at[i])
        for i, (src, dst) in enumerate(
            [(small_ref, small_in), (tokens_ref, tokens_in), (ff_ref, ff_in), (att_ref, att_in), (mixed_ref, mixed_in)]
        )
    ]
    for copy in copies:
        copy.start()
    stores = []

    def store(src, dst):
        stores.append(pltpu.make_async_copy(src, dst, sems.at[len(copies) + len(stores)]))
        stores[-1].start()

    width = mixed_ref.shape[-1]
    shard = width // GROUP
    copies[0].wait()
    table[...] = small_in[: table.shape[0], : table.shape[1]]
    store(table, table_out)
    mine = lax.axis_index("dp") // (n_dp // GROUP)
    for row, part, out in ((12, gn_two, gn_two_out), (18, gn_one, gn_one_out)):
        gains = jnp.concatenate([small_in[row + i : row + i + 1, :] for i in range(width // 128)], axis=1)
        total = jnp.zeros((1, shard), F32)
        for s in range(GROUP):
            total = total + jnp.where(mine == s, gains[:, shard * s : shard * s + shard], 0.0)
        part[...] = total
        store(part, out)
    copies[1].wait()
    tokens[...] = tokens_in[...].astype(F32)
    store(tokens, tokens_out)
    copies[2].wait()
    for k, (part, out) in enumerate(((gg, gg_out), (gu, gu_out))):
        for g in range(4):
            for i in range(4):
                col = 512 * g + 128 * i
                part[:, col : col + 128] = ff_in[4 + 2 * g + k, shard * i : shard * i + shard, :].astype(F32)
        store(part, out)
    for p in range(4):
        for i in range(width // 128):
            gd[64 * p : 64 * p + 64, 128 * i : 128 * i + 128] = ff_in[p, 64 * i : 64 * i + 64, :].astype(F32)
    store(gd, gd_out)
    copies[3].wait()
    for j, (part, out) in enumerate(((go, go_out), (gv, gv_out), (gk, gk_out), (gq, gq_out))):
        for k in range(2):
            for i in range(width // 256):
                col = width // 2 * k + 128 * i
                part[:, col : col + 128] = att_in[2 * j + k, shard * i : shard * i + shard, :].astype(F32)
        store(part, out)
    copies[4].wait()
    store(mixed_in, mixed_out)
    for copy in stores:
        copy.wait()


def outputs(n_dp, buckets, heads, mixed, tokens, ff, att, small):
    width = mixed.shape[-1]
    shard = width // GROUP
    full = lambda *shape: jax.ShapeDtypeStruct(shape, F32)
    square, wide = full(shard, width), full(shard, 2048)
    results = [
        jax.ShapeDtypeStruct(mixed.shape, LOW), full(*tokens.shape), full(1, shard), square, square, square, square,
        full(heads, buckets), full(1, shard), wide, wide, full(256, width),
    ]
    any_ = pl.BlockSpec(memory_space=pl.ANY)
    return pl.pallas_call(
        functools.partial(outputs_kernel, n_dp),
        out_shape=results,
        in_specs=[any_] * 5,
        out_specs=[any_] * len(results),
        scratch_shapes=[VMEM(a.shape, a.dtype) for a in [mixed, tokens, ff, att, small] + results[2:] + results[1:2]]
        + [pltpu.SemaphoreType.DMA((5 + len(results),))],
        compiler_params=pltpu.CompilerParams(vmem_limit_bytes=VMEM_BYTES),
        name="outputs",
    )(mixed, tokens, ff, att, small)


def solution(mesh):
    n_dp, n_seq = mesh.shape["dp"], mesh.shape["seq"]

    def on_device(
        tokens, segments, offset_buckets, norm_attn, w_query, w_key, w_value, w_output, bias_table,
        norm_ff, w_gate, w_up, w_down, cotangent,
    ):
        weights = (w_query, w_key, w_value, w_output, w_gate, w_up, w_down)
        sums = layer(
            n_dp, n_seq, tokens, cotangent, segments, offset_buckets, norm_attn, norm_ff, bias_table.T, weights
        )[:5]
        results = list(outputs(n_dp, bias_table.shape[0], bias_table.shape[1], *sums))
        results[2], results[7], results[8] = results[2].reshape(-1), results[7].T, results[8].reshape(-1)
        rest = n_dp // GROUP
        if rest > 1:
            groups = [[i * rest + j for j in range(rest)] for i in range(GROUP)]
            for i in (2, 3, 4, 5, 6, 8, 9, 10, 11):
                results[i] = lax.psum_scatter(
                    results[i], "dp", scatter_dimension=0, axis_index_groups=groups, tiled=True
                )
            results[7] = lax.psum(results[7], "dp", axis_index_groups=groups)
        return tuple(results)

    rows, shares = P("dp", "seq", None), P("dp", None)
    return jax.shard_map(
        on_device,
        mesh=mesh,
        in_specs=(rows, P("dp", "seq")) + (P(),) * 11 + (rows,),
        out_specs=(rows, rows, P("dp"), shares, shares, shares, shares, P(), P("dp"), shares, shares, shares),
        check_vma=False,
    )
```

```python
import functools

import jax
import jax.numpy as jnp
from jax import lax
from jax.experimental import pallas as pl
from jax.experimental.pallas import tpu as pltpu
from jax.sharding import PartitionSpec as P

MESH = pl.DeviceIdType.MESH
VMEM = pltpu.VMEM
LOW = jnp.bfloat16
F32 = jnp.float32
EPSILON = 1e-06
MASKED = -1e30
GROUP = 8
VMEM_BYTES = 63 * 2**20


def dot(left, right):
    return jnp.dot(left, right, preferred_element_type=F32)


def dot_back(left, right):
    return lax.dot_general(left, right, (((1,), (1,)), ((), ())), preferred_element_type=F32)


def inverse_rms(values):
    return lax.rsqrt(jnp.mean(values * values, -1, keepdims=True) + EPSILON)


def zero_padded(block, half):
    blank = jnp.zeros_like(block)
    return jnp.concatenate([blank, block] if half else [block, blank], axis=0)


class Place:
    def __init__(self, n_dp, n_seq):
        stride = n_dp // GROUP
        dp = lax.axis_index("dp")
        z = lax.axis_index("seq")
        index = dp // stride
        self.n_seq = n_seq
        self.core, self.x, self.y, self.z = index % 2, (index // 2) % 2, index // 4, z
        self.dp = dp
        self.core_peer = (dp + stride * (1 - 2 * self.core), z)
        self.x_peer = (dp + 2 * stride * (1 - 2 * self.x), z)
        self.y_peer = (dp + 4 * stride * (1 - 2 * self.y), z)

    def z_peer(self, z):
        return (self.dp, z)

    def z_pair(self, bit):
        return (self.dp, self.z + bit * (1 - 2 * ((self.z // bit) % 2)))


def remote(src, dst, send_sem, recv_sem, peer):
    return pltpu.make_async_remote_copy(
        src_ref=src, dst_ref=dst, send_sem=send_sem, recv_sem=recv_sem, device_id=peer, device_id_type=MESH
    )


class Sums:
    def __init__(self, place, own, got0, got1, got2, low_z, high_z, send_sems, recv_sems, z_sems, out_sem):
        self.place, self.own = place, own
        self.got0, self.got1, self.got2, self.low_z, self.high_z = got0, got1, got2, low_z, high_z
        self.send_sems, self.recv_sems, self.z_sems, self.out_sem = send_sems, recv_sems, z_sems, out_sem

    def arrived(self, stage, j):
        got = (self.got0, self.got1, self.got2)[stage].at[pl.ds(2 * j, 2)]
        remote(got, got, self.send_sems.at[stage], self.recv_sems.at[stage, j], self.place.core_peer).wait_recv()

    def send0(self, j, k):
        at, p = self.place, 2 * j + k
        remote(
            self.own.at[p, 1 - at.core], self.got0.at[p], self.send_sems.at[0], self.recv_sems.at[0, j], at.core_peer
        ).start()

    def send1(self, j, k):
        at, p = self.place, 2 * j + k
        mine = self.own.at[p, at.core]
        src = mine.at[1 - at.y] if k else mine.at[:, 1 - at.x]
        remote(
            src, self.got1.at[p], self.send_sems.at[1], self.recv_sems.at[1, j], at.y_peer if k else at.x_peer
        ).start()

    def send2(self, j, k):
        at, p = self.place, 2 * j + k
        mine = self.own.at[p, at.core]
        src = mine.at[at.y, 1 - at.x] if k else mine.at[1 - at.y, at.x]
        remote(
            src, self.got2.at[p], self.send_sems.at[2], self.recv_sems.at[2, j], at.x_peer if k else at.y_peer
        ).start()

    def kept(self, p):
        at = self.place
        return self.own.at[p, at.core, at.y, at.x]

    def up(self, p, first):
        src = self.kept(p) if first else self.got2.at[p]
        return remote(
            src, self.low_z.at[p], self.send_sems.at[3], self.z_sems.at[0, p], self.place.z_peer(self.place.z + 1)
        )

    def down(self, p, first):
        src = self.kept(p) if first else self.got1.at[p, 0]
        return remote(
            src, self.high_z.at[p], self.send_sems.at[4], self.z_sems.at[1, p], self.place.z_peer(self.place.z - 1)
        )

    def stage0(self, j):
        for k in range(2):
            self.send0(j, k)

    def stage1(self, j):
        at = self.place
        self.arrived(0, j)
        for k in range(2):
            p = 2 * j + k
            for a in range(2):
                for b in range(2):
                    self.own[p, at.core, a, b] = self.own[p, at.core, a, b] + self.got0[p, a, b]
            self.send1(j, k)

    def stage2(self, j):
        at = self.place
        self.arrived(1, j)
        for k in range(2):
            p = 2 * j + k
            for a in range(2):
                if k:
                    self.own[p, at.core, at.y, a] = self.own[p, at.core, at.y, a] + self.got1[p, a]
                else:
                    self.own[p, at.core, a, at.x] = self.own[p, at.core, a, at.x] + self.got1[p, a]
            self.send2(j, k)

    def stage3(self, j):
        at = self.place
        self.arrived(2, j)
        for k in range(2):
            p = 2 * j + k
            self.own[p, at.core, at.y, at.x] = self.own[p, at.core, at.y, at.x] + self.got2[p]
        self.hop(j, 0)

    def hop(self, j, step):
        at = self.place
        last = at.n_seq - 1

        @pl.when(at.z == step)
        def _():
            for k in range(2):
                p = 2 * j + k
                if step:
                    self.up(p, False).wait_recv()
                    self.got2[p] = self.low_z[p] + self.own[p, at.core, at.y, at.x]
                self.up(p, step == 0).start()

        @pl.when(at.z == last - step)
        def _():
            for k in range(2):
                p = 2 * j + k
                if step:
                    self.down(p, False).wait_recv()
                    self.got1[p, 0] = self.high_z[p] + self.own[p, at.core, at.y, at.x]
                self.down(p, step == 0).start()

    def finish(self, j, out):
        at = self.place
        last = at.n_seq - 1
        for k in range(2):
            p = 2 * j + k

            @pl.when(at.z == last)
            def _():
                self.up(p, False).wait_recv()
                self.low_z[p] = self.low_z[p] + self.own[p, at.core, at.y, at.x]

            @pl.when(at.z == 0)
            def _():
                self.down(p, False).wait_recv()
                self.low_z[p] = self.high_z[p] + self.own[p, at.core, at.y, at.x]

            @pl.when((at.z > 0) & (at.z < last))
            def _():
                total = self.low_z[p].astype(F32) + self.high_z[p].astype(F32)
                self.low_z[p] = (total + self.own[p, at.core, at.y, at.x].astype(F32)).astype(LOW)

            pltpu.make_async_copy(self.low_z.at[p], out.at[p], self.out_sem.at[0]).start()

    def drain(self, out):
        at = self.place
        last = at.n_seq - 1

        def sent(stage, all_pieces):
            remote(
                all_pieces, all_pieces, self.send_sems.at[stage], self.recv_sems.at[0, 0], at.core_peer
            ).wait_send()

        for stage, got in enumerate((self.got0, self.got1, self.got2)):
            sent(stage, got)

        @pl.when(at.z < last)
        def _():
            sent(3, self.low_z)

        @pl.when(at.z > 0)
        def _():
            sent(4, self.high_z)

        pltpu.make_async_copy(self.low_z, out, self.out_sem.at[0]).wait()


FF_JOBS, ATT_JOBS = 6, 4
FF_ROWS, ATT_ROWS = 384, 288


def layer_kernel(
    n_dp, n_seq,
    tokens_hbm, cot_hbm, seg_ref, bucket_row, gain_one_row, gain_two_row, table_ref,
    wq_hbm, wk_hbm, wv_hbm, wo_hbm, wg_hbm, wu_hbm, wd_hbm,
    mixed_out, tokens_out, ff_out, att_out, small_out, probs_hbm, slope_hbm,
    ff_own, ff_got0, ff_got1, ff_got2, ff_low, ff_high, ff_sends, ff_recvs, ff_z_recvs, ff_out_sem,
    att_own, att_got0, att_got1, att_got2, att_low, att_high, att_sends, att_recvs, att_z_recvs, att_out_sem,
    small_own, small_got, small_rows, small_sems,
    x_ref, cot_ref, seg_send_ref, seg_rows_ref, mixed_ref,
    wo_ref, wgu_ref, wd_ref, probs_ref, inverse_ref,
    activ_t_ref, attended_t_ref, q_ref, k_ref, v_ref, k_t_ref, resid_ref, acc_ref, branch_ref, d_branch_ref,
    d_att_t_ref, d_q_t_ref, offset_ref, diag_ref, bucket_ref, gain_one_ref, gain_two_ref,
    load_sems, ff_load_sems, probs_sems, send_sems, recv_sems, token_sems, own_sems,
):
    span, width = x_ref.shape
    heads, buckets = table_ref.shape
    buckets_wide = bucket_ref.shape[1]
    head_dim = width // heads
    blocks = span // 128
    pairs = heads // 2
    tiles = wg_hbm.shape[1] // 512
    shard = width // GROUP
    at = Place(n_dp, n_seq)
    d_back_ref = cot_ref

    wq_ref, wk_ref, wv_ref = wgu_ref.at[0, :, pl.ds(0, width)], wgu_ref.at[1, :, pl.ds(0, width)], wd_ref.at[pl.ds(0, width)]
    loads = [
        pltpu.make_async_copy(src, dst, load_sems.at[i])
        for i, (src, dst) in enumerate([(wq_hbm, wq_ref), (wk_hbm, wk_ref), (wv_hbm, wv_ref)])
    ]
    output_load = pltpu.make_async_copy(wo_hbm, wo_ref, load_sems.at[3])

    def weight_loads(g, slot):
        cols = pl.ds(pl.multiple_of(g * 512, 512), 512)
        sides = [
            (wd_hbm.at[cols, :], wd_ref.at[pl.ds(pl.multiple_of(slot * 512, 512), 512)]),
            (wg_hbm.at[:, cols], wgu_ref.at[slot, :, pl.ds(0, 512)]),
            (wu_hbm.at[:, cols], wgu_ref.at[slot, :, pl.ds(512, 512)]),
        ]
        return [pltpu.make_async_copy(src, dst, ff_load_sems.at[i, slot]) for i, (src, dst) in enumerate(sides)]

    def slope_copy(g, slot, store):
        sides = (slope_hbm.at[g], probs_ref.at[slot])
        return pltpu.make_async_copy(*(sides[::-1] if store else sides), probs_sems.at[slot])

    def probs_copy(pair, slot, store):
        sides = (probs_hbm.at[pl.ds(2 * pair, 2)], probs_ref.at[slot])
        return pltpu.make_async_copy(*(sides[::-1] if store else sides), probs_sems.at[slot])

    def start(copies):
        for copy in copies:
            copy.start()

    def wait(copies):
        for copy in copies:
            copy.wait()

    barrier = pltpu.get_barrier_semaphore()
    peers = [at.core_peer, at.x_peer, at.y_peer] + [
        at.z_peer(lax.rem(at.z + i, n_seq)) for i in range(1, n_seq)
    ]
    for peer in peers:
        pl.semaphore_signal(barrier, inc=1, device_id=peer, device_id_type=MESH)
    start(loads)
    output_load.start()
    for i in range(n_seq):
        seg_send_ref[i] = jnp.broadcast_to(seg_ref[i : i + 1, :], (8, 128))

    pl.semaphore_wait(barrier, len(peers))

    ff = Sums(
        at, ff_own, ff_got0, ff_got1, ff_got2, ff_low, ff_high, ff_sends, ff_recvs, ff_z_recvs, ff_out_sem
    )
    att = Sums(
        at, att_own, att_got0, att_got1, att_got2, att_low, att_high, att_sends, att_recvs, att_z_recvs, att_out_sem
    )

    def block(z):
        return pl.ds(pl.multiple_of(z * 128, 128), 128)

    def pick(values):
        return sum(jnp.where(at.z == z, value, 0) for z, value in enumerate(values))

    nearest = [sorted(range(n_seq), key=lambda other: abs(other - z)) for z in range(n_seq)]

    def exchange(kind, src, dst, recv_of=None):
        sends = []
        for i in range(n_seq - 1):
            to = pick([near[i + 1] for near in nearest])
            recv = recv_sems.at[kind] if recv_of is None else recv_of.at[at.z]
            sends.append(remote(src(to), dst(at.z), send_sems.at[kind], recv, at.z_peer(to)))
        return sends, pltpu.make_async_copy(src(at.z), dst(at.z), own_sems.at[kind])

    def begin(exchanged):
        sends, own = exchanged
        start(sends)
        own.start()

    def arrive(kind, others, one):
        remote(others, others, send_sems.at[kind], recv_sems.at[kind], at.core_peer).wait_recv()
        pltpu.make_async_copy(one, one, own_sems.at[kind]).wait()

    def sent(kind, others):
        remote(others, others, send_sems.at[kind], recv_sems.at[kind], at.core_peer).wait_send()

    SEGS, TOKENS, COT, MIXED, BACK = range(5)
    segs = exchange(SEGS, lambda z: seg_send_ref.at[z], lambda z: seg_rows_ref.at[z])
    tokens_in = exchange(TOKENS, lambda z: tokens_hbm.at[z], lambda z: x_ref.at[block(z), :], token_sems)
    cot_in = exchange(COT, lambda z: cot_hbm.at[z], lambda z: cot_ref.at[block(z), :])
    mixed_back = exchange(MIXED, lambda z: mixed_ref.at[block(z), :], lambda z: mixed_out.at[z])
    tokens_back = [
        exchange(
            BACK,
            lambda z, part=part: d_back_ref.at[pl.ds(pl.multiple_of(z * 128 + 32 * part, 32), 32), :],
            lambda z, part=part: tokens_out.at[z, pl.ds(32 * part, 32), :],
        )
        for part in range(4)
    ]
    three_segs, one_seg = seg_rows_ref.at[pl.ds(0, n_seq - 1)], seg_rows_ref.at[0]
    three_blocks, one_block = x_ref.at[pl.ds(0, 128 * (n_seq - 1)), :], x_ref.at[pl.ds(0, 128), :]
    begin(segs)
    bucket_ref[...] = jnp.zeros_like(bucket_ref)
    bucket_ref[:, : bucket_row.shape[0]] = bucket_row[...].reshape(1, -1)
    gain_one_ref[...] = gain_one_row[...].reshape(1, -1)
    gain_two_ref[...] = gain_two_row[...].reshape(1, -1)
    begin(tokens_in)
    def forward(bias_ref, key_seg_ref, query_seg_ref):
        one_hot = (lax.broadcasted_iota(jnp.int32, (buckets, buckets_wide), 0) == bucket_ref[...]).astype(F32)
        offset_ref[:heads, :] = lax.dot_general(
            table_ref[...], one_hot, (((1,), (0,)), ((), ())),
            precision=lax.Precision.HIGHEST, preferred_element_type=F32,
        )

        @pl.loop(0, heads)
        def _(h):
            row = offset_ref[pl.ds(h, 1), :]
            for d in range(2 * blocks - 1):
                window = jnp.broadcast_to(row[:, 128 * d : 128 * d + 256], (128, 256))
                bias_ref[h, d] = pltpu.roll(window, 129, 1, stride=1, stride_axis=0)[:, :128].T

        arrive(SEGS, three_segs, one_seg)
        seg_rows = [seg_rows_ref[i, 0:1, :].astype(F32) for i in range(blocks)]
        for i in range(blocks):
            column = jnp.broadcast_to(seg_rows[i], (128, 128)).T
            across = lax.broadcasted_iota(jnp.int32, (128, 128), 1).astype(F32)
            along = lax.broadcasted_iota(jnp.int32, (128, 128), 0).astype(F32)
            key_seg_ref[128 * i : 128 * i + 128, :] = jnp.where(column == across, 1.0, 0.0).astype(LOW)
            query_seg_ref[:, 128 * i : 128 * i + 128] = jnp.where(seg_rows[i] == along, 0.0, MASKED).astype(LOW)
        wait(loads)
        q_t_ref, v_t_ref = d_att_t_ref, d_q_t_ref

        @pl.loop(0, n_seq)
        def _(i):
            source = pick([jnp.where(i == 0, z, 0) for z in range(n_seq)])
            for j in range(1, n_seq):
                source = source + jnp.where(i == j, pick([near[j] for near in nearest]), 0)

            @pl.when(i == 0)
            def _():
                tokens_in[1].wait()

            @pl.when(i > 0)
            def _():
                arrived = x_ref.at[block(source), :]
                remote(
                    arrived, arrived, send_sems.at[TOKENS], token_sems.at[source], at.z_peer(source)
                ).wait_recv()

            @pl.when(i == n_seq - 1)
            def _():
                begin(cot_in)

            rows = block(source)
            inputs = x_ref[rows, :].astype(F32)
            hidden = (inputs * inverse_rms(inputs) * gain_one_ref[...]).astype(LOW)
            for tile in range(width // 256):
                cols = slice(256 * tile, 256 * tile + 256)
                q, k, v = [dot(hidden, ref[:, cols]) for ref in (wq_ref, wk_ref, wv_ref)]
                q_t_ref[cols, rows] = q.T.astype(LOW)
                k_t_ref[cols, rows] = k.T.astype(LOW)
                v_t_ref[cols, rows] = v.T.astype(LOW)
                for b in range(2):
                    lanes = slice(128 * b, 128 * b + 128)
                    q_ref[2 * tile + b, rows, :] = q[:, lanes].astype(LOW)
                    k_ref[2 * tile + b, rows, :] = k[:, lanes].astype(LOW)
                    v_ref[2 * tile + b, rows, :] = v[:, lanes].astype(LOW)

        start(weight_loads(0, 0))
        score_refs = (acc_ref, resid_ref)

        def put_scores(pair, b):
            rows = pl.ds(pl.multiple_of((2 * pair + b) * head_dim, head_dim), head_dim)
            keys = jnp.concatenate([k_ref[pair], key_seg_ref[...]], axis=1)
            q_t = jnp.concatenate([zero_padded(q_t_ref[rows, :], b), query_seg_ref[...]], axis=0)

            def half_of(half):
                cols = slice(256 * half, 256 * half + 256)
                score_refs[b][:, cols] = dot(keys, q_t[:, cols])

            return half_of

        def put_attended(pair, b, slot):
            h = 2 * pair + b
            rows = pl.ds(pl.multiple_of(h * head_dim, head_dim), head_dim)
            v_t = v_t_ref[rows, :]

            def half_of(half):
                cols = slice(256 * half, 256 * half + 256)
                bias = jnp.concatenate(
                    [
                        jnp.concatenate(
                            [bias_ref[h, kb - qb + blocks - 1] for qb in (2 * half, 2 * half + 1)], axis=1
                        )
                        for kb in range(blocks)
                    ],
                    axis=0,
                )
                scores = score_refs[b][:, cols] + bias
                powers = jnp.exp(scores - jnp.max(scores, axis=0, keepdims=True))
                inverse = 1.0 / jnp.sum(powers, axis=0, keepdims=True)
                probs = powers.astype(LOW)
                probs_ref[slot, b, :, cols] = probs
                attended_t_ref[rows, cols] = (dot(v_t, probs) * inverse).astype(LOW)
                inverse_ref[pl.ds(h, 1), cols] = inverse

            return half_of

        first = put_scores(0, 0)
        for half in range(2):
            first(half)

        @pl.loop(0, pairs)
        def _(pair):
            slot = lax.rem(pair, 2)

            @pl.when(pair >= 2)
            def _():
                probs_copy(pair - 2, slot, True).wait()

            for b in range(2):
                ahead = put_scores(pair, 1) if b == 0 else put_scores(jnp.minimum(pair + 1, pairs - 1), 0)
                now = put_attended(pair, b, slot)
                for half in range(2):
                    ahead(half)
                    now(half)
            probs_copy(pair, slot, True).start()

        output_load.wait()
        attended = attended_t_ref[...].T
        for tile in range(width // 256):
            cols = slice(256 * tile, 256 * tile + 256)
            resid_ref[:, cols] = x_ref[:, cols].astype(F32) + dot(attended, wo_ref[:, cols])

        @pl.loop(0, blocks)
        def _(i):
            resid = resid_ref[block(i), :]
            branch_ref[block(i), :] = (resid * inverse_rms(resid) * gain_two_ref[...]).astype(LOW)
            acc_ref[block(i), :] = resid

        for pair in (pairs - 2, pairs - 1):
            probs_copy(pair, pair % 2, True).wait()

        @pl.loop(0, tiles)
        def _(g):
            slot = lax.rem(g, 2)

            @pl.when(g >= 2)
            def _():
                slope_copy(g - 2, slot, True).wait()

            wait(weight_loads(g, slot))

            @pl.when(g < tiles - 1)
            def _():
                start(weight_loads(g + 1, 1 - slot))

            gates = [dot(branch_ref[...], wgu_ref[slot, :, 256 * i : 256 * i + 256]) for i in range(4)]
            activs = []
            for sub in range(2):
                gate, upper = gates[sub], gates[2 + sub]
                lanes = slice(256 * sub, 256 * sub + 256)
                square = gate * gate
                curve = jnp.tanh(0.7978845608028654 * gate * (1.0 + 0.044715 * square))
                gelu = 0.5 * gate * (1.0 + curve)
                slope = 0.5 * (1.0 + curve) + 0.5 * gate * (1.0 - curve * curve) * (
                    0.7978845608028654 * (1.0 + 3 * 0.044715 * square)
                )
                activ = gelu * upper
                probs_ref[slot, 0, :, lanes] = gelu.astype(LOW)
                probs_ref[slot, 1, :, lanes] = (upper * slope).astype(LOW)
                activ_t_ref[2 * g + sub] = activ.T.astype(LOW)
                activs.append(activ.astype(LOW))
            down = wd_ref[pl.ds(pl.multiple_of(slot * 512, 512), 512)]
            acc_ref[...] += dot(jnp.concatenate(activs, axis=1), down)

            @pl.when(g < tiles - 2)
            def _():
                slope_copy(g, slot, True).start()


        mixed_ref[...] = acc_ref[...].astype(LOW)

    pl.run_scoped(
        forward,
        bias_ref=VMEM((heads, 2 * blocks - 1, 128, 128), F32),
        key_seg_ref=VMEM((span, 128), LOW),
        query_seg_ref=VMEM((128, span), LOW),
    )
    arrive(COT, three_blocks, one_block)

    def backward(hidden_t_ref, d_att_ref, d_k_ref, d_v_ref, d_probs_ref):
        for s in range(GROUP):
            product = dot(activ_t_ref[s], cot_ref[...]).astype(LOW)
            for p in range(4):
                for i in range(width // 128):
                    ff_own[p, s % 2, s // 4, (s // 2) % 2, 64 * i : 64 * i + 64, :] = product[
                        64 * p : 64 * p + 64, 128 * i : 128 * i + 128
                    ]
        ff.stage0(0)
        ff.stage0(1)
        @pl.when((at.z == 0) | (at.z == n_seq - 1))
        def _():
            sent(COT, three_blocks)
            begin(mixed_back)


        def d_slot(g, k, lanes, half):
            n = 2 * lanes + half
            return att_own.at[2 * g + k, n // 4, (n // 2) % 2, n % 2, pl.ds(0, 256), :]

        def put_d_sides(g):
            slot = g % 2
            for sub in range(2):
                lanes = slice(256 * sub, 256 * sub + 256)
                d_act = dot_back(cot_ref[...], wd_ref[512 * slot + 256 * sub : 512 * slot + 256 * sub + 256, :])
                for k in range(2):
                    d_side = (d_act * probs_ref[slot, 1 - k, :, lanes].astype(F32)).astype(LOW)
                    for i in range(2):
                        for half in range(2):
                            d_slot(g, k, 2 * sub + i, half)[...] = d_side[
                                256 * half : 256 * half + 256, 128 * i : 128 * i + 128
                            ]

        def add_d_hidden(g, first):
            slot = g % 2
            d_both = jnp.concatenate(
                [
                    jnp.concatenate([d_slot(g, k, lanes, half)[...] for half in range(2)], axis=0)
                    for k in range(2)
                    for lanes in range(4)
                ],
                axis=1,
            )
            for tile in range(width // 256):
                cols = slice(256 * tile, 256 * tile + 256)
                term = dot_back(d_both, wgu_ref[slot, cols, :])
                acc_ref[:, cols] = term if first else acc_ref[:, cols] + term

        steps_back = list(range(tiles - 1, -1, -1))
        put_d_sides(steps_back[0])
        for i, g in enumerate(steps_back):
            if g >= 2:
                weight_loads(g - 2, g % 2)[0].start()
                slope_copy(g - 2, g % 2, False).start()
            if i >= 2:
                wait(weight_loads(g, g % 2)[1:])
            if g >= 1:
                if i >= 1:
                    weight_loads(g - 1, (g - 1) % 2)[0].wait()
                    slope_copy(g - 1, (g - 1) % 2, False).wait()
                put_d_sides(g - 1)
            rows = slice(128 * i, 128 * i + 128)
            resid = resid_ref[rows, :]
            hidden_t_ref[:, rows] = (resid * inverse_rms(resid) * gain_two_ref[...]).T.astype(LOW)
            add_d_hidden(g, i == 0)
            if g >= 2:
                start(weight_loads(g - 2, g % 2)[1:])
            if i <= 1:
                ff.stage1(i)
            if i == 0:

                @pl.when((at.z > 0) & (at.z < n_seq - 1))
                def _():
                    sent(COT, three_blocks)
                    begin(mixed_back)


        start(loads)
        probs_copy(0, 0, False).start()


        def product(g, k, sub):
            right = jnp.concatenate(
                [
                    jnp.concatenate([d_slot(g, k, 2 * sub + i, half)[...] for half in range(2)], axis=0)
                    for i in range(2)
                ],
                axis=1,
            )
            result = dot(hidden_t_ref[...], right).astype(LOW)
            for s in range(GROUP):
                for i in range(2):
                    place = shard * (2 * sub + i)
                    ff_own[4 + 2 * g + k, s % 2, s // 4, (s // 2) % 2, place : place + shard, :] = result[
                        shard * s : shard * s + shard, 128 * i : 128 * i + 128
                    ]

        def norm_back(grad_ref, vector_ref, gain_ref, extra_ref, out_ref, low_ref, row):
            total = jnp.zeros((1, width), F32)
            for i in range(blocks):
                rows = slice(128 * i, 128 * i + 128)
                vector = vector_ref[rows, :].astype(F32)
                scale = inverse_rms(vector)
                normed = vector * scale
                grad = grad_ref[rows, :]
                total = total + jnp.sum(grad * normed, axis=0, keepdims=True)
                inner = grad * gain_ref[...]
                result = extra_ref[rows, :].astype(F32) + scale * (
                    inner - normed * jnp.mean(inner * normed, -1, keepdims=True)
                )
                if out_ref is not None:
                    out_ref[rows, :] = result
                low_ref[rows, :] = result.astype(LOW)
            for i in range(width // 128):
                small_own[0, row + i : row + i + 1, :] = total[:, 128 * i : 128 * i + 128]

        norm_back(acc_ref, resid_ref, gain_two_ref, cot_ref, acc_ref, d_branch_ref, 12)

        def share(sums, j, left_t, right):
            for k in range(2):
                half = slice(width // 2 * k, width // 2 * k + width // 2)
                product = dot(left_t, right[:, half]).astype(LOW)
                for s in range(GROUP):
                    for i in range(width // 256):
                        sums.own[2 * j + k, s % 2, s // 4, (s // 2) % 2, shard * i : shard * i + shard, :] = product[
                            shard * s : shard * s + shard, 128 * i : 128 * i + 128
                        ]
            sums.stage0(j)

        for tile in range(width // 256):
            rows = slice(256 * tile, 256 * tile + 256)
            d_att_t = dot_back(d_branch_ref[...], wo_ref[rows, :]).T
            for i in range(256 // head_dim):
                h = 256 // head_dim * tile + i
                d_att_t_ref[head_dim * h : head_dim * (h + 1), :] = (
                    d_att_t[head_dim * i : head_dim * (i + 1), :] * inverse_ref[h : h + 1, :]
                ).astype(LOW)
            for i in range(2):
                d_att_ref[2 * tile + i] = d_att_t_ref[256 * tile + 128 * i : 256 * tile + 128 * i + 128, :].T
        left_half = lax.broadcasted_iota(jnp.int32, (span, 128), 1) < head_dim
        d_probs_refs = (resid_ref, d_probs_ref)

        def put_d_probs(pair, b):
            rows = pl.ds(pl.multiple_of((2 * pair + b) * head_dim, head_dim), head_dim)
            values = v_ref[pair]
            d_att_t = zero_padded(d_att_t_ref[rows, :], b)

            def half_of(half):
                cols = slice(256 * half, 256 * half + 256)
                d_probs_refs[b][:, cols] = dot(values, d_att_t[:, cols])

            return half_of

        across = lax.broadcasted_iota(jnp.int32, (8, 128), 1)

        def put_d_scores(pair, b, slot):
            h = 2 * pair + b
            rows = pl.ds(pl.multiple_of(h * head_dim, head_dim), head_dim)
            k_t = k_t_ref[rows, :]
            sums = [None] * (2 * blocks - 1)

            def half_of(half):
                cols = slice(256 * half, 256 * half + 256)
                d_probs = d_probs_refs[b][:, cols]
                probs = probs_ref[slot, b, :, cols].astype(F32)
                inner = jnp.sum(probs * d_probs, axis=0, keepdims=True) * inverse_ref[pl.ds(h, 1), cols]
                d_scores = probs * (d_probs - inner)
                for kb in range(blocks):
                    for i in range(2):
                        d = kb - (2 * half + i) + blocks - 1
                        part = d_scores[128 * kb : 128 * kb + 128, 128 * i : 128 * i + 128]
                        sums[d] = part if sums[d] is None else sums[d] + part
                d_scores = d_scores.astype(LOW)
                for i in range(2):
                    activ_t_ref[2 * b + i, :, cols] = d_scores[256 * i : 256 * i + 256, :]
                d_q_t_ref[rows, cols] = dot(k_t, d_scores).astype(LOW)
                if half == 1:
                    for d in range(2 * blocks - 1):
                        every, low_lanes = sums[d][:8, :], sums[d][:8, :]
                        for a in range(1, 16):
                            rolled = pltpu.roll(sums[d][8 * a : 8 * a + 8, :], 128 - 8 * a, 1)
                            every = every + rolled
                            low_lanes = low_lanes + jnp.where(across < 128 - 8 * a, rolled, 0.0)
                        diag_ref[h, d] = jnp.concatenate([low_lanes, every - low_lanes], axis=1)

            return half_of

        ff.stage2(0)
        first = put_d_probs(0, 0)
        for half in range(2):
            first(half)

        def attention_back(pair, with_products):
            slot = lax.rem(pair, 2)
            probs_copy(pair, slot, False).wait()

            @pl.when(pair < pairs - 1)
            def _():
                probs_copy(pair + 1, 1 - slot, False).start()

            for b in range(2):
                ahead = put_d_probs(pair, 1) if b == 0 else put_d_probs(jnp.minimum(pair + 1, pairs - 1), 0)
                now = put_d_scores(pair, b, slot)
                for half in range(2):
                    ahead(half)
                    if with_products:
                        product(pair, b, half)
                    now(half)
            lanes = pl.ds(pl.multiple_of(pair * 128, 128), 128)
            d_att, queries = d_att_ref[pair], q_ref[pair]
            blank = jnp.zeros_like(d_att)
            d_scores = [activ_t_ref[2 * b : 2 * b + 2].reshape(span, span) for b in range(2)]
            d_v_ref[:, lanes] = (
                dot(probs_ref[slot, 0], jnp.where(left_half, d_att, blank))
                + dot(probs_ref[slot, 1], jnp.where(left_half, blank, d_att))
            ).astype(LOW)
            d_k_ref[:, lanes] = (
                dot(d_scores[0], jnp.where(left_half, queries, blank))
                + dot(d_scores[1], jnp.where(left_half, blank, queries))
            ).astype(LOW)

        @pl.loop(0, tiles)
        def _(pair):
            attention_back(pair, True)
            ff.stage0(2 + pair)

            @pl.when(pair == 1)
            def _():
                ff.stage2(1)
                ff.stage1(2)
                ff.stage3(0)

            @pl.when(pair == 2)
            def _():
                ff.stage1(3)
                ff.stage3(1)

        @pl.loop(tiles, pairs)
        def _(pair):
            attention_back(pair, False)

            @pl.when(pair == tiles)
            def _():
                ff.hop(0, 1)

        ff.stage2(2)
        ff.stage1(4)
        branch_ref[...] = d_q_t_ref[...].T
        wait(loads)
        for tile in range(width // 256):
            rows = slice(256 * tile, 256 * tile + 256)
            resid_ref[:, rows] = (
                dot_back(branch_ref[...], wgu_ref[0, rows, :width])
                + dot_back(d_k_ref[...], wgu_ref[1, rows, :width])
                + dot_back(d_v_ref[...], wd_ref[rows, :])
            )
        ff.hop(1, 1)
        norm_back(resid_ref, x_ref, gain_one_ref, acc_ref, None, d_back_ref, 18)
        begin(tokens_back[0])
        ff.stage2(3)
        ff.stage1(5)
        ff.stage3(2)
        begin(tokens_back[1])
        share(att, 0, attended_t_ref[...], d_branch_ref[...])
        ff.hop(0, 2)

        @pl.loop(0, blocks)
        def _(i):
            inputs = x_ref[block(i), :].astype(F32)
            hidden_t_ref[:, block(i)] = (inputs * inverse_rms(inputs) * gain_one_ref[...]).T.astype(LOW)

        share(att, 1, hidden_t_ref[...], d_v_ref[...])
        share(att, 2, hidden_t_ref[...], d_k_ref[...])
        ff.stage2(4)
        att.stage1(0)
        share(att, 3, hidden_t_ref[...], branch_ref[...])
        ff.hop(2, 1)
        ff.hop(1, 2)
        begin(tokens_back[2])
        ff.stage3(3)

    pl.run_scoped(
        backward,
        hidden_t_ref=VMEM((width, span), LOW),
        d_att_ref=VMEM((pairs, span, 128), LOW),
        d_k_ref=VMEM((span, width), LOW),
        d_v_ref=VMEM((span, width), LOW),
        d_probs_ref=VMEM((span, span), F32),
    )

    flip = (
        lax.broadcasted_iota(jnp.int32, (256, 256), 0) + lax.broadcasted_iota(jnp.int32, (256, 256), 1) == 255
    ).astype(F32)

    @pl.loop(0, heads)
    def _(h):
        tiles_ = diag_ref[h].reshape(8 * (2 * blocks - 1), 256)
        flipped = jnp.dot(tiles_, flip, precision=lax.Precision.HIGHEST, preferred_element_type=F32)
        totals = [
            jnp.sum(pltpu.roll(flipped[8 * d : 8 * d + 8, :], 0, 1, stride=1, stride_axis=0), axis=0, keepdims=True)
            for d in range(2 * blocks - 1)
        ]
        pieces = [totals[0][:, 128:]]
        for d in range(1, 2 * blocks - 1):
            pieces.append(totals[d - 1][:, :128] + totals[d][:, 128:])
        pieces.append(totals[-1][:, :128])
        offset_ref[pl.ds(h, 1), :] = jnp.concatenate(pieces, axis=1)

    one_hot = (lax.broadcasted_iota(jnp.int32, (128, buckets_wide), 0) == bucket_ref[...]).astype(F32)
    small_own[0, :12, :] = lax.dot_general(
        offset_ref[:12, :], one_hot, (((1,), (1,)), ((), ())),
        precision=lax.Precision.HIGHEST, preferred_element_type=F32,
    )
    small_peers = [at.core_peer, at.x_peer, at.y_peer]
    steps = len(small_peers)

    def small_copy(i):
        return remote(small_own.at[i], small_got.at[i], small_sems.at[3], small_sems.at[i], small_peers[i])

    def small_row(i):
        return remote(
            small_own.at[steps], small_rows.at[at.z], small_sems.at[4], small_sems.at[5],
            at.z_peer(lax.rem(at.z + i, n_seq)),
        )

    def small_step(i):
        small_copy(i).wait_recv()
        small_own[i + 1] = small_own[i] + small_got[i]
        if i + 1 < steps:
            small_copy(i + 1).start()

    inner = (at.z > 0) & (at.z < n_seq - 1)
    small_copy(0).start()
    ff.stage2(5)
    att.stage1(1)
    ff.stage3(4)
    small_step(0)
    att.stage2(0)
    att.stage1(2)
    ff.hop(3, 1)
    begin(tokens_back[3])
    ff.stage3(5)
    ff.hop(2, 2)
    att.stage2(1)
    att.stage1(3)
    ff.hop(4, 1)
    ff.hop(3, 2)
    att.stage3(0)
    small_step(1)
    att.stage2(2)
    ff.hop(5, 1)
    ff.hop(4, 2)
    att.stage3(1)
    att.stage2(3)
    att.hop(0, 1)
    ff.hop(5, 2)
    small_step(2)
    small_rows[at.z] = small_own[steps]
    att.stage3(2)
    att.hop(1, 1)
    att.hop(0, 2)
    att.stage3(3)
    for i in range(1, n_seq):
        small_row(i).start()
    att.hop(2, 1)
    att.hop(1, 2)
    att.hop(3, 1)
    att.hop(2, 2)
    att.hop(3, 2)

    @pl.loop(0, FF_JOBS)
    def _(j):
        ff.finish(j, ff_out)

    @pl.loop(0, ATT_JOBS)
    def _(j):
        att.finish(j, att_out)


    three_rows = small_rows.at[pl.ds(0, n_seq - 1)]
    remote(three_rows, three_rows, small_sems.at[4], small_sems.at[5], at.core_peer).wait_recv()
    total = small_rows[0]
    for i in range(1, n_seq):
        total = total + small_rows[i]
    small_rows[0] = total
    small_store = pltpu.make_async_copy(small_rows.at[0], small_out, own_sems.at[5])
    small_store.start()
    ff.drain(ff_out)
    att.drain(att_out)
    three_steps = small_own.at[pl.ds(0, steps)]
    remote(three_steps, three_steps, small_sems.at[3], small_sems.at[0], at.core_peer).wait_send()
    remote(three_rows, three_rows, small_sems.at[4], small_sems.at[5], at.core_peer).wait_send()
    sent(SEGS, three_segs)
    for kind in (TOKENS, MIXED, BACK):
        sent(kind, three_blocks)
    for kind in (MIXED, BACK):
        arrive(kind, three_blocks, one_block)
    small_store.wait()


def layer(n_dp, n_seq, tokens, cot, seg, buckets, gain_one, gain_two, table, weights):
    width = tokens.shape[-1]
    span = tokens.shape[0] * tokens.shape[1]
    heads = table.shape[0]
    ff_width = weights[4].shape[1]
    ff_pieces, att_pieces = 2 * FF_JOBS, 2 * ATT_JOBS
    low = lambda *shape: VMEM(shape, LOW)
    dma = pltpu.SemaphoreType.DMA
    steps = 3

    def sums(pieces, rows):
        return [
            low(pieces, 2, 2, 2, rows, 128), low(pieces, 2, 2, rows, 128), low(pieces, 2, rows, 128),
            low(pieces, rows, 128), low(pieces, rows, 128), low(pieces, rows, 128),
            dma((5,)), dma((3, pieces // 2)), dma((2, pieces)), dma((1,)),
        ]

    pairs = low(heads // 2, span, 128)
    rows, turned = low(span, width), low(width, span)
    any_, vmem = pl.BlockSpec(memory_space=pl.ANY), pl.BlockSpec(memory_space=VMEM)
    result = lambda *shape: jax.ShapeDtypeStruct(shape, LOW)
    return pl.pallas_call(
        functools.partial(layer_kernel, n_dp, n_seq),
        out_shape=[
            result(n_seq, span // n_seq, width), result(n_seq, span // n_seq, width),
            result(ff_pieces, FF_ROWS, 128), result(att_pieces, ATT_ROWS, 128),
            jax.ShapeDtypeStruct((24, 128), F32),
            result(heads, span, span), result(ff_width // 512, 2, span, 512),
        ],
        in_specs=[any_] * 2 + [vmem] * 5 + [any_] * 7,
        out_specs=[any_] * 7,
        scratch_shapes=sums(ff_pieces, FF_ROWS)
        + sums(att_pieces, ATT_ROWS)
        + [
            VMEM((steps + 1, 24, 128), F32), VMEM((steps, 24, 128), F32), VMEM((n_seq, 24, 128), F32),
            dma((6,)),
        ]
        + [
            rows, rows, VMEM((n_seq, 8, 128), jnp.int32), VMEM((n_seq, 8, 128), jnp.int32), rows,
            low(width, width), low(2, width, 1024), low(1024, width), low(2, 2, span, span), VMEM((16, span), F32),
            low(ff_width // 256, 256, span), turned, pairs, pairs, pairs, turned, VMEM((span, width), F32),
            VMEM((span, width), F32), rows, rows, turned, turned, VMEM((16, 1024), F32),
            VMEM((heads, 2 * (span // 128) - 1, 8, 256), F32),
            VMEM((1, 1024), jnp.int32), VMEM((1, width), F32), VMEM((1, width), F32),
            dma((4,)), dma((3, 2)), dma((2,)), dma((5,)), dma((5,)), dma((n_seq,)), dma((6,)),
        ],
        compiler_params=pltpu.CompilerParams(
            collective_id=0, has_side_effects=True, vmem_limit_bytes=VMEM_BYTES
        ),
        name="layer",
    )(tokens, cot, seg, buckets, gain_one, gain_two, table, *weights)


def outputs_kernel(
    n_dp, mixed_ref, tokens_ref, ff_ref, att_ref, small_ref,
    mixed_out, tokens_out, gn_one_out, gq_out, gk_out, gv_out, go_out, table_out, gn_two_out, gg_out, gu_out, gd_out,
    mixed_in, tokens_in, ff_in, att_in, small_in, gn_one, gq, gk, gv, go, table, gn_two, gg, gu, gd, tokens, sems,
):
    copies = [
        pltpu.make_async_copy(src, dst, sems.at[i])
        for i, (src, dst) in enumerate(
            [(small_ref, small_in), (tokens_ref, tokens_in), (ff_ref, ff_in), (att_ref, att_in), (mixed_ref, mixed_in)]
        )
    ]
    for copy in copies:
        copy.start()
    stores = []

    def store(src, dst):
        stores.append(pltpu.make_async_copy(src, dst, sems.at[len(copies) + len(stores)]))
        stores[-1].start()

    width = mixed_ref.shape[-1]
    shard = width // GROUP
    copies[0].wait()
    table[...] = small_in[: table.shape[0], : table.shape[1]]
    store(table, table_out)
    mine = lax.axis_index("dp") // (n_dp // GROUP)
    for row, part, out in ((12, gn_two, gn_two_out), (18, gn_one, gn_one_out)):
        gains = jnp.concatenate([small_in[row + i : row + i + 1, :] for i in range(width // 128)], axis=1)
        total = jnp.zeros((1, shard), F32)
        for s in range(GROUP):
            total = total + jnp.where(mine == s, gains[:, shard * s : shard * s + shard], 0.0)
        part[...] = total
        store(part, out)
    copies[1].wait()
    tokens[...] = tokens_in[...].astype(F32)
    store(tokens, tokens_out)
    copies[2].wait()
    for k, (part, out) in enumerate(((gg, gg_out), (gu, gu_out))):
        for g in range(4):
            for i in range(4):
                col = 512 * g + 128 * i
                part[:, col : col + 128] = ff_in[4 + 2 * g + k, shard * i : shard * i + shard, :].astype(F32)
        store(part, out)
    for p in range(4):
        for i in range(width // 128):
            gd[64 * p : 64 * p + 64, 128 * i : 128 * i + 128] = ff_in[p, 64 * i : 64 * i + 64, :].astype(F32)
    store(gd, gd_out)
    copies[3].wait()
    for j, (part, out) in enumerate(((go, go_out), (gv, gv_out), (gk, gk_out), (gq, gq_out))):
        for k in range(2):
            for i in range(width // 256):
                col = width // 2 * k + 128 * i
                part[:, col : col + 128] = att_in[2 * j + k, shard * i : shard * i + shard, :].astype(F32)
        store(part, out)
    copies[4].wait()
    store(mixed_in, mixed_out)
    for copy in stores:
        copy.wait()


def outputs(n_dp, buckets, heads, mixed, tokens, ff, att, small):
    width = mixed.shape[-1]
    shard = width // GROUP
    full = lambda *shape: jax.ShapeDtypeStruct(shape, F32)
    square, wide = full(shard, width), full(shard, 2048)
    results = [
        jax.ShapeDtypeStruct(mixed.shape, LOW), full(*tokens.shape), full(1, shard), square, square, square, square,
        full(heads, buckets), full(1, shard), wide, wide, full(256, width),
    ]
    any_ = pl.BlockSpec(memory_space=pl.ANY)
    return pl.pallas_call(
        functools.partial(outputs_kernel, n_dp),
        out_shape=results,
        in_specs=[any_] * 5,
        out_specs=[any_] * len(results),
        scratch_shapes=[VMEM(a.shape, a.dtype) for a in [mixed, tokens, ff, att, small] + results[2:] + results[1:2]]
        + [pltpu.SemaphoreType.DMA((5 + len(results),))],
        compiler_params=pltpu.CompilerParams(vmem_limit_bytes=VMEM_BYTES),
        name="outputs",
    )(mixed, tokens, ff, att, small)


def solution(mesh):
    n_dp, n_seq = mesh.shape["dp"], mesh.shape["seq"]

    def on_device(
        tokens, segments, offset_buckets, norm_attn, w_query, w_key, w_value, w_output, bias_table,
        norm_ff, w_gate, w_up, w_down, cotangent,
    ):
        weights = (w_query, w_key, w_value, w_output, w_gate, w_up, w_down)
        sums = layer(
            n_dp, n_seq, tokens, cotangent, segments, offset_buckets, norm_attn, norm_ff, bias_table.T, weights
        )[:5]
        results = list(outputs(n_dp, bias_table.shape[0], bias_table.shape[1], *sums))
        results[2], results[7], results[8] = results[2].reshape(-1), results[7].T, results[8].reshape(-1)
        rest = n_dp // GROUP
        if rest > 1:
            groups = [[i * rest + j for j in range(rest)] for i in range(GROUP)]
            for i in (2, 3, 4, 5, 6, 8, 9, 10, 11):
                results[i] = lax.psum_scatter(
                    results[i], "dp", scatter_dimension=0, axis_index_groups=groups, tiled=True
                )
            results[7] = lax.psum(results[7], "dp", axis_index_groups=groups)
        return tuple(results)

    rows, shares = P("dp", "seq", None), P("dp", None)
    return jax.shard_map(
        on_device,
        mesh=mesh,
        in_specs=(rows, P("dp", "seq")) + (P(),) * 11 + (rows,),
        out_specs=(rows, rows, P("dp"), shares, shares, shares, shares, P(), P("dp"), shares, shares, shares),
        check_vma=False,
    )
```

```python
import functools

import jax
import jax.numpy as jnp
from jax import lax
from jax.experimental import pallas as pl
from jax.experimental.pallas import tpu as pltpu
from jax.sharding import PartitionSpec as P

MESH = pl.DeviceIdType.MESH
VMEM = pltpu.VMEM
LOW = jnp.bfloat16
F32 = jnp.float32
EPSILON = 1e-06
MASKED = -1e30
GROUP = 8
VMEM_BYTES = 63 * 2**20


def dot(left, right):
    return jnp.dot(left, right, preferred_element_type=F32)


def dot_back(left, right):
    return lax.dot_general(left, right, (((1,), (1,)), ((), ())), preferred_element_type=F32)


def inverse_rms(values):
    return lax.rsqrt(jnp.mean(values * values, -1, keepdims=True) + EPSILON)


def zero_padded(block, half):
    blank = jnp.zeros_like(block)
    return jnp.concatenate([blank, block] if half else [block, blank], axis=0)


class Place:
    def __init__(self, n_dp, n_seq):
        stride = n_dp // GROUP
        dp = lax.axis_index("dp")
        z = lax.axis_index("seq")
        index = dp // stride
        self.n_seq = n_seq
        self.core, self.x, self.y, self.z = index % 2, (index // 2) % 2, index // 4, z
        self.dp = dp
        self.core_peer = (dp + stride * (1 - 2 * self.core), z)
        self.x_peer = (dp + 2 * stride * (1 - 2 * self.x), z)
        self.y_peer = (dp + 4 * stride * (1 - 2 * self.y), z)

    def z_peer(self, z):
        return (self.dp, z)

    def z_pair(self, bit):
        return (self.dp, self.z + bit * (1 - 2 * ((self.z // bit) % 2)))


def remote(src, dst, send_sem, recv_sem, peer):
    return pltpu.make_async_remote_copy(
        src_ref=src, dst_ref=dst, send_sem=send_sem, recv_sem=recv_sem, device_id=peer, device_id_type=MESH
    )


class Sums:
    def __init__(self, place, own, got0, got1, got2, low_z, high_z, send_sems, recv_sems, z_sems, out_sem):
        self.place, self.own = place, own
        self.got0, self.got1, self.got2, self.low_z, self.high_z = got0, got1, got2, low_z, high_z
        self.send_sems, self.recv_sems, self.z_sems, self.out_sem = send_sems, recv_sems, z_sems, out_sem

    def arrived(self, stage, j):
        got = (self.got0, self.got1, self.got2)[stage].at[pl.ds(2 * j, 2)]
        remote(got, got, self.send_sems.at[stage], self.recv_sems.at[stage, j], self.place.core_peer).wait_recv()

    def send0(self, j, k):
        at, p = self.place, 2 * j + k
        remote(
            self.own.at[p, 1 - at.core], self.got0.at[p], self.send_sems.at[0], self.recv_sems.at[0, j], at.core_peer
        ).start()

    def send1(self, j, k):
        at, p = self.place, 2 * j + k
        mine = self.own.at[p, at.core]
        src = mine.at[1 - at.y] if k else mine.at[:, 1 - at.x]
        remote(
            src, self.got1.at[p], self.send_sems.at[1], self.recv_sems.at[1, j], at.y_peer if k else at.x_peer
        ).start()

    def send2(self, j, k):
        at, p = self.place, 2 * j + k
        mine = self.own.at[p, at.core]
        src = mine.at[at.y, 1 - at.x] if k else mine.at[1 - at.y, at.x]
        remote(
            src, self.got2.at[p], self.send_sems.at[2], self.recv_sems.at[2, j], at.x_peer if k else at.y_peer
        ).start()

    def kept(self, p):
        at = self.place
        return self.own.at[p, at.core, at.y, at.x]

    def up(self, p, first):
        src = self.kept(p) if first else self.got2.at[p]
        return remote(
            src, self.low_z.at[p], self.send_sems.at[3], self.z_sems.at[0, p], self.place.z_peer(lax.rem(self.place.z + 1, self.place.n_seq))
        )

    def down(self, p, first):
        src = self.kept(p) if first else self.got1.at[p, 0]
        return remote(
            src, self.high_z.at[p], self.send_sems.at[4], self.z_sems.at[1, p], self.place.z_peer(lax.rem(self.place.z + self.place.n_seq - 1, self.place.n_seq))
        )

    def stage0(self, j):
        for k in range(2):
            self.send0(j, k)

    def stage1(self, j):
        at = self.place
        self.arrived(0, j)
        for k in range(2):
            p = 2 * j + k
            for a in range(2):
                for b in range(2):
                    self.own[p, at.core, a, b] = self.own[p, at.core, a, b] + self.got0[p, a, b]
            self.send1(j, k)

    def stage2(self, j):
        at = self.place
        self.arrived(1, j)
        for k in range(2):
            p = 2 * j + k
            for a in range(2):
                if k:
                    self.own[p, at.core, at.y, a] = self.own[p, at.core, at.y, a] + self.got1[p, a]
                else:
                    self.own[p, at.core, a, at.x] = self.own[p, at.core, a, at.x] + self.got1[p, a]
            self.send2(j, k)

    def stage3(self, j):
        at = self.place
        self.arrived(2, j)
        for k in range(2):
            p = 2 * j + k
            self.own[p, at.core, at.y, at.x] = self.own[p, at.core, at.y, at.x] + self.got2[p]
        self.hop(j, 0)

    def hop(self, j, step):
        at = self.place
        last = at.n_seq - 1

        @pl.when(at.z == step)
        def _():
            for k in range(2):
                p = 2 * j + k
                if step:
                    self.up(p, False).wait_recv()
                    self.got2[p] = self.low_z[p] + self.own[p, at.core, at.y, at.x]
                self.up(p, step == 0).start()

        @pl.when(at.z == last - step)
        def _():
            for k in range(2):
                p = 2 * j + k
                if step:
                    self.down(p, False).wait_recv()
                    self.got1[p, 0] = self.high_z[p] + self.own[p, at.core, at.y, at.x]
                self.down(p, step == 0).start()

    def finish(self, j, out):
        at = self.place
        last = at.n_seq - 1
        for k in range(2):
            p = 2 * j + k

            @pl.when(at.z == last)
            def _():
                self.up(p, False).wait_recv()
                self.low_z[p] = self.low_z[p] + self.own[p, at.core, at.y, at.x]

            @pl.when(at.z == 0)
            def _():
                self.down(p, False).wait_recv()
                self.low_z[p] = self.high_z[p] + self.own[p, at.core, at.y, at.x]

            @pl.when((at.z > 0) & (at.z < last))
            def _():
                total = self.low_z[p].astype(F32) + self.high_z[p].astype(F32)
                self.low_z[p] = (total + self.own[p, at.core, at.y, at.x].astype(F32)).astype(LOW)

            pltpu.make_async_copy(self.low_z.at[p], out.at[p], self.out_sem.at[0]).start()

    def drain(self, out):
        at = self.place
        last = at.n_seq - 1

        def sent(stage, all_pieces):
            remote(
                all_pieces, all_pieces, self.send_sems.at[stage], self.recv_sems.at[0, 0], at.core_peer
            ).wait_send()

        for stage, got in enumerate((self.got0, self.got1, self.got2)):
            sent(stage, got)

        @pl.when(at.z < last)
        def _():
            sent(3, self.low_z)

        @pl.when(at.z > 0)
        def _():
            sent(4, self.high_z)

        pltpu.make_async_copy(self.low_z, out, self.out_sem.at[0]).wait()


FF_JOBS, ATT_JOBS = 6, 4
FF_ROWS, ATT_ROWS = 384, 288


def layer_kernel(
    n_dp, n_seq,
    tokens_hbm, cot_hbm, seg_ref, bucket_row, gain_one_row, gain_two_row, table_ref,
    wq_hbm, wk_hbm, wv_hbm, wo_hbm, wg_hbm, wu_hbm, wd_hbm,
    mixed_out, tokens_out, ff_out, att_out, small_out, probs_hbm, slope_hbm,
    ff_own, ff_got0, ff_got1, ff_got2, ff_low, ff_high, ff_sends, ff_recvs, ff_z_recvs, ff_out_sem,
    att_own, att_got0, att_got1, att_got2, att_low, att_high, att_sends, att_recvs, att_z_recvs, att_out_sem,
    small_own, small_got, small_rows, small_sems,
    x_ref, cot_ref, seg_send_ref, seg_rows_ref, mixed_ref,
    wo_ref, wgu_ref, wd_ref, probs_ref, inverse_ref,
    activ_t_ref, attended_t_ref, q_ref, k_ref, v_ref, k_t_ref, resid_ref, acc_ref, branch_ref, d_branch_ref,
    d_att_t_ref, d_q_t_ref, offset_ref, diag_ref, bucket_ref, gain_one_ref, gain_two_ref,
    load_sems, ff_load_sems, probs_sems, send_sems, recv_sems, token_sems, own_sems,
):
    span, width = x_ref.shape
    heads, buckets = table_ref.shape
    buckets_wide = bucket_ref.shape[1]
    head_dim = width // heads
    blocks = span // 128
    pairs = heads // 2
    tiles = wg_hbm.shape[1] // 512
    shard = width // GROUP
    at = Place(n_dp, n_seq)
    d_back_ref = cot_ref

    wq_ref, wk_ref, wv_ref = wgu_ref.at[0, :, pl.ds(0, width)], wgu_ref.at[1, :, pl.ds(0, width)], wd_ref.at[pl.ds(0, width)]
    loads = [
        pltpu.make_async_copy(src, dst, load_sems.at[i])
        for i, (src, dst) in enumerate([(wq_hbm, wq_ref), (wk_hbm, wk_ref), (wv_hbm, wv_ref)])
    ]
    output_load = pltpu.make_async_copy(wo_hbm, wo_ref, load_sems.at[3])

    def weight_loads(g, slot):
        cols = pl.ds(pl.multiple_of(g * 512, 512), 512)
        sides = [
            (wd_hbm.at[cols, :], wd_ref.at[pl.ds(pl.multiple_of(slot * 512, 512), 512)]),
            (wg_hbm.at[:, cols], wgu_ref.at[slot, :, pl.ds(0, 512)]),
            (wu_hbm.at[:, cols], wgu_ref.at[slot, :, pl.ds(512, 512)]),
        ]
        return [pltpu.make_async_copy(src, dst, ff_load_sems.at[i, slot]) for i, (src, dst) in enumerate(sides)]

    def slope_copy(g, slot, store):
        sides = (slope_hbm.at[g], probs_ref.at[slot])
        return pltpu.make_async_copy(*(sides[::-1] if store else sides), probs_sems.at[slot])

    def probs_copy(pair, slot, store):
        sides = (probs_hbm.at[pl.ds(2 * pair, 2)], probs_ref.at[slot])
        return pltpu.make_async_copy(*(sides[::-1] if store else sides), probs_sems.at[slot])

    def start(copies):
        for copy in copies:
            copy.start()

    def wait(copies):
        for copy in copies:
            copy.wait()

    barrier = pltpu.get_barrier_semaphore()
    peers = [at.core_peer, at.x_peer, at.y_peer] + [
        at.z_peer(lax.rem(at.z + i, n_seq)) for i in range(1, n_seq)
    ]
    for peer in peers:
        pl.semaphore_signal(barrier, inc=1, device_id=peer, device_id_type=MESH)
    start(loads)
    output_load.start()
    for i in range(n_seq):
        seg_send_ref[i] = jnp.broadcast_to(seg_ref[i : i + 1, :], (8, 128))

    pl.semaphore_wait(barrier, len(peers))

    ff = Sums(
        at, ff_own, ff_got0, ff_got1, ff_got2, ff_low, ff_high, ff_sends, ff_recvs, ff_z_recvs, ff_out_sem
    )
    att = Sums(
        at, att_own, att_got0, att_got1, att_got2, att_low, att_high, att_sends, att_recvs, att_z_recvs, att_out_sem
    )

    def block(z):
        return pl.ds(pl.multiple_of(z * 128, 128), 128)

    def pick(values):
        return sum(jnp.where(at.z == z, value, 0) for z, value in enumerate(values))

    nearest = [sorted(range(n_seq), key=lambda other: abs(other - z)) for z in range(n_seq)]

    def exchange(kind, src, dst, recv_of=None):
        sends = []
        for i in range(n_seq - 1):
            to = pick([near[i + 1] for near in nearest])
            recv = recv_sems.at[kind] if recv_of is None else recv_of.at[at.z]
            sends.append(remote(src(to), dst(at.z), send_sems.at[kind], recv, at.z_peer(to)))
        return sends, pltpu.make_async_copy(src(at.z), dst(at.z), own_sems.at[kind])

    def begin(exchanged):
        sends, own = exchanged
        start(sends)
        own.start()

    def arrive(kind, others, one):
        remote(others, others, send_sems.at[kind], recv_sems.at[kind], at.core_peer).wait_recv()
        pltpu.make_async_copy(one, one, own_sems.at[kind]).wait()

    def sent(kind, others):
        remote(others, others, send_sems.at[kind], recv_sems.at[kind], at.core_peer).wait_send()

    SEGS, TOKENS, COT, MIXED, BACK = range(5)
    segs = exchange(SEGS, lambda z: seg_send_ref.at[z], lambda z: seg_rows_ref.at[z])
    tokens_in = exchange(TOKENS, lambda z: tokens_hbm.at[z], lambda z: x_ref.at[block(z), :], token_sems)
    cot_in = exchange(COT, lambda z: cot_hbm.at[z], lambda z: cot_ref.at[block(z), :])
    mixed_back = exchange(MIXED, lambda z: mixed_ref.at[block(z), :], lambda z: mixed_out.at[z])
    tokens_back = [
        exchange(
            BACK,
            lambda z, part=part: d_back_ref.at[pl.ds(pl.multiple_of(z * 128 + 32 * part, 32), 32), :],
            lambda z, part=part: tokens_out.at[z, pl.ds(32 * part, 32), :],
        )
        for part in range(4)
    ]
    three_segs, one_seg = seg_rows_ref.at[pl.ds(0, n_seq - 1)], seg_rows_ref.at[0]
    three_blocks, one_block = x_ref.at[pl.ds(0, 128 * (n_seq - 1)), :], x_ref.at[pl.ds(0, 128), :]
    begin(segs)
    bucket_ref[...] = jnp.zeros_like(bucket_ref)
    bucket_ref[:, : bucket_row.shape[0]] = bucket_row[...].reshape(1, -1)
    gain_one_ref[...] = gain_one_row[...].reshape(1, -1)
    gain_two_ref[...] = gain_two_row[...].reshape(1, -1)
    begin(tokens_in)
    def forward(bias_ref, key_seg_ref, query_seg_ref):
        one_hot = (lax.broadcasted_iota(jnp.int32, (buckets, buckets_wide), 0) == bucket_ref[...]).astype(F32)
        offset_ref[:heads, :] = lax.dot_general(
            table_ref[...], one_hot, (((1,), (0,)), ((), ())),
            precision=lax.Precision.HIGHEST, preferred_element_type=F32,
        )

        @pl.loop(0, heads)
        def _(h):
            row = offset_ref[pl.ds(h, 1), :]
            for d in range(2 * blocks - 1):
                window = jnp.broadcast_to(row[:, 128 * d : 128 * d + 256], (128, 256))
                bias_ref[h, d] = pltpu.roll(window, 129, 1, stride=1, stride_axis=0)[:, :128].T

        arrive(SEGS, three_segs, one_seg)
        seg_rows = [seg_rows_ref[i, 0:1, :].astype(F32) for i in range(blocks)]
        for i in range(blocks):
            column = jnp.broadcast_to(seg_rows[i], (128, 128)).T
            across = lax.broadcasted_iota(jnp.int32, (128, 128), 1).astype(F32)
            along = lax.broadcasted_iota(jnp.int32, (128, 128), 0).astype(F32)
            key_seg_ref[128 * i : 128 * i + 128, :] = jnp.where(column == across, 1.0, 0.0).astype(LOW)
            query_seg_ref[:, 128 * i : 128 * i + 128] = jnp.where(seg_rows[i] == along, 0.0, MASKED).astype(LOW)
        wait(loads)
        q_t_ref, v_t_ref = d_att_t_ref, d_q_t_ref

        @pl.loop(0, n_seq)
        def _(i):
            source = pick([jnp.where(i == 0, z, 0) for z in range(n_seq)])
            for j in range(1, n_seq):
                source = source + jnp.where(i == j, pick([near[j] for near in nearest]), 0)

            @pl.when(i == 0)
            def _():
                tokens_in[1].wait()

            @pl.when(i > 0)
            def _():
                arrived = x_ref.at[block(source), :]
                remote(
                    arrived, arrived, send_sems.at[TOKENS], token_sems.at[source], at.z_peer(source)
                ).wait_recv()

            @pl.when(i == n_seq - 1)
            def _():
                begin(cot_in)

            rows = block(source)
            inputs = x_ref[rows, :].astype(F32)
            hidden = (inputs * inverse_rms(inputs) * gain_one_ref[...]).astype(LOW)
            for tile in range(width // 256):
                cols = slice(256 * tile, 256 * tile + 256)
                q, k, v = [dot(hidden, ref[:, cols]) for ref in (wq_ref, wk_ref, wv_ref)]
                q_t_ref[cols, rows] = q.T.astype(LOW)
                k_t_ref[cols, rows] = k.T.astype(LOW)
                v_t_ref[cols, rows] = v.T.astype(LOW)
                for b in range(2):
                    lanes = slice(128 * b, 128 * b + 128)
                    q_ref[2 * tile + b, rows, :] = q[:, lanes].astype(LOW)
                    k_ref[2 * tile + b, rows, :] = k[:, lanes].astype(LOW)
                    v_ref[2 * tile + b, rows, :] = v[:, lanes].astype(LOW)

        start(weight_loads(0, 0))
        score_refs = (acc_ref, resid_ref)

        def put_scores(pair, b):
            rows = pl.ds(pl.multiple_of((2 * pair + b) * head_dim, head_dim), head_dim)
            keys = jnp.concatenate([k_ref[pair], key_seg_ref[...]], axis=1)
            q_t = jnp.concatenate([zero_padded(q_t_ref[rows, :], b), query_seg_ref[...]], axis=0)

            def half_of(half):
                cols = slice(256 * half, 256 * half + 256)
                score_refs[b][:, cols] = dot(keys, q_t[:, cols])

            return half_of

        def put_attended(pair, b, slot):
            h = 2 * pair + b
            rows = pl.ds(pl.multiple_of(h * head_dim, head_dim), head_dim)
            v_t = v_t_ref[rows, :]

            def half_of(half):
                cols = slice(256 * half, 256 * half + 256)
                bias = jnp.concatenate(
                    [
                        jnp.concatenate(
                            [bias_ref[h, kb - qb + blocks - 1] for qb in (2 * half, 2 * half + 1)], axis=1
                        )
                        for kb in range(blocks)
                    ],
                    axis=0,
                )
                scores = score_refs[b][:, cols] + bias
                powers = jnp.exp(scores - jnp.max(scores, axis=0, keepdims=True))
                inverse = 1.0 / jnp.sum(powers, axis=0, keepdims=True)
                probs = powers.astype(LOW)
                probs_ref[slot, b, :, cols] = probs
                attended_t_ref[rows, cols] = (dot(v_t, probs) * inverse).astype(LOW)
                inverse_ref[pl.ds(h, 1), cols] = inverse

            return half_of

        first = put_scores(0, 0)
        for half in range(2):
            first(half)

        @pl.loop(0, pairs)
        def _(pair):
            slot = lax.rem(pair, 2)

            @pl.when(pair >= 2)
            def _():
                probs_copy(pair - 2, slot, True).wait()

            for b in range(2):
                ahead = put_scores(pair, 1) if b == 0 else put_scores(jnp.minimum(pair + 1, pairs - 1), 0)
                now = put_attended(pair, b, slot)
                for half in range(2):
                    ahead(half)
                    now(half)
            probs_copy(pair, slot, True).start()

        output_load.wait()
        attended = attended_t_ref[...].T
        for tile in range(width // 256):
            cols = slice(256 * tile, 256 * tile + 256)
            resid_ref[:, cols] = x_ref[:, cols].astype(F32) + dot(attended, wo_ref[:, cols])

        @pl.loop(0, blocks)
        def _(i):
            resid = resid_ref[block(i), :]
            branch_ref[block(i), :] = (resid * inverse_rms(resid) * gain_two_ref[...]).astype(LOW)
            acc_ref[block(i), :] = resid

        for pair in (pairs - 2, pairs - 1):
            probs_copy(pair, pair % 2, True).wait()

        @pl.loop(0, tiles)
        def _(g):
            slot = lax.rem(g, 2)

            @pl.when(g >= 2)
            def _():
                slope_copy(g - 2, slot, True).wait()

            wait(weight_loads(g, slot))

            @pl.when(g < tiles - 1)
            def _():
                start(weight_loads(g + 1, 1 - slot))

            gates = [dot(branch_ref[...], wgu_ref[slot, :, 256 * i : 256 * i + 256]) for i in range(4)]
            activs = []
            for sub in range(2):
                gate, upper = gates[sub], gates[2 + sub]
                lanes = slice(256 * sub, 256 * sub + 256)
                square = gate * gate
                curve = jnp.tanh(0.7978845608028654 * gate * (1.0 + 0.044715 * square))
                gelu = 0.5 * gate * (1.0 + curve)
                slope = 0.5 * (1.0 + curve) + 0.5 * gate * (1.0 - curve * curve) * (
                    0.7978845608028654 * (1.0 + 3 * 0.044715 * square)
                )
                activ = gelu * upper
                probs_ref[slot, 0, :, lanes] = gelu.astype(LOW)
                probs_ref[slot, 1, :, lanes] = (upper * slope).astype(LOW)
                activ_t_ref[2 * g + sub] = activ.T.astype(LOW)
                activs.append(activ.astype(LOW))
            down = wd_ref[pl.ds(pl.multiple_of(slot * 512, 512), 512)]
            acc_ref[...] += dot(jnp.concatenate(activs, axis=1), down)

            @pl.when(g < tiles - 2)
            def _():
                slope_copy(g, slot, True).start()


        mixed_ref[...] = acc_ref[...].astype(LOW)

    pl.run_scoped(
        forward,
        bias_ref=VMEM((heads, 2 * blocks - 1, 128, 128), F32),
        key_seg_ref=VMEM((span, 128), LOW),
        query_seg_ref=VMEM((128, span), LOW),
    )
    arrive(COT, three_blocks, one_block)

    def backward(hidden_t_ref, d_att_ref, d_k_ref, d_v_ref, d_probs_ref):
        for s in range(GROUP):
            product = dot(activ_t_ref[s], cot_ref[...]).astype(LOW)
            for p in range(4):
                for i in range(width // 128):
                    ff_own[p, s % 2, s // 4, (s // 2) % 2, 64 * i : 64 * i + 64, :] = product[
                        64 * p : 64 * p + 64, 128 * i : 128 * i + 128
                    ]
        ff.stage0(0)
        ff.stage0(1)
        @pl.when((at.z == 0) | (at.z == n_seq - 1))
        def _():
            sent(COT, three_blocks)
            begin(mixed_back)


        def d_slot(g, k, lanes, half):
            n = 2 * lanes + half
            return att_own.at[2 * g + k, n // 4, (n // 2) % 2, n % 2, pl.ds(0, 256), :]

        def put_d_sides(g):
            slot = g % 2
            for sub in range(2):
                lanes = slice(256 * sub, 256 * sub + 256)
                d_act = dot_back(cot_ref[...], wd_ref[512 * slot + 256 * sub : 512 * slot + 256 * sub + 256, :])
                for k in range(2):
                    d_side = (d_act * probs_ref[slot, 1 - k, :, lanes].astype(F32)).astype(LOW)
                    for i in range(2):
                        for half in range(2):
                            d_slot(g, k, 2 * sub + i, half)[...] = d_side[
                                256 * half : 256 * half + 256, 128 * i : 128 * i + 128
                            ]

        def add_d_hidden(g, first):
            slot = g % 2
            d_both = jnp.concatenate(
                [
                    jnp.concatenate([d_slot(g, k, lanes, half)[...] for half in range(2)], axis=0)
                    for k in range(2)
                    for lanes in range(4)
                ],
                axis=1,
            )
            for tile in range(width // 256):
                cols = slice(256 * tile, 256 * tile + 256)
                term = dot_back(d_both, wgu_ref[slot, cols, :])
                acc_ref[:, cols] = term if first else acc_ref[:, cols] + term

        steps_back = list(range(tiles - 1, -1, -1))
        put_d_sides(steps_back[0])
        for i, g in enumerate(steps_back):
            if g >= 2:
                weight_loads(g - 2, g % 2)[0].start()
                slope_copy(g - 2, g % 2, False).start()
            if i >= 2:
                wait(weight_loads(g, g % 2)[1:])
            if g >= 1:
                if i >= 1:
                    weight_loads(g - 1, (g - 1) % 2)[0].wait()
                    slope_copy(g - 1, (g - 1) % 2, False).wait()
                put_d_sides(g - 1)
            rows = slice(128 * i, 128 * i + 128)
            resid = resid_ref[rows, :]
            hidden_t_ref[:, rows] = (resid * inverse_rms(resid) * gain_two_ref[...]).T.astype(LOW)
            add_d_hidden(g, i == 0)
            if g >= 2:
                start(weight_loads(g - 2, g % 2)[1:])
            if i <= 1:
                ff.stage1(i)
            if i == 0:

                @pl.when((at.z > 0) & (at.z < n_seq - 1))
                def _():
                    sent(COT, three_blocks)
                    begin(mixed_back)


        start(loads)
        probs_copy(0, 0, False).start()


        def product(g, k, sub):
            right = jnp.concatenate(
                [
                    jnp.concatenate([d_slot(g, k, 2 * sub + i, half)[...] for half in range(2)], axis=0)
                    for i in range(2)
                ],
                axis=1,
            )
            result = dot(hidden_t_ref[...], right).astype(LOW)
            for s in range(GROUP):
                for i in range(2):
                    place = shard * (2 * sub + i)
                    ff_own[4 + 2 * g + k, s % 2, s // 4, (s // 2) % 2, place : place + shard, :] = result[
                        shard * s : shard * s + shard, 128 * i : 128 * i + 128
                    ]

        def norm_back(grad_ref, vector_ref, gain_ref, extra_ref, out_ref, low_ref, row):
            total = jnp.zeros((1, width), F32)
            for i in range(blocks):
                rows = slice(128 * i, 128 * i + 128)
                vector = vector_ref[rows, :].astype(F32)
                scale = inverse_rms(vector)
                normed = vector * scale
                grad = grad_ref[rows, :]
                total = total + jnp.sum(grad * normed, axis=0, keepdims=True)
                inner = grad * gain_ref[...]
                result = extra_ref[rows, :].astype(F32) + scale * (
                    inner - normed * jnp.mean(inner * normed, -1, keepdims=True)
                )
                if out_ref is not None:
                    out_ref[rows, :] = result
                low_ref[rows, :] = result.astype(LOW)
            for i in range(width // 128):
                small_own[0, row + i : row + i + 1, :] = total[:, 128 * i : 128 * i + 128]

        norm_back(acc_ref, resid_ref, gain_two_ref, cot_ref, acc_ref, d_branch_ref, 12)

        def share(sums, j, left_t, right):
            for k in range(2):
                half = slice(width // 2 * k, width // 2 * k + width // 2)
                product = dot(left_t, right[:, half]).astype(LOW)
                for s in range(GROUP):
                    for i in range(width // 256):
                        sums.own[2 * j + k, s % 2, s // 4, (s // 2) % 2, shard * i : shard * i + shard, :] = product[
                            shard * s : shard * s + shard, 128 * i : 128 * i + 128
                        ]
            sums.stage0(j)

        for tile in range(width // 256):
            rows = slice(256 * tile, 256 * tile + 256)
            d_att_t = dot_back(d_branch_ref[...], wo_ref[rows, :]).T
            for i in range(256 // head_dim):
                h = 256 // head_dim * tile + i
                d_att_t_ref[head_dim * h : head_dim * (h + 1), :] = (
                    d_att_t[head_dim * i : head_dim * (i + 1), :] * inverse_ref[h : h + 1, :]
                ).astype(LOW)
            for i in range(2):
                d_att_ref[2 * tile + i] = d_att_t_ref[256 * tile + 128 * i : 256 * tile + 128 * i + 128, :].T
        left_half = lax.broadcasted_iota(jnp.int32, (span, 128), 1) < head_dim
        d_probs_refs = (resid_ref, d_probs_ref)

        def put_d_probs(pair, b):
            rows = pl.ds(pl.multiple_of((2 * pair + b) * head_dim, head_dim), head_dim)
            values = v_ref[pair]
            d_att_t = zero_padded(d_att_t_ref[rows, :], b)

            def half_of(half):
                cols = slice(256 * half, 256 * half + 256)
                d_probs_refs[b][:, cols] = dot(values, d_att_t[:, cols])

            return half_of

        across = lax.broadcasted_iota(jnp.int32, (8, 128), 1)

        def put_d_scores(pair, b, slot):
            h = 2 * pair + b
            rows = pl.ds(pl.multiple_of(h * head_dim, head_dim), head_dim)
            k_t = k_t_ref[rows, :]
            sums = [None] * (2 * blocks - 1)

            def half_of(half):
                cols = slice(256 * half, 256 * half + 256)
                d_probs = d_probs_refs[b][:, cols]
                probs = probs_ref[slot, b, :, cols].astype(F32)
                inner = jnp.sum(probs * d_probs, axis=0, keepdims=True) * inverse_ref[pl.ds(h, 1), cols]
                d_scores = probs * (d_probs - inner)
                for kb in range(blocks):
                    for i in range(2):
                        d = kb - (2 * half + i) + blocks - 1
                        part = d_scores[128 * kb : 128 * kb + 128, 128 * i : 128 * i + 128]
                        sums[d] = part if sums[d] is None else sums[d] + part
                d_scores = d_scores.astype(LOW)
                for i in range(2):
                    activ_t_ref[2 * b + i, :, cols] = d_scores[256 * i : 256 * i + 256, :]
                d_q_t_ref[rows, cols] = dot(k_t, d_scores).astype(LOW)
                if half == 1:
                    for d in range(2 * blocks - 1):
                        every, low_lanes = sums[d][:8, :], sums[d][:8, :]
                        for a in range(1, 16):
                            rolled = pltpu.roll(sums[d][8 * a : 8 * a + 8, :], 128 - 8 * a, 1)
                            every = every + rolled
                            low_lanes = low_lanes + jnp.where(across < 128 - 8 * a, rolled, 0.0)
                        diag_ref[h, d] = jnp.concatenate([low_lanes, every - low_lanes], axis=1)

            return half_of

        ff.stage2(0)
        first = put_d_probs(0, 0)
        for half in range(2):
            first(half)

        def attention_back(pair, with_products):
            slot = lax.rem(pair, 2)
            probs_copy(pair, slot, False).wait()

            @pl.when(pair < pairs - 1)
            def _():
                probs_copy(pair + 1, 1 - slot, False).start()

            for b in range(2):
                ahead = put_d_probs(pair, 1) if b == 0 else put_d_probs(jnp.minimum(pair + 1, pairs - 1), 0)
                now = put_d_scores(pair, b, slot)
                for half in range(2):
                    ahead(half)
                    if with_products:
                        product(pair, b, half)
                    now(half)
            lanes = pl.ds(pl.multiple_of(pair * 128, 128), 128)
            d_att, queries = d_att_ref[pair], q_ref[pair]
            blank = jnp.zeros_like(d_att)
            d_scores = [activ_t_ref[2 * b : 2 * b + 2].reshape(span, span) for b in range(2)]
            d_v_ref[:, lanes] = (
                dot(probs_ref[slot, 0], jnp.where(left_half, d_att, blank))
                + dot(probs_ref[slot, 1], jnp.where(left_half, blank, d_att))
            ).astype(LOW)
            d_k_ref[:, lanes] = (
                dot(d_scores[0], jnp.where(left_half, queries, blank))
                + dot(d_scores[1], jnp.where(left_half, blank, queries))
            ).astype(LOW)

        @pl.loop(0, tiles)
        def _(pair):
            attention_back(pair, True)
            ff.stage0(2 + pair)

            @pl.when(pair == 1)
            def _():
                ff.stage2(1)
                ff.stage1(2)
                ff.stage3(0)

            @pl.when(pair == 2)
            def _():
                ff.stage1(3)
                ff.stage3(1)

        @pl.loop(tiles, pairs)
        def _(pair):
            attention_back(pair, False)

            @pl.when(pair == tiles)
            def _():
                ff.hop(0, 1)

        ff.stage2(2)
        ff.stage1(4)
        branch_ref[...] = d_q_t_ref[...].T
        wait(loads)
        for tile in range(width // 256):
            rows = slice(256 * tile, 256 * tile + 256)
            resid_ref[:, rows] = (
                dot_back(branch_ref[...], wgu_ref[0, rows, :width])
                + dot_back(d_k_ref[...], wgu_ref[1, rows, :width])
                + dot_back(d_v_ref[...], wd_ref[rows, :])
            )
        ff.hop(1, 1)
        norm_back(resid_ref, x_ref, gain_one_ref, acc_ref, None, d_back_ref, 18)
        begin(tokens_back[0])
        ff.stage2(3)
        ff.stage1(5)
        ff.stage3(2)
        begin(tokens_back[1])
        share(att, 0, attended_t_ref[...], d_branch_ref[...])
        ff.hop(0, 2)

        @pl.loop(0, blocks)
        def _(i):
            inputs = x_ref[block(i), :].astype(F32)
            hidden_t_ref[:, block(i)] = (inputs * inverse_rms(inputs) * gain_one_ref[...]).T.astype(LOW)

        share(att, 1, hidden_t_ref[...], d_v_ref[...])
        share(att, 2, hidden_t_ref[...], d_k_ref[...])
        ff.stage2(4)
        att.stage1(0)
        share(att, 3, hidden_t_ref[...], branch_ref[...])
        ff.hop(2, 1)
        ff.hop(1, 2)
        begin(tokens_back[2])
        ff.stage3(3)

    pl.run_scoped(
        backward,
        hidden_t_ref=VMEM((width, span), LOW),
        d_att_ref=VMEM((pairs, span, 128), LOW),
        d_k_ref=VMEM((span, width), LOW),
        d_v_ref=VMEM((span, width), LOW),
        d_probs_ref=VMEM((span, span), F32),
    )

    flip = (
        lax.broadcasted_iota(jnp.int32, (256, 256), 0) + lax.broadcasted_iota(jnp.int32, (256, 256), 1) == 255
    ).astype(F32)

    @pl.loop(0, heads)
    def _(h):
        tiles_ = diag_ref[h].reshape(8 * (2 * blocks - 1), 256)
        flipped = jnp.dot(tiles_, flip, precision=lax.Precision.HIGHEST, preferred_element_type=F32)
        totals = [
            jnp.sum(pltpu.roll(flipped[8 * d : 8 * d + 8, :], 0, 1, stride=1, stride_axis=0), axis=0, keepdims=True)
            for d in range(2 * blocks - 1)
        ]
        pieces = [totals[0][:, 128:]]
        for d in range(1, 2 * blocks - 1):
            pieces.append(totals[d - 1][:, :128] + totals[d][:, 128:])
        pieces.append(totals[-1][:, :128])
        offset_ref[pl.ds(h, 1), :] = jnp.concatenate(pieces, axis=1)

    one_hot = (lax.broadcasted_iota(jnp.int32, (128, buckets_wide), 0) == bucket_ref[...]).astype(F32)
    small_own[0, :12, :] = lax.dot_general(
        offset_ref[:12, :], one_hot, (((1,), (1,)), ((), ())),
        precision=lax.Precision.HIGHEST, preferred_element_type=F32,
    )
    small_peers = [at.core_peer, at.x_peer, at.y_peer]
    steps = len(small_peers)

    def small_copy(i):
        return remote(small_own.at[i], small_got.at[i], small_sems.at[3], small_sems.at[i], small_peers[i])

    def small_row(i):
        return remote(
            small_own.at[steps], small_rows.at[at.z], small_sems.at[4], small_sems.at[5],
            at.z_peer(lax.rem(at.z + i, n_seq)),
        )

    def small_step(i):
        small_copy(i).wait_recv()
        small_own[i + 1] = small_own[i] + small_got[i]
        if i + 1 < steps:
            small_copy(i + 1).start()

    inner = (at.z > 0) & (at.z < n_seq - 1)
    small_copy(0).start()
    ff.stage2(5)
    att.stage1(1)
    ff.stage3(4)
    small_step(0)
    att.stage2(0)
    att.stage1(2)
    ff.hop(3, 1)
    begin(tokens_back[3])
    ff.stage3(5)
    ff.hop(2, 2)
    att.stage2(1)
    att.stage1(3)
    ff.hop(4, 1)
    ff.hop(3, 2)
    att.stage3(0)
    small_step(1)
    att.stage2(2)
    ff.hop(5, 1)
    ff.hop(4, 2)
    att.stage3(1)
    att.stage2(3)
    att.hop(0, 1)
    ff.hop(5, 2)
    small_step(2)
    small_rows[at.z] = small_own[steps]
    att.stage3(2)
    att.hop(1, 1)
    att.hop(0, 2)
    att.stage3(3)
    for i in range(1, n_seq):
        small_row(i).start()
    att.hop(2, 1)
    att.hop(1, 2)
    att.hop(3, 1)
    att.hop(2, 2)
    att.hop(3, 2)

    @pl.loop(0, FF_JOBS)
    def _(j):
        ff.finish(j, ff_out)

    @pl.loop(0, ATT_JOBS)
    def _(j):
        att.finish(j, att_out)


    three_rows = small_rows.at[pl.ds(0, n_seq - 1)]
    remote(three_rows, three_rows, small_sems.at[4], small_sems.at[5], at.core_peer).wait_recv()
    total = small_rows[0]
    for i in range(1, n_seq):
        total = total + small_rows[i]
    small_rows[0] = total
    small_store = pltpu.make_async_copy(small_rows.at[0], small_out, own_sems.at[5])
    small_store.start()
    ff.drain(ff_out)
    att.drain(att_out)
    three_steps = small_own.at[pl.ds(0, steps)]
    remote(three_steps, three_steps, small_sems.at[3], small_sems.at[0], at.core_peer).wait_send()
    remote(three_rows, three_rows, small_sems.at[4], small_sems.at[5], at.core_peer).wait_send()
    sent(SEGS, three_segs)
    for kind in (TOKENS, MIXED, BACK):
        sent(kind, three_blocks)
    for kind in (MIXED, BACK):
        arrive(kind, three_blocks, one_block)
    small_store.wait()


def layer(n_dp, n_seq, tokens, cot, seg, buckets, gain_one, gain_two, table, weights):
    width = tokens.shape[-1]
    span = tokens.shape[0] * tokens.shape[1]
    heads = table.shape[0]
    ff_width = weights[4].shape[1]
    ff_pieces, att_pieces = 2 * FF_JOBS, 2 * ATT_JOBS
    low = lambda *shape: VMEM(shape, LOW)
    dma = pltpu.SemaphoreType.DMA
    steps = 3

    def sums(pieces, rows):
        return [
            low(pieces, 2, 2, 2, rows, 128), low(pieces, 2, 2, rows, 128), low(pieces, 2, rows, 128),
            low(pieces, rows, 128), low(pieces, rows, 128), low(pieces, rows, 128),
            dma((5,)), dma((3, pieces // 2)), dma((2, pieces)), dma((1,)),
        ]

    pairs = low(heads // 2, span, 128)
    rows, turned = low(span, width), low(width, span)
    any_, vmem = pl.BlockSpec(memory_space=pl.ANY), pl.BlockSpec(memory_space=VMEM)
    result = lambda *shape: jax.ShapeDtypeStruct(shape, LOW)
    return pl.pallas_call(
        functools.partial(layer_kernel, n_dp, n_seq),
        out_shape=[
            result(n_seq, span // n_seq, width), result(n_seq, span // n_seq, width),
            result(ff_pieces, FF_ROWS, 128), result(att_pieces, ATT_ROWS, 128),
            jax.ShapeDtypeStruct((24, 128), F32),
            result(heads, span, span), result(ff_width // 512, 2, span, 512),
        ],
        in_specs=[any_] * 2 + [vmem] * 5 + [any_] * 7,
        out_specs=[any_] * 7,
        scratch_shapes=sums(ff_pieces, FF_ROWS)
        + sums(att_pieces, ATT_ROWS)
        + [
            VMEM((steps + 1, 24, 128), F32), VMEM((steps, 24, 128), F32), VMEM((n_seq, 24, 128), F32),
            dma((6,)),
        ]
        + [
            rows, rows, VMEM((n_seq, 8, 128), jnp.int32), VMEM((n_seq, 8, 128), jnp.int32), rows,
            low(width, width), low(2, width, 1024), low(1024, width), low(2, 2, span, span), VMEM((16, span), F32),
            low(ff_width // 256, 256, span), turned, pairs, pairs, pairs, turned, VMEM((span, width), F32),
            VMEM((span, width), F32), rows, rows, turned, turned, VMEM((16, 1024), F32),
            VMEM((heads, 2 * (span // 128) - 1, 8, 256), F32),
            VMEM((1, 1024), jnp.int32), VMEM((1, width), F32), VMEM((1, width), F32),
            dma((4,)), dma((3, 2)), dma((2,)), dma((5,)), dma((5,)), dma((n_seq,)), dma((6,)),
        ],
        compiler_params=pltpu.CompilerParams(
            collective_id=0, has_side_effects=True, vmem_limit_bytes=VMEM_BYTES
        ),
        name="layer",
    )(tokens, cot, seg, buckets, gain_one, gain_two, table, *weights)


def outputs_kernel(
    n_dp, mixed_ref, tokens_ref, ff_ref, att_ref, small_ref,
    mixed_out, tokens_out, gn_one_out, gq_out, gk_out, gv_out, go_out, table_out, gn_two_out, gg_out, gu_out, gd_out,
    mixed_in, tokens_in, ff_in, att_in, small_in, gn_one, gq, gk, gv, go, table, gn_two, gg, gu, gd, tokens, sems,
):
    copies = [
        pltpu.make_async_copy(src, dst, sems.at[i])
        for i, (src, dst) in enumerate(
            [(small_ref, small_in), (tokens_ref, tokens_in), (ff_ref, ff_in), (att_ref, att_in), (mixed_ref, mixed_in)]
        )
    ]
    for copy in copies:
        copy.start()
    stores = []

    def store(src, dst):
        stores.append(pltpu.make_async_copy(src, dst, sems.at[len(copies) + len(stores)]))
        stores[-1].start()

    width = mixed_ref.shape[-1]
    shard = width // GROUP
    copies[0].wait()
    table[...] = small_in[: table.shape[0], : table.shape[1]]
    store(table, table_out)
    mine = lax.axis_index("dp") // (n_dp // GROUP)
    for row, part, out in ((12, gn_two, gn_two_out), (18, gn_one, gn_one_out)):
        gains = jnp.concatenate([small_in[row + i : row + i + 1, :] for i in range(width // 128)], axis=1)
        total = jnp.zeros((1, shard), F32)
        for s in range(GROUP):
            total = total + jnp.where(mine == s, gains[:, shard * s : shard * s + shard], 0.0)
        part[...] = total
        store(part, out)
    copies[1].wait()
    tokens[...] = tokens_in[...].astype(F32)
    store(tokens, tokens_out)
    copies[2].wait()
    for k, (part, out) in enumerate(((gg, gg_out), (gu, gu_out))):
        for g in range(4):
            for i in range(4):
                col = 512 * g + 128 * i
                part[:, col : col + 128] = ff_in[4 + 2 * g + k, shard * i : shard * i + shard, :].astype(F32)
        store(part, out)
    for p in range(4):
        for i in range(width // 128):
            gd[64 * p : 64 * p + 64, 128 * i : 128 * i + 128] = ff_in[p, 64 * i : 64 * i + 64, :].astype(F32)
    store(gd, gd_out)
    copies[3].wait()
    for j, (part, out) in enumerate(((go, go_out), (gv, gv_out), (gk, gk_out), (gq, gq_out))):
        for k in range(2):
            for i in range(width // 256):
                col = width // 2 * k + 128 * i
                part[:, col : col + 128] = att_in[2 * j + k, shard * i : shard * i + shard, :].astype(F32)
        store(part, out)
    copies[4].wait()
    store(mixed_in, mixed_out)
    for copy in stores:
        copy.wait()


def outputs(n_dp, buckets, heads, mixed, tokens, ff, att, small):
    width = mixed.shape[-1]
    shard = width // GROUP
    full = lambda *shape: jax.ShapeDtypeStruct(shape, F32)
    square, wide = full(shard, width), full(shard, 2048)
    results = [
        jax.ShapeDtypeStruct(mixed.shape, LOW), full(*tokens.shape), full(1, shard), square, square, square, square,
        full(heads, buckets), full(1, shard), wide, wide, full(256, width),
    ]
    any_ = pl.BlockSpec(memory_space=pl.ANY)
    return pl.pallas_call(
        functools.partial(outputs_kernel, n_dp),
        out_shape=results,
        in_specs=[any_] * 5,
        out_specs=[any_] * len(results),
        scratch_shapes=[VMEM(a.shape, a.dtype) for a in [mixed, tokens, ff, att, small] + results[2:] + results[1:2]]
        + [pltpu.SemaphoreType.DMA((5 + len(results),))],
        compiler_params=pltpu.CompilerParams(vmem_limit_bytes=VMEM_BYTES),
        name="outputs",
    )(mixed, tokens, ff, att, small)


def solution(mesh):
    n_dp, n_seq = mesh.shape["dp"], mesh.shape["seq"]

    def on_device(
        tokens, segments, offset_buckets, norm_attn, w_query, w_key, w_value, w_output, bias_table,
        norm_ff, w_gate, w_up, w_down, cotangent,
    ):
        weights = (w_query, w_key, w_value, w_output, w_gate, w_up, w_down)
        sums = layer(
            n_dp, n_seq, tokens, cotangent, segments, offset_buckets, norm_attn, norm_ff, bias_table.T, weights
        )[:5]
        results = list(outputs(n_dp, bias_table.shape[0], bias_table.shape[1], *sums))
        results[2], results[7], results[8] = results[2].reshape(-1), results[7].T, results[8].reshape(-1)
        rest = n_dp // GROUP
        if rest > 1:
            groups = [[i * rest + j for j in range(rest)] for i in range(GROUP)]
            for i in (2, 3, 4, 5, 6, 8, 9, 10, 11):
                results[i] = lax.psum_scatter(
                    results[i], "dp", scatter_dimension=0, axis_index_groups=groups, tiled=True
                )
            results[7] = lax.psum(results[7], "dp", axis_index_groups=groups)
        return tuple(results)

    rows, shares = P("dp", "seq", None), P("dp", None)
    return jax.shard_map(
        on_device,
        mesh=mesh,
        in_specs=(rows, P("dp", "seq")) + (P(),) * 11 + (rows,),
        out_specs=(rows, rows, P("dp"), shares, shares, shares, shares, P(), P("dp"), shares, shares, shares),
        check_vma=False,
    )
```

```python
import functools

import jax
import jax.numpy as jnp
from jax import lax
from jax.experimental import pallas as pl
from jax.experimental.pallas import tpu as pltpu
from jax.sharding import PartitionSpec as P

MESH = pl.DeviceIdType.MESH
VMEM = pltpu.VMEM
LOW = jnp.bfloat16
F32 = jnp.float32
EPSILON = 1e-06
MASKED = -1e30
GROUP = 8
VMEM_BYTES = 63 * 2**20


def dot(left, right):
    return jnp.dot(left, right, preferred_element_type=F32)


def dot_back(left, right):
    return lax.dot_general(left, right, (((1,), (1,)), ((), ())), preferred_element_type=F32)


def inverse_rms(values):
    return lax.rsqrt(jnp.mean(values * values, -1, keepdims=True) + EPSILON)


def zero_padded(block, half):
    blank = jnp.zeros_like(block)
    return jnp.concatenate([blank, block] if half else [block, blank], axis=0)


class Place:
    def __init__(self, n_dp, n_seq):
        stride = n_dp // GROUP
        dp = lax.axis_index("dp")
        z = lax.axis_index("seq")
        index = dp // stride
        self.n_seq = n_seq
        self.core, self.x, self.y, self.z = index % 2, (index // 2) % 2, index // 4, z
        self.dp = dp
        self.core_peer = (dp + stride * (1 - 2 * self.core), z)
        self.x_peer = (dp + 2 * stride * (1 - 2 * self.x), z)
        self.y_peer = (dp + 4 * stride * (1 - 2 * self.y), z)

    def z_peer(self, z):
        return (self.dp, z)

    def z_pair(self, bit):
        return (self.dp, self.z + bit * (1 - 2 * ((self.z // bit) % 2)))


def remote(src, dst, send_sem, recv_sem, peer):
    return pltpu.make_async_remote_copy(
        src_ref=src, dst_ref=dst, send_sem=send_sem, recv_sem=recv_sem, device_id=peer, device_id_type=MESH
    )


class Sums:
    def __init__(self, place, own, got0, got1, got2, low_z, high_z, send_sems, recv_sems, z_sems, out_sem):
        self.place, self.own = place, own
        self.got0, self.got1, self.got2, self.low_z, self.high_z = got0, got1, got2, low_z, high_z
        self.send_sems, self.recv_sems, self.z_sems, self.out_sem = send_sems, recv_sems, z_sems, out_sem

    def arrived(self, stage, j):
        got = (self.got0, self.got1, self.got2)[stage].at[pl.ds(2 * j, 2)]
        remote(got, got, self.send_sems.at[stage], self.recv_sems.at[stage, j], self.place.core_peer).wait_recv()

    def send0(self, j, k):
        at, p = self.place, 2 * j + k
        remote(
            self.own.at[p, 1 - at.core], self.got0.at[p], self.send_sems.at[0], self.recv_sems.at[0, j], at.core_peer
        ).start()

    def send1(self, j, k):
        at, p = self.place, 2 * j + k
        mine = self.own.at[p, at.core]
        src = mine.at[1 - at.y] if k else mine.at[:, 1 - at.x]
        remote(
            src, self.got1.at[p], self.send_sems.at[1], self.recv_sems.at[1, j], at.y_peer if k else at.x_peer
        ).start()

    def send2(self, j, k):
        at, p = self.place, 2 * j + k
        mine = self.own.at[p, at.core]
        src = mine.at[at.y, 1 - at.x] if k else mine.at[1 - at.y, at.x]
        remote(
            src, self.got2.at[p], self.send_sems.at[2], self.recv_sems.at[2, j], at.x_peer if k else at.y_peer
        ).start()

    def kept(self, p):
        at = self.place
        return self.own.at[p, at.core, at.y, at.x]

    def up(self, p, first):
        src = self.kept(p) if first else self.got2.at[p]
        return remote(
            src, self.low_z.at[p], self.send_sems.at[3], self.z_sems.at[0, p], self.place.z_peer(lax.rem(self.place.z + 1, self.place.n_seq))
        )

    def down(self, p, first):
        src = self.kept(p) if first else self.got1.at[p, 0]
        return remote(
            src, self.high_z.at[p], self.send_sems.at[4], self.z_sems.at[1, p], self.place.z_peer(lax.rem(self.place.z + self.place.n_seq - 1, self.place.n_seq))
        )

    def stage0(self, j):
        for k in range(2):
            self.send0(j, k)

    def stage1(self, j):
        at = self.place
        self.arrived(0, j)
        for k in range(2):
            p = 2 * j + k
            for a in range(2):
                for b in range(2):
                    self.own[p, at.core, a, b] = self.own[p, at.core, a, b] + self.got0[p, a, b]
            self.send1(j, k)

    def stage2(self, j):
        at = self.place
        self.arrived(1, j)
        for k in range(2):
            p = 2 * j + k
            for a in range(2):
                if k:
                    self.own[p, at.core, at.y, a] = self.own[p, at.core, at.y, a] + self.got1[p, a]
                else:
                    self.own[p, at.core, a, at.x] = self.own[p, at.core, a, at.x] + self.got1[p, a]
            self.send2(j, k)

    def stage3(self, j):
        at = self.place
        self.arrived(2, j)
        for k in range(2):
            p = 2 * j + k
            self.own[p, at.core, at.y, at.x] = self.own[p, at.core, at.y, at.x] + self.got2[p]
        self.hop(j, 0)

    def hop(self, j, step):
        at = self.place
        last = at.n_seq - 1

        @pl.when(at.z == step)
        def _():
            for k in range(2):
                p = 2 * j + k
                if step:
                    self.up(p, False).wait_recv()
                    self.got2[p] = self.low_z[p] + self.own[p, at.core, at.y, at.x]
                self.up(p, step == 0).start()

        @pl.when(at.z == last - step)
        def _():
            for k in range(2):
                p = 2 * j + k
                if step:
                    self.down(p, False).wait_recv()
                    self.got1[p, 0] = self.high_z[p] + self.own[p, at.core, at.y, at.x]
                self.down(p, step == 0).start()

    def finish(self, j, out):
        at = self.place
        last = at.n_seq - 1
        for k in range(2):
            p = 2 * j + k

            @pl.when(at.z == last)
            def _():
                self.up(p, False).wait_recv()
                self.low_z[p] = self.low_z[p] + self.own[p, at.core, at.y, at.x]

            @pl.when(at.z == 0)
            def _():
                self.down(p, False).wait_recv()
                self.low_z[p] = self.high_z[p] + self.own[p, at.core, at.y, at.x]

            @pl.when((at.z > 0) & (at.z < last))
            def _():
                total = self.low_z[p].astype(F32) + self.high_z[p].astype(F32)
                self.low_z[p] = (total + self.own[p, at.core, at.y, at.x].astype(F32)).astype(LOW)

            pltpu.make_async_copy(self.low_z.at[p], out.at[p], self.out_sem.at[0]).start()

    def drain(self, out):
        at = self.place
        last = at.n_seq - 1

        def sent(stage, all_pieces):
            remote(
                all_pieces, all_pieces, self.send_sems.at[stage], self.recv_sems.at[0, 0], at.core_peer
            ).wait_send()

        for stage, got in enumerate((self.got0, self.got1, self.got2)):
            sent(stage, got)

        @pl.when(at.z < last)
        def _():
            sent(3, self.low_z)

        @pl.when(at.z > 0)
        def _():
            sent(4, self.high_z)

        pltpu.make_async_copy(self.low_z, out, self.out_sem.at[0]).wait()


FF_JOBS, ATT_JOBS = 6, 4
FF_ROWS, ATT_ROWS = 384, 288


def layer_kernel(
    n_dp, n_seq,
    tokens_hbm, cot_hbm, seg_ref, bucket_row, gain_one_row, gain_two_row, table_ref,
    wq_hbm, wk_hbm, wv_hbm, wo_hbm, wg_hbm, wu_hbm, wd_hbm,
    mixed_out, tokens_out, ff_out, att_out, small_out, probs_hbm, slope_hbm,
    ff_own, ff_got0, ff_got1, ff_got2, ff_low, ff_high, ff_sends, ff_recvs, ff_z_recvs, ff_out_sem,
    att_own, att_got0, att_got1, att_got2, att_low, att_high, att_sends, att_recvs, att_z_recvs, att_out_sem,
    small_own, small_got, small_rows, small_sems,
    x_ref, cot_ref, seg_send_ref, seg_rows_ref, mixed_ref,
    wo_ref, wgu_ref, wd_ref, probs_ref, inverse_ref,
    activ_t_ref, attended_t_ref, q_ref, k_ref, v_ref, k_t_ref, resid_ref, acc_ref, branch_ref, d_branch_ref,
    d_att_t_ref, d_q_t_ref, offset_ref, diag_ref, bucket_ref, gain_one_ref, gain_two_ref,
    load_sems, ff_load_sems, probs_sems, send_sems, recv_sems, token_sems, own_sems,
):
    span, width = x_ref.shape
    heads, buckets = table_ref.shape
    buckets_wide = bucket_ref.shape[1]
    head_dim = width // heads
    blocks = span // 128
    pairs = heads // 2
    tiles = wg_hbm.shape[1] // 512
    shard = width // GROUP
    at = Place(n_dp, n_seq)
    d_back_ref = cot_ref

    wq_ref, wk_ref, wv_ref = wgu_ref.at[0, :, pl.ds(0, width)], wgu_ref.at[1, :, pl.ds(0, width)], wd_ref.at[pl.ds(0, width)]
    loads = [
        pltpu.make_async_copy(src, dst, load_sems.at[i])
        for i, (src, dst) in enumerate([(wq_hbm, wq_ref), (wk_hbm, wk_ref), (wv_hbm, wv_ref)])
    ]
    output_load = pltpu.make_async_copy(wo_hbm, wo_ref, load_sems.at[3])

    def weight_loads(g, slot):
        cols = pl.ds(pl.multiple_of(g * 512, 512), 512)
        sides = [
            (wd_hbm.at[cols, :], wd_ref.at[pl.ds(pl.multiple_of(slot * 512, 512), 512)]),
            (wg_hbm.at[:, cols], wgu_ref.at[slot, :, pl.ds(0, 512)]),
            (wu_hbm.at[:, cols], wgu_ref.at[slot, :, pl.ds(512, 512)]),
        ]
        return [pltpu.make_async_copy(src, dst, ff_load_sems.at[i, slot]) for i, (src, dst) in enumerate(sides)]

    def slope_copy(g, slot, store):
        sides = (slope_hbm.at[g], probs_ref.at[slot])
        return pltpu.make_async_copy(*(sides[::-1] if store else sides), probs_sems.at[slot])

    def probs_copy(pair, slot, store):
        sides = (probs_hbm.at[pl.ds(2 * pair, 2)], probs_ref.at[slot])
        return pltpu.make_async_copy(*(sides[::-1] if store else sides), probs_sems.at[slot])

    def start(copies):
        for copy in copies:
            copy.start()

    def wait(copies):
        for copy in copies:
            copy.wait()

    barrier = pltpu.get_barrier_semaphore()
    peers = [at.core_peer, at.x_peer, at.y_peer] + [
        at.z_peer(lax.rem(at.z + i, n_seq)) for i in range(1, n_seq)
    ]
    for peer in peers:
        pl.semaphore_signal(barrier, inc=1, device_id=peer, device_id_type=MESH)
    start(loads)
    output_load.start()
    for i in range(n_seq):
        seg_send_ref[i] = jnp.broadcast_to(seg_ref[i : i + 1, :], (8, 128))

    pl.semaphore_wait(barrier, len(peers))

    ff = Sums(
        at, ff_own, ff_got0, ff_got1, ff_got2, ff_low, ff_high, ff_sends, ff_recvs, ff_z_recvs, ff_out_sem
    )
    att = Sums(
        at, att_own, att_got0, att_got1, att_got2, att_low, att_high, att_sends, att_recvs, att_z_recvs, att_out_sem
    )

    def block(z):
        return pl.ds(pl.multiple_of(z * 128, 128), 128)

    def pick(values):
        return sum(jnp.where(at.z == z, value, 0) for z, value in enumerate(values))

    nearest = [sorted(range(n_seq), key=lambda other: abs(other - z)) for z in range(n_seq)]

    def exchange(kind, src, dst, recv_of=None):
        sends = []
        for i in range(n_seq - 1):
            to = pick([near[i + 1] for near in nearest])
            recv = recv_sems.at[kind] if recv_of is None else recv_of.at[at.z]
            sends.append(remote(src(to), dst(at.z), send_sems.at[kind], recv, at.z_peer(to)))
        return sends, pltpu.make_async_copy(src(at.z), dst(at.z), own_sems.at[kind])

    def begin(exchanged):
        sends, own = exchanged
        start(sends)
        own.start()

    def arrive(kind, others, one):
        remote(others, others, send_sems.at[kind], recv_sems.at[kind], at.core_peer).wait_recv()
        pltpu.make_async_copy(one, one, own_sems.at[kind]).wait()

    def sent(kind, others):
        remote(others, others, send_sems.at[kind], recv_sems.at[kind], at.core_peer).wait_send()

    SEGS, TOKENS, COT, MIXED, BACK = range(5)
    segs = exchange(SEGS, lambda z: seg_send_ref.at[z], lambda z: seg_rows_ref.at[z])
    tokens_in = exchange(TOKENS, lambda z: tokens_hbm.at[z], lambda z: x_ref.at[block(z), :], token_sems)
    cot_in = exchange(COT, lambda z: cot_hbm.at[z], lambda z: cot_ref.at[block(z), :])
    mixed_back = exchange(MIXED, lambda z: mixed_ref.at[block(z), :], lambda z: mixed_out.at[z])
    tokens_back = [
        exchange(
            BACK,
            lambda z, part=part: d_back_ref.at[pl.ds(pl.multiple_of(z * 128 + 32 * part, 32), 32), :],
            lambda z, part=part: tokens_out.at[z, pl.ds(32 * part, 32), :],
        )
        for part in range(4)
    ]
    three_segs, one_seg = seg_rows_ref.at[pl.ds(0, n_seq - 1)], seg_rows_ref.at[0]
    three_blocks, one_block = x_ref.at[pl.ds(0, 128 * (n_seq - 1)), :], x_ref.at[pl.ds(0, 128), :]
    begin(segs)
    bucket_ref[...] = jnp.zeros_like(bucket_ref)
    bucket_ref[:, : bucket_row.shape[0]] = bucket_row[...].reshape(1, -1)
    gain_one_ref[...] = gain_one_row[...].reshape(1, -1)
    gain_two_ref[...] = gain_two_row[...].reshape(1, -1)
    begin(tokens_in)
    def forward(bias_ref, key_seg_ref, query_seg_ref):
        one_hot = (lax.broadcasted_iota(jnp.int32, (buckets, buckets_wide), 0) == bucket_ref[...]).astype(F32)
        offset_ref[:heads, :] = lax.dot_general(
            table_ref[...], one_hot, (((1,), (0,)), ((), ())),
            precision=lax.Precision.HIGHEST, preferred_element_type=F32,
        )

        @pl.loop(0, heads)
        def _(h):
            row = offset_ref[pl.ds(h, 1), :]
            for d in range(2 * blocks - 1):
                window = jnp.broadcast_to(row[:, 128 * d : 128 * d + 256], (128, 256))
                bias_ref[h, d] = pltpu.roll(window, 129, 1, stride=1, stride_axis=0)[:, :128].T

        arrive(SEGS, three_segs, one_seg)
        seg_rows = [seg_rows_ref[i, 0:1, :].astype(F32) for i in range(blocks)]
        for i in range(blocks):
            column = jnp.broadcast_to(seg_rows[i], (128, 128)).T
            across = lax.broadcasted_iota(jnp.int32, (128, 128), 1).astype(F32)
            along = lax.broadcasted_iota(jnp.int32, (128, 128), 0).astype(F32)
            key_seg_ref[128 * i : 128 * i + 128, :] = jnp.where(column == across, 1.0, 0.0).astype(LOW)
            query_seg_ref[:, 128 * i : 128 * i + 128] = jnp.where(seg_rows[i] == along, 0.0, MASKED).astype(LOW)
        wait(loads)
        q_t_ref, v_t_ref = d_att_t_ref, d_q_t_ref

        @pl.loop(0, n_seq)
        def _(i):
            source = pick([jnp.where(i == 0, z, 0) for z in range(n_seq)])
            for j in range(1, n_seq):
                source = source + jnp.where(i == j, pick([near[j] for near in nearest]), 0)

            @pl.when(i == 0)
            def _():
                tokens_in[1].wait()

            @pl.when(i > 0)
            def _():
                arrived = x_ref.at[block(source), :]
                remote(
                    arrived, arrived, send_sems.at[TOKENS], token_sems.at[source], at.z_peer(source)
                ).wait_recv()

            @pl.when(i == n_seq - 1)
            def _():
                begin(cot_in)

            rows = block(source)
            inputs = x_ref[rows, :].astype(F32)
            hidden = (inputs * inverse_rms(inputs) * gain_one_ref[...]).astype(LOW)
            for tile in range(width // 256):
                cols = slice(256 * tile, 256 * tile + 256)
                q, k, v = [dot(hidden, ref[:, cols]) for ref in (wq_ref, wk_ref, wv_ref)]
                q_t_ref[cols, rows] = q.T.astype(LOW)
                k_t_ref[cols, rows] = k.T.astype(LOW)
                v_t_ref[cols, rows] = v.T.astype(LOW)
                for b in range(2):
                    lanes = slice(128 * b, 128 * b + 128)
                    q_ref[2 * tile + b, rows, :] = q[:, lanes].astype(LOW)
                    k_ref[2 * tile + b, rows, :] = k[:, lanes].astype(LOW)
                    v_ref[2 * tile + b, rows, :] = v[:, lanes].astype(LOW)

        start(weight_loads(0, 0))
        score_refs = (acc_ref, resid_ref)

        def put_scores(pair, b):
            rows = pl.ds(pl.multiple_of((2 * pair + b) * head_dim, head_dim), head_dim)
            keys = jnp.concatenate([k_ref[pair], key_seg_ref[...]], axis=1)
            q_t = jnp.concatenate([zero_padded(q_t_ref[rows, :], b), query_seg_ref[...]], axis=0)

            def half_of(half):
                cols = slice(256 * half, 256 * half + 256)
                score_refs[b][:, cols] = dot(keys, q_t[:, cols])

            return half_of

        def put_attended(pair, b, slot):
            h = 2 * pair + b
            rows = pl.ds(pl.multiple_of(h * head_dim, head_dim), head_dim)
            v_t = v_t_ref[rows, :]

            def half_of(half):
                cols = slice(256 * half, 256 * half + 256)
                bias = jnp.concatenate(
                    [
                        jnp.concatenate(
                            [bias_ref[h, kb - qb + blocks - 1] for qb in (2 * half, 2 * half + 1)], axis=1
                        )
                        for kb in range(blocks)
                    ],
                    axis=0,
                )
                scores = score_refs[b][:, cols] + bias
                powers = jnp.exp(scores - jnp.max(scores, axis=0, keepdims=True))
                inverse = 1.0 / jnp.sum(powers, axis=0, keepdims=True)
                probs = powers.astype(LOW)
                probs_ref[slot, b, :, cols] = probs
                attended_t_ref[rows, cols] = (dot(v_t, probs) * inverse).astype(LOW)
                inverse_ref[pl.ds(h, 1), cols] = inverse

            return half_of

        first = put_scores(0, 0)
        for half in range(2):
            first(half)

        @pl.loop(0, pairs)
        def _(pair):
            slot = lax.rem(pair, 2)

            @pl.when(pair >= 2)
            def _():
                probs_copy(pair - 2, slot, True).wait()

            for b in range(2):
                ahead = put_scores(pair, 1) if b == 0 else put_scores(jnp.minimum(pair + 1, pairs - 1), 0)
                now = put_attended(pair, b, slot)
                for half in range(2):
                    ahead(half)
                    now(half)
            probs_copy(pair, slot, True).start()

        output_load.wait()
        attended = attended_t_ref[...].T
        for tile in range(width // 256):
            cols = slice(256 * tile, 256 * tile + 256)
            resid_ref[:, cols] = x_ref[:, cols].astype(F32) + dot(attended, wo_ref[:, cols])

        @pl.loop(0, blocks)
        def _(i):
            resid = resid_ref[block(i), :]
            branch_ref[block(i), :] = (resid * inverse_rms(resid) * gain_two_ref[...]).astype(LOW)
            acc_ref[block(i), :] = resid

        for pair in (pairs - 2, pairs - 1):
            probs_copy(pair, pair % 2, True).wait()

        @pl.loop(0, tiles)
        def _(g):
            slot = lax.rem(g, 2)

            @pl.when(g >= 2)
            def _():
                slope_copy(g - 2, slot, True).wait()

            wait(weight_loads(g, slot))

            @pl.when(g < tiles - 1)
            def _():
                start(weight_loads(g + 1, 1 - slot))

            gates = [dot(branch_ref[...], wgu_ref[slot, :, 256 * i : 256 * i + 256]) for i in range(4)]
            activs = []
            for sub in range(2):
                gate, upper = gates[sub], gates[2 + sub]
                lanes = slice(256 * sub, 256 * sub + 256)
                square = gate * gate
                curve = jnp.tanh(0.7978845608028654 * gate * (1.0 + 0.044715 * square))
                gelu = 0.5 * gate * (1.0 + curve)
                slope = 0.5 * (1.0 + curve) + 0.5 * gate * (1.0 - curve * curve) * (
                    0.7978845608028654 * (1.0 + 3 * 0.044715 * square)
                )
                activ = gelu * upper
                probs_ref[slot, 0, :, lanes] = gelu.astype(LOW)
                probs_ref[slot, 1, :, lanes] = (upper * slope).astype(LOW)
                activ_t_ref[2 * g + sub] = activ.T.astype(LOW)
                activs.append(activ.astype(LOW))
            down = wd_ref[pl.ds(pl.multiple_of(slot * 512, 512), 512)]
            acc_ref[...] += dot(jnp.concatenate(activs, axis=1), down)

            @pl.when(g < tiles - 2)
            def _():
                slope_copy(g, slot, True).start()


        mixed_ref[...] = acc_ref[...].astype(LOW)

    pl.run_scoped(
        forward,
        bias_ref=VMEM((heads, 2 * blocks - 1, 128, 128), F32),
        key_seg_ref=VMEM((span, 128), LOW),
        query_seg_ref=VMEM((128, span), LOW),
    )
    arrive(COT, three_blocks, one_block)

    def backward(hidden_t_ref, d_att_ref, d_k_ref, d_v_ref, d_probs_ref):
        for s in range(GROUP):
            product = dot(activ_t_ref[s], cot_ref[...]).astype(LOW)
            for p in range(4):
                for i in range(width // 128):
                    ff_own[p, s % 2, s // 4, (s // 2) % 2, 64 * i : 64 * i + 64, :] = product[
                        64 * p : 64 * p + 64, 128 * i : 128 * i + 128
                    ]
        ff.stage0(0)
        ff.stage0(1)
        @pl.when((at.z == 0) | (at.z == n_seq - 1))
        def _():
            sent(COT, three_blocks)
            begin(mixed_back)


        def d_slot(g, k, lanes, half):
            n = 2 * lanes + half
            return att_own.at[2 * g + k, n // 4, (n // 2) % 2, n % 2, pl.ds(0, 256), :]

        def put_d_sides(g):
            slot = g % 2
            for sub in range(2):
                lanes = slice(256 * sub, 256 * sub + 256)
                d_act = dot_back(cot_ref[...], wd_ref[512 * slot + 256 * sub : 512 * slot + 256 * sub + 256, :])
                for k in range(2):
                    d_side = (d_act * probs_ref[slot, 1 - k, :, lanes].astype(F32)).astype(LOW)
                    for i in range(2):
                        for half in range(2):
                            d_slot(g, k, 2 * sub + i, half)[...] = d_side[
                                256 * half : 256 * half + 256, 128 * i : 128 * i + 128
                            ]

        def add_d_hidden(g, first):
            slot = g % 2
            d_both = jnp.concatenate(
                [
                    jnp.concatenate([d_slot(g, k, lanes, half)[...] for half in range(2)], axis=0)
                    for k in range(2)
                    for lanes in range(4)
                ],
                axis=1,
            )
            for tile in range(width // 256):
                cols = slice(256 * tile, 256 * tile + 256)
                term = dot_back(d_both, wgu_ref[slot, cols, :])
                acc_ref[:, cols] = term if first else acc_ref[:, cols] + term

        steps_back = list(range(tiles - 1, -1, -1))
        put_d_sides(steps_back[0])
        for i, g in enumerate(steps_back):
            if g >= 2:
                weight_loads(g - 2, g % 2)[0].start()
                slope_copy(g - 2, g % 2, False).start()
            if i >= 2:
                wait(weight_loads(g, g % 2)[1:])
            if g >= 1:
                if i >= 1:
                    weight_loads(g - 1, (g - 1) % 2)[0].wait()
                    slope_copy(g - 1, (g - 1) % 2, False).wait()
                put_d_sides(g - 1)
            rows = slice(128 * i, 128 * i + 128)
            resid = resid_ref[rows, :]
            hidden_t_ref[:, rows] = (resid * inverse_rms(resid) * gain_two_ref[...]).T.astype(LOW)
            add_d_hidden(g, i == 0)
            if g >= 2:
                start(weight_loads(g - 2, g % 2)[1:])
            if i <= 1:
                ff.stage1(i)
            if i == 0:

                @pl.when((at.z > 0) & (at.z < n_seq - 1))
                def _():
                    sent(COT, three_blocks)
                    begin(mixed_back)


        start(loads)
        probs_copy(0, 0, False).start()


        def product(g, k, sub):
            right = jnp.concatenate(
                [
                    jnp.concatenate([d_slot(g, k, 2 * sub + i, half)[...] for half in range(2)], axis=0)
                    for i in range(2)
                ],
                axis=1,
            )
            result = dot(hidden_t_ref[...], right).astype(LOW)
            for s in range(GROUP):
                for i in range(2):
                    place = shard * (2 * sub + i)
                    ff_own[4 + 2 * g + k, s % 2, s // 4, (s // 2) % 2, place : place + shard, :] = result[
                        shard * s : shard * s + shard, 128 * i : 128 * i + 128
                    ]

        def norm_back(grad_ref, vector_ref, gain_ref, extra_ref, out_ref, low_ref, row):
            total = jnp.zeros((1, width), F32)
            for i in range(blocks):
                rows = slice(128 * i, 128 * i + 128)
                vector = vector_ref[rows, :].astype(F32)
                scale = inverse_rms(vector)
                normed = vector * scale
                grad = grad_ref[rows, :]
                total = total + jnp.sum(grad * normed, axis=0, keepdims=True)
                inner = grad * gain_ref[...]
                result = extra_ref[rows, :].astype(F32) + scale * (
                    inner - normed * jnp.mean(inner * normed, -1, keepdims=True)
                )
                if out_ref is not None:
                    out_ref[rows, :] = result
                low_ref[rows, :] = result.astype(LOW)
            for i in range(width // 128):
                small_own[0, row + i : row + i + 1, :] = total[:, 128 * i : 128 * i + 128]

        norm_back(acc_ref, resid_ref, gain_two_ref, cot_ref, acc_ref, d_branch_ref, 12)

        def share(sums, j, left_t, right):
            for k in range(2):
                half = slice(width // 2 * k, width // 2 * k + width // 2)
                product = dot(left_t, right[:, half]).astype(LOW)
                for s in range(GROUP):
                    for i in range(width // 256):
                        sums.own[2 * j + k, s % 2, s // 4, (s // 2) % 2, shard * i : shard * i + shard, :] = product[
                            shard * s : shard * s + shard, 128 * i : 128 * i + 128
                        ]
            sums.stage0(j)

        for tile in range(width // 256):
            rows = slice(256 * tile, 256 * tile + 256)
            d_att_t = dot_back(d_branch_ref[...], wo_ref[rows, :]).T
            for i in range(256 // head_dim):
                h = 256 // head_dim * tile + i
                d_att_t_ref[head_dim * h : head_dim * (h + 1), :] = (
                    d_att_t[head_dim * i : head_dim * (i + 1), :] * inverse_ref[h : h + 1, :]
                ).astype(LOW)
            for i in range(2):
                d_att_ref[2 * tile + i] = d_att_t_ref[256 * tile + 128 * i : 256 * tile + 128 * i + 128, :].T
        left_half = lax.broadcasted_iota(jnp.int32, (span, 128), 1) < head_dim
        d_probs_refs = (resid_ref, d_probs_ref)

        def put_d_probs(pair, b):
            rows = pl.ds(pl.multiple_of((2 * pair + b) * head_dim, head_dim), head_dim)
            values = v_ref[pair]
            d_att_t = zero_padded(d_att_t_ref[rows, :], b)

            def half_of(half):
                cols = slice(256 * half, 256 * half + 256)
                d_probs_refs[b][:, cols] = dot(values, d_att_t[:, cols])

            return half_of

        across = lax.broadcasted_iota(jnp.int32, (8, 128), 1)

        def put_d_scores(pair, b, slot):
            h = 2 * pair + b
            rows = pl.ds(pl.multiple_of(h * head_dim, head_dim), head_dim)
            k_t = k_t_ref[rows, :]
            sums = [None] * (2 * blocks - 1)

            def half_of(half):
                cols = slice(256 * half, 256 * half + 256)
                d_probs = d_probs_refs[b][:, cols]
                probs = probs_ref[slot, b, :, cols].astype(F32)
                inner = jnp.sum(probs * d_probs, axis=0, keepdims=True) * inverse_ref[pl.ds(h, 1), cols]
                d_scores = probs * (d_probs - inner)
                for kb in range(blocks):
                    for i in range(2):
                        d = kb - (2 * half + i) + blocks - 1
                        part = d_scores[128 * kb : 128 * kb + 128, 128 * i : 128 * i + 128]
                        sums[d] = part if sums[d] is None else sums[d] + part
                d_scores = d_scores.astype(LOW)
                for i in range(2):
                    activ_t_ref[2 * b + i, :, cols] = d_scores[256 * i : 256 * i + 256, :]
                d_q_t_ref[rows, cols] = dot(k_t, d_scores).astype(LOW)
                if half == 1:
                    for d in range(2 * blocks - 1):
                        every, low_lanes = sums[d][:8, :], sums[d][:8, :]
                        for a in range(1, 16):
                            rolled = pltpu.roll(sums[d][8 * a : 8 * a + 8, :], 128 - 8 * a, 1)
                            every = every + rolled
                            low_lanes = low_lanes + jnp.where(across < 128 - 8 * a, rolled, 0.0)
                        diag_ref[h, d] = jnp.concatenate([low_lanes, every - low_lanes], axis=1)

            return half_of

        ff.stage2(0)
        first = put_d_probs(0, 0)
        for half in range(2):
            first(half)

        def attention_back(pair, with_products):
            slot = lax.rem(pair, 2)
            probs_copy(pair, slot, False).wait()

            @pl.when(pair < pairs - 1)
            def _():
                probs_copy(pair + 1, 1 - slot, False).start()

            for b in range(2):
                ahead = put_d_probs(pair, 1) if b == 0 else put_d_probs(jnp.minimum(pair + 1, pairs - 1), 0)
                now = put_d_scores(pair, b, slot)
                for half in range(2):
                    ahead(half)
                    if with_products:
                        product(pair, b, half)
                    now(half)
            lanes = pl.ds(pl.multiple_of(pair * 128, 128), 128)
            d_att, queries = d_att_ref[pair], q_ref[pair]
            blank = jnp.zeros_like(d_att)
            d_scores = [activ_t_ref[2 * b : 2 * b + 2].reshape(span, span) for b in range(2)]
            d_v_ref[:, lanes] = (
                dot(probs_ref[slot, 0], jnp.where(left_half, d_att, blank))
                + dot(probs_ref[slot, 1], jnp.where(left_half, blank, d_att))
            ).astype(LOW)
            d_k_ref[:, lanes] = (
                dot(d_scores[0], jnp.where(left_half, queries, blank))
                + dot(d_scores[1], jnp.where(left_half, blank, queries))
            ).astype(LOW)

        @pl.loop(0, tiles)
        def _(pair):
            attention_back(pair, True)
            ff.stage0(2 + pair)

            @pl.when(pair == 1)
            def _():
                ff.stage2(1)
                ff.stage1(2)
                ff.stage3(0)

            @pl.when(pair == 2)
            def _():
                ff.stage1(3)
                ff.stage3(1)

        @pl.loop(tiles, pairs)
        def _(pair):
            attention_back(pair, False)

            @pl.when(pair == tiles)
            def _():
                ff.hop(0, 1)

        ff.stage2(2)
        ff.stage1(4)
        branch_ref[...] = d_q_t_ref[...].T
        wait(loads)
        for tile in range(width // 256):
            rows = slice(256 * tile, 256 * tile + 256)
            resid_ref[:, rows] = (
                dot_back(branch_ref[...], wgu_ref[0, rows, :width])
                + dot_back(d_k_ref[...], wgu_ref[1, rows, :width])
                + dot_back(d_v_ref[...], wd_ref[rows, :])
            )
        ff.hop(1, 1)
        norm_back(resid_ref, x_ref, gain_one_ref, acc_ref, None, d_back_ref, 18)
        begin(tokens_back[0])
        ff.stage2(3)
        ff.stage1(5)
        ff.stage3(2)
        begin(tokens_back[1])
        share(att, 0, attended_t_ref[...], d_branch_ref[...])
        ff.hop(0, 2)

        @pl.loop(0, blocks)
        def _(i):
            inputs = x_ref[block(i), :].astype(F32)
            hidden_t_ref[:, block(i)] = (inputs * inverse_rms(inputs) * gain_one_ref[...]).T.astype(LOW)

        share(att, 1, hidden_t_ref[...], d_v_ref[...])
        share(att, 2, hidden_t_ref[...], d_k_ref[...])
        ff.stage2(4)
        att.stage1(0)
        share(att, 3, hidden_t_ref[...], branch_ref[...])
        ff.hop(2, 1)
        ff.hop(1, 2)
        begin(tokens_back[2])
        ff.stage3(3)

    pl.run_scoped(
        backward,
        hidden_t_ref=VMEM((width, span), LOW),
        d_att_ref=VMEM((pairs, span, 128), LOW),
        d_k_ref=VMEM((span, width), LOW),
        d_v_ref=VMEM((span, width), LOW),
        d_probs_ref=VMEM((span, span), F32),
    )

    flip = (
        lax.broadcasted_iota(jnp.int32, (256, 256), 0) + lax.broadcasted_iota(jnp.int32, (256, 256), 1) == 255
    ).astype(F32)

    @pl.loop(0, heads)
    def _(h):
        tiles_ = diag_ref[h].reshape(8 * (2 * blocks - 1), 256)
        flipped = jnp.dot(tiles_, flip, precision=lax.Precision.HIGHEST, preferred_element_type=F32)
        totals = [
            jnp.sum(pltpu.roll(flipped[8 * d : 8 * d + 8, :], 0, 1, stride=1, stride_axis=0), axis=0, keepdims=True)
            for d in range(2 * blocks - 1)
        ]
        pieces = [totals[0][:, 128:]]
        for d in range(1, 2 * blocks - 1):
            pieces.append(totals[d - 1][:, :128] + totals[d][:, 128:])
        pieces.append(totals[-1][:, :128])
        offset_ref[pl.ds(h, 1), :] = jnp.concatenate(pieces, axis=1)

    one_hot = (lax.broadcasted_iota(jnp.int32, (128, buckets_wide), 0) == bucket_ref[...]).astype(F32)
    small_own[0, :12, :] = lax.dot_general(
        offset_ref[:12, :], one_hot, (((1,), (1,)), ((), ())),
        precision=lax.Precision.HIGHEST, preferred_element_type=F32,
    )
    small_peers = [at.core_peer, at.x_peer, at.y_peer]
    steps = len(small_peers)

    def small_copy(i):
        return remote(small_own.at[i], small_got.at[i], small_sems.at[3], small_sems.at[i], small_peers[i])

    def small_row(i):
        return remote(
            small_own.at[steps], small_rows.at[at.z], small_sems.at[4], small_sems.at[5],
            at.z_peer(lax.rem(at.z + i, n_seq)),
        )

    def small_step(i):
        small_copy(i).wait_recv()
        small_own[i + 1] = small_own[i] + small_got[i]
        if i + 1 < steps:
            small_copy(i + 1).start()

    inner = (at.z > 0) & (at.z < n_seq - 1)
    small_copy(0).start()
    ff.stage2(5)
    att.stage1(1)
    ff.stage3(4)
    small_step(0)
    att.stage2(0)
    att.stage1(2)
    ff.hop(3, 1)
    begin(tokens_back[3])
    ff.stage3(5)
    ff.hop(2, 2)
    att.stage2(1)
    att.stage1(3)
    ff.hop(4, 1)
    ff.hop(3, 2)
    att.stage3(0)
    small_step(1)
    att.stage2(2)
    ff.hop(5, 1)
    ff.hop(4, 2)
    att.stage3(1)
    att.stage2(3)
    att.hop(0, 1)
    ff.hop(5, 2)
    small_step(2)
    small_rows[at.z] = small_own[steps]
    att.stage3(2)
    att.hop(1, 1)
    att.hop(0, 2)
    att.stage3(3)
    for i in range(1, n_seq):
        small_row(i).start()
    att.hop(2, 1)
    att.hop(1, 2)
    att.hop(3, 1)
    att.hop(2, 2)
    att.hop(3, 2)

    @pl.loop(0, FF_JOBS)
    def _(j):
        ff.finish(j, ff_out)

    @pl.loop(0, ATT_JOBS)
    def _(j):
        att.finish(j, att_out)


    three_rows = small_rows.at[pl.ds(0, n_seq - 1)]
    remote(three_rows, three_rows, small_sems.at[4], small_sems.at[5], at.core_peer).wait_recv()
    total = small_rows[0]
    for i in range(1, n_seq):
        total = total + small_rows[i]
    small_rows[0] = total
    small_store = pltpu.make_async_copy(small_rows.at[0], small_out, own_sems.at[5])
    small_store.start()
    ff.drain(ff_out)
    att.drain(att_out)
    three_steps = small_own.at[pl.ds(0, steps)]
    remote(three_steps, three_steps, small_sems.at[3], small_sems.at[0], at.core_peer).wait_send()
    remote(three_rows, three_rows, small_sems.at[4], small_sems.at[5], at.core_peer).wait_send()
    sent(SEGS, three_segs)
    for kind in (TOKENS, MIXED, BACK):
        sent(kind, three_blocks)
    for kind in (MIXED, BACK):
        arrive(kind, three_blocks, one_block)
    small_store.wait()


def layer(n_dp, n_seq, tokens, cot, seg, buckets, gain_one, gain_two, table, weights):
    width = tokens.shape[-1]
    span = tokens.shape[0] * tokens.shape[1]
    heads = table.shape[0]
    ff_width = weights[4].shape[1]
    ff_pieces, att_pieces = 2 * FF_JOBS, 2 * ATT_JOBS
    low = lambda *shape: VMEM(shape, LOW)
    dma = pltpu.SemaphoreType.DMA
    steps = 3

    def sums(pieces, rows):
        return [
            low(pieces, 2, 2, 2, rows, 128), low(pieces, 2, 2, rows, 128), low(pieces, 2, rows, 128),
            low(pieces, rows, 128), low(pieces, rows, 128), low(pieces, rows, 128),
            dma((5,)), dma((3, pieces // 2)), dma((2, pieces)), dma((1,)),
        ]

    pairs = low(heads // 2, span, 128)
    rows, turned = low(span, width), low(width, span)
    any_, vmem = pl.BlockSpec(memory_space=pl.ANY), pl.BlockSpec(memory_space=VMEM)
    result = lambda *shape: jax.ShapeDtypeStruct(shape, LOW)
    return pl.pallas_call(
        functools.partial(layer_kernel, n_dp, n_seq),
        out_shape=[
            result(n_seq, span // n_seq, width), result(n_seq, span // n_seq, width),
            result(ff_pieces, FF_ROWS, 128), result(att_pieces, ATT_ROWS, 128),
            jax.ShapeDtypeStruct((24, 128), F32),
            result(heads, span, span), result(ff_width // 512, 2, span, 512),
        ],
        in_specs=[any_] * 2 + [vmem] * 5 + [any_] * 7,
        out_specs=[any_] * 7,
        scratch_shapes=sums(ff_pieces, FF_ROWS)
        + sums(att_pieces, ATT_ROWS)
        + [
            VMEM((steps + 1, 24, 128), F32), VMEM((steps, 24, 128), F32), VMEM((n_seq, 24, 128), F32),
            dma((6,)),
        ]
        + [
            rows, rows, VMEM((n_seq, 8, 128), jnp.int32), VMEM((n_seq, 8, 128), jnp.int32), rows,
            low(width, width), low(2, width, 1024), low(1024, width), low(2, 2, span, span), VMEM((16, span), F32),
            low(ff_width // 256, 256, span), turned, pairs, pairs, pairs, turned, VMEM((span, width), F32),
            VMEM((span, width), F32), rows, rows, turned, turned, VMEM((16, 1024), F32),
            VMEM((heads, 2 * (span // 128) - 1, 8, 256), F32),
            VMEM((1, 1024), jnp.int32), VMEM((1, width), F32), VMEM((1, width), F32),
            dma((4,)), dma((3, 2)), dma((2,)), dma((5,)), dma((5,)), dma((n_seq,)), dma((6,)),
        ],
        compiler_params=pltpu.CompilerParams(
            collective_id=0, has_side_effects=True, vmem_limit_bytes=VMEM_BYTES
        ),
        name="layer",
    )(tokens, cot, seg, buckets, gain_one, gain_two, table, *weights)


def outputs_kernel(
    n_dp, mixed_ref, tokens_ref, ff_ref, att_ref, small_ref,
    mixed_out, tokens_out, gn_one_out, gq_out, gk_out, gv_out, go_out, table_out, gn_two_out, gg_out, gu_out, gd_out,
    mixed_in, tokens_in, ff_in, att_in, small_in, gn_one, gq, gk, gv, go, table, gn_two, gg, gu, gd, tokens, sems,
):
    blocks = tokens_ref.shape[0]
    copies = [
        pltpu.make_async_copy(src, dst, sems.at[i])
        for i, (src, dst) in enumerate(
            [(tokens_ref.at[z], tokens_in.at[z]) for z in range(blocks)]
            + [(small_ref, small_in), (ff_ref, ff_in), (att_ref, att_in), (mixed_ref, mixed_in)]
        )
    ]
    for copy in copies:
        copy.start()
    stores = []

    def store(src, dst):
        stores.append(pltpu.make_async_copy(src, dst, sems.at[len(copies) + len(stores)]))
        stores[-1].start()

    width = mixed_ref.shape[-1]
    shard = width // GROUP
    for z in range(blocks):
        copies[z].wait()
        tokens[z] = tokens_in[z].astype(F32)
        store(tokens.at[z], tokens_out.at[z])
    copies[blocks].wait()
    table[...] = small_in[: table.shape[0], : table.shape[1]]
    store(table, table_out)
    mine = lax.axis_index("dp") // (n_dp // GROUP)
    for row, part, out in ((12, gn_two, gn_two_out), (18, gn_one, gn_one_out)):
        gains = jnp.concatenate([small_in[row + i : row + i + 1, :] for i in range(width // 128)], axis=1)
        total = jnp.zeros((1, shard), F32)
        for s in range(GROUP):
            total = total + jnp.where(mine == s, gains[:, shard * s : shard * s + shard], 0.0)
        part[...] = total
        store(part, out)
    copies[blocks + 1].wait()
    for k, (part, out) in enumerate(((gg, gg_out), (gu, gu_out))):
        for g in range(4):
            for i in range(4):
                col = 512 * g + 128 * i
                part[:, col : col + 128] = ff_in[4 + 2 * g + k, shard * i : shard * i + shard, :].astype(F32)
        store(part, out)
    for p in range(4):
        for i in range(width // 128):
            gd[64 * p : 64 * p + 64, 128 * i : 128 * i + 128] = ff_in[p, 64 * i : 64 * i + 64, :].astype(F32)
    store(gd, gd_out)
    copies[blocks + 2].wait()
    for j, (part, out) in enumerate(((go, go_out), (gv, gv_out), (gk, gk_out), (gq, gq_out))):
        for k in range(2):
            for i in range(width // 256):
                col = width // 2 * k + 128 * i
                part[:, col : col + 128] = att_in[2 * j + k, shard * i : shard * i + shard, :].astype(F32)
        store(part, out)
    copies[blocks + 3].wait()
    store(mixed_in, mixed_out)
    for copy in stores:
        copy.wait()


def outputs(n_dp, buckets, heads, mixed, tokens, ff, att, small):
    width = mixed.shape[-1]
    shard = width // GROUP
    full = lambda *shape: jax.ShapeDtypeStruct(shape, F32)
    square, wide = full(shard, width), full(shard, 2048)
    results = [
        jax.ShapeDtypeStruct(mixed.shape, LOW), full(*tokens.shape), full(1, shard), square, square, square, square,
        full(heads, buckets), full(1, shard), wide, wide, full(256, width),
    ]
    any_ = pl.BlockSpec(memory_space=pl.ANY)
    return pl.pallas_call(
        functools.partial(outputs_kernel, n_dp),
        out_shape=results,
        in_specs=[any_] * 5,
        out_specs=[any_] * len(results),
        scratch_shapes=[VMEM(a.shape, a.dtype) for a in [mixed, tokens, ff, att, small] + results[2:] + results[1:2]]
        + [pltpu.SemaphoreType.DMA((3 + len(results) + 2 * tokens.shape[0],))],
        compiler_params=pltpu.CompilerParams(vmem_limit_bytes=VMEM_BYTES),
        name="outputs",
    )(mixed, tokens, ff, att, small)


def solution(mesh):
    n_dp, n_seq = mesh.shape["dp"], mesh.shape["seq"]

    def on_device(
        tokens, segments, offset_buckets, norm_attn, w_query, w_key, w_value, w_output, bias_table,
        norm_ff, w_gate, w_up, w_down, cotangent,
    ):
        weights = (w_query, w_key, w_value, w_output, w_gate, w_up, w_down)
        sums = layer(
            n_dp, n_seq, tokens, cotangent, segments, offset_buckets, norm_attn, norm_ff, bias_table.T, weights
        )[:5]
        results = list(outputs(n_dp, bias_table.shape[0], bias_table.shape[1], *sums))
        results[2], results[7], results[8] = results[2].reshape(-1), results[7].T, results[8].reshape(-1)
        rest = n_dp // GROUP
        if rest > 1:
            groups = [[i * rest + j for j in range(rest)] for i in range(GROUP)]
            for i in (2, 3, 4, 5, 6, 8, 9, 10, 11):
                results[i] = lax.psum_scatter(
                    results[i], "dp", scatter_dimension=0, axis_index_groups=groups, tiled=True
                )
            results[7] = lax.psum(results[7], "dp", axis_index_groups=groups)
        return tuple(results)

    rows, shares = P("dp", "seq", None), P("dp", None)
    return jax.shard_map(
        on_device,
        mesh=mesh,
        in_specs=(rows, P("dp", "seq")) + (P(),) * 11 + (rows,),
        out_specs=(rows, rows, P("dp"), shares, shares, shares, shares, P(), P("dp"), shares, shares, shares),
        check_vma=False,
    )
```
